256 devices in a mesh: gx: 16 (over z, y_lo), yz: 16 (over y_hi, x, core).
Axes of the slice: x: 4, y: 4 (y_hi: 2, y_lo: 2; y = y_hi * 2 + y_lo), z: 8, core: 2. Of those that a mesh axis runs over, the one named last changes fastest.
Arguments:
- positions: float32 [16, 16, 3, 80], P('gx', 'yz'), may hold values from -1 to 138, as said below
- velocities: float32 [16, 16, 3, 80], P('gx', 'yz'), may hold values from -4 to 4
- forces: float32 [16, 16, 3, 80], P('gx', 'yz'), may hold values from -4 to 4
- species: int32 [16, 16, 80], P('gx', 'yz'), may hold values from 0 to 4
- neighbours: int32 [16, 16, 96, 80], P('gx', 'yz'), may hold values from 0 to 319, as said below
- slot_mask: int32 [16, 16, 96, 80], P('gx', 'yz'), may hold values from 0 to 1
- send_x: int32 [16, 16, 2, 40], P('gx', 'yz'), may hold values from 0 to 79, as said below
- send_y: int32 [16, 16, 2, 80], P('gx', 'yz'), may hold values from 0 to 159, as said below
- move_send: int32 [16, 16, 2, 5], P('gx', 'yz'), may hold values from 0 to 80, as said below
- move_recv: int32 [16, 16, 2, 5], P('gx', 'yz'), may hold values from 0 to 80, as said below
- w_bessel: float32 [8, 32], replicated, may hold values from -2 to 2
- emb_center: float32 [32, 5], replicated, may hold values from -4 to 4
- emb_neigh: float32 [32, 5], replicated, may hold values from -4 to 4
- w_env: float32 [32, 32], replicated, may hold values from -1 to 1
- w_latent: float32 [128, 32], replicated, may hold values from -0.5 to 0.5
- w_out: float32 [32], replicated, may hold values from -1 to 1
Outputs:
- new_velocity: float32 [16, 16, 3, 80], P('gx', 'yz')
- new_travel: float32 [16, 16, 3, 80], P('gx', 'yz')
The draws below stay inside these ranges and needn't reach their ends.
Inputs may be any that keep to these rules, and one draw needn't show every extreme that they name: `positions`: positions lie near a cubic lattice of spacing 2.15 whose sites fill each brick (4 by 4 by 5 sites); z is periodic over the brick. `neighbours`: rows of the brick's table: 80 owned rows, 40 ghosts from the lower gx neighbour, 40 from the upper, 80 from the lower yz neighbour, 80 from the upper, each ghost block in its sender's list order. Valid slots name distinct atoms other than the slot's own. `send_x`: rows 0 and 1 are disjoint. `send_y`: rows 0 and 1 are disjoint. `move_send`: 80 marks an empty slot; filled slots come first and name distinct rows; some brick fills all 5 slots of both rows. `move_recv`: 80 exactly where the sender's matching entry is 80; other entries are distinct rows that are vacant or leave.
All inputs are finite; a program needn't handle non-finite values.
Results may differ from the reference program's by a relative error of at most 0.0003.
Values sent between devices are 32-bit elements; how exact they have to be, the bound alone decides.
A program may use at most 64 MiB of HBM per device.

```python
import jax
import jax.numpy as jnp
import numpy as np
from jax import lax

CH = 32
NBASIS = 8
NSPEC = 5
NB = 96
PX = 4
PY = 4
PZ = 5
DEPTH = 2
STEPS = 1
MIG = 5
ATOMS = 80
GX1 = 40
GY2 = 80
TABLE = 320
N_GX = 16
N_YZ = 16


SPACING = 2.15


def offset_table():
    found = []
    for shift_x in range(-2, 3):
        for shift_y in range(-2, 3):
            for shift_z in range(-2, 3):
                square = shift_x * shift_x + shift_y * shift_y + shift_z * shift_z
                if 0 < square <= 8:
                    found.append((shift_x, shift_y, shift_z))
    return np.array(found, np.int32)


def lattice_world(key):
    bricks = N_GX * N_YZ
    world_key = jax.random.fold_in(key, 7001)
    brick_ids = jnp.arange(bricks, dtype=jnp.int32)
    row_ids = jnp.arange(ATOMS, dtype=jnp.int32)
    brick_keys = jax.random.split(jax.random.fold_in(world_key, 1), bricks)
    site_order = jax.vmap(lambda one_key: jax.random.permutation(one_key, ATOMS))(brick_keys).astype(jnp.int32)
    row_of_site = jnp.zeros((bricks, ATOMS), jnp.int32).at[brick_ids[:, None], site_order].set(jnp.broadcast_to(row_ids[None, :], (bricks, ATOMS)))
    vacancy_keys = jax.random.split(jax.random.fold_in(world_key, 2), bricks)
    vacancy_rank = jax.vmap(lambda one_key: jax.random.permutation(one_key, ATOMS))(vacancy_keys).astype(jnp.int32)
    vacancies = jax.random.randint(jax.random.fold_in(world_key, 3), (bricks,), ATOMS // 8, ATOMS // 4 + 1)
    alive_row = (vacancy_rank >= vacancies[:, None]).astype(jnp.int32)
    alive_site = jnp.take_along_axis(alive_row, row_of_site, axis=1)
    brick_x = brick_ids // N_YZ
    brick_y = brick_ids % N_YZ
    wide = PX + 2 * DEPTH
    offsets = jnp.asarray(offset_table())
    offset_count = offsets.shape[0]
    column_x = site_order // (PY * PZ)
    column_y = site_order // PZ % PY
    column_z = site_order % PZ
    ext_x = column_x[:, :, None] + offsets[None, None, :, 0]
    ext_y = column_y[:, :, None] + offsets[None, None, :, 1]
    ext_z = (column_z[:, :, None] + offsets[None, None, :, 2]) % PZ
    clip_x = jnp.clip(ext_x, 0, PX - 1)
    clip_y = jnp.clip(ext_y, 0, PY - 1)
    own_site = (clip_x * PY + clip_y) * PZ + ext_z
    own_row = jnp.take_along_axis(row_of_site, own_site.reshape(bricks, -1), axis=1).reshape(ext_x.shape)
    lower_x = ATOMS + ((ext_x + DEPTH) * PY + clip_y) * PZ + ext_z
    upper_x = ATOMS + GX1 + ((ext_x - PX) * PY + clip_y) * PZ + ext_z
    inside_x = (ext_x >= 0) & (ext_x < PX)
    ext_index = jnp.where(inside_x, own_row, jnp.where(ext_x < 0, lower_x, upper_x))
    lower_y = ATOMS + 2 * GX1 + ((ext_y + DEPTH) * wide + ext_x + DEPTH) * PZ + ext_z
    upper_y = ATOMS + 2 * GX1 + GY2 + ((ext_y - PY) * wide + ext_x + DEPTH) * PZ + ext_z
    inside_y = (ext_y >= 0) & (ext_y < PY)
    table_index = jnp.where(inside_y, ext_index, jnp.where(ext_y < 0, lower_y, upper_y)).astype(jnp.int32)
    owner_x = (brick_x[:, None, None] + jnp.floor_divide(ext_x, PX)) % N_GX
    owner_y = (brick_y[:, None, None] + jnp.floor_divide(ext_y, PY)) % N_YZ
    owner = owner_x * N_YZ + owner_y
    owner_site = (ext_x % PX * PY + ext_y % PY) * PZ + ext_z
    owner_alive = alive_site[owner, owner_site]
    valid = (owner_alive * alive_row[:, :, None]).astype(jnp.int32)
    scores = jax.random.randint(jax.random.fold_in(world_key, 4), (bricks, ATOMS, NB), 0, 1 << 20) * NB + jnp.arange(NB, dtype=jnp.int32)
    slot_order = jnp.argsort(scores, axis=-1).astype(jnp.int32)[:, :, :offset_count]
    filler = jax.random.randint(jax.random.fold_in(world_key, 5), (bricks, ATOMS, NB), 0, TABLE)
    place = jax.vmap(jax.vmap(lambda row_fill, slot_place, slot_values: row_fill.at[slot_place].set(slot_values)))
    neighbour_rows = place(filler, slot_order, table_index)
    live_rows = place(jnp.zeros((bricks, ATOMS, NB), jnp.int32), slot_order, valid)
    neighbour_rows = neighbour_rows.reshape(N_GX, N_YZ, ATOMS, NB).transpose(0, 1, 3, 2)
    live_rows = live_rows.reshape(N_GX, N_YZ, ATOMS, NB).transpose(0, 1, 3, 2)
    pieces_x = jnp.arange(GX1, dtype=jnp.int32)
    layer_x = pieces_x // (PY * PZ)
    rest_x = pieces_x % (PY * PZ)
    send_low = row_of_site[:, layer_x * PY * PZ + rest_x]
    send_high = row_of_site[:, (PX - DEPTH + layer_x) * PY * PZ + rest_x]
    send_x = jnp.stack([send_low, send_high], axis=1)
    pieces_y = jnp.arange(GY2, dtype=jnp.int32)
    band_rows = pieces_y // (wide * PZ)
    across = pieces_y // PZ % wide - DEPTH
    depth_z = pieces_y % PZ

    def ext_rows(row_y):
        inside = (across >= 0) & (across < PX)
        owned_part = row_of_site[:, (jnp.clip(across, 0, PX - 1) * PY + row_y) * PZ + depth_z]
        lower_portion = ATOMS + ((across + DEPTH) * PY + row_y) * PZ + depth_z
        upper_portion = ATOMS + GX1 + ((across - PX) * PY + row_y) * PZ + depth_z
        return jnp.where(inside[None], owned_part, jnp.where(across < 0, lower_portion, upper_portion)[None])
    send_y = jnp.stack([ext_rows(band_rows), ext_rows(PY - DEPTH + band_rows)], axis=1)
    counts = jax.random.randint(jax.random.fold_in(world_key, 6), (bricks, 2), 1, MIG + 1)
    chosen = jax.random.randint(jax.random.fold_in(world_key, 7), (), 0, bricks)
    counts = jnp.where((brick_ids == chosen)[:, None], MIG, counts)
    counts = jnp.where((brick_ids == (chosen + 1) % bricks)[:, None], 1, counts)
    face_sites = jnp.arange(PY * PZ, dtype=jnp.int32)
    face_rows = jnp.stack([row_of_site[:, face_sites], row_of_site[:, (PX - 1) * PY * PZ + face_sites]], axis=1)
    face_alive = jnp.take_along_axis(jnp.broadcast_to(alive_row[:, None, :], (bricks, 2, ATOMS)), face_rows, axis=2)
    face_scores = jax.random.randint(jax.random.fold_in(world_key, 8), (bricks, 2, PY * PZ), 0, 1 << 20) * (PY * PZ) + face_sites
    priority = (1 - face_alive) * (1 << 29) + face_scores
    picked = jnp.argsort(priority, axis=2)[:, :, :MIG]
    chosen_rows = jnp.take_along_axis(face_rows, picked, axis=2)
    slot_index = jnp.arange(MIG, dtype=jnp.int32)
    move_send = jnp.where(slot_index[None, None, :] < counts[:, :, None], chosen_rows, ATOMS).astype(jnp.int32)
    lower_brick = (brick_x - 1) % N_GX * N_YZ + brick_y
    upper_brick = (brick_x + 1) % N_GX * N_YZ + brick_y
    received_below = counts[lower_brick, 1]
    received_above = counts[upper_brick, 0]
    leaving = jnp.zeros((bricks, ATOMS + 1), jnp.int32).at[brick_ids[:, None], move_send.reshape(bricks, -1)].set(1)[:, :ATOMS]
    free_rows = jnp.maximum(1 - alive_row, leaving)
    pool_scores = jax.random.randint(jax.random.fold_in(world_key, 9), (bricks, ATOMS), 0, 1 << 16) * ATOMS + row_ids + (1 - free_rows) * (1 << 28)
    free_order = jnp.argsort(pool_scores, axis=1).astype(jnp.int32)
    recv_low = jnp.where(slot_index[None] < received_below[:, None], free_order[:, :MIG], ATOMS)
    high_place = jnp.clip(received_below[:, None] + slot_index[None], 0, ATOMS - 1)
    recv_high = jnp.where(slot_index[None] < received_above[:, None], jnp.take_along_axis(free_order, high_place, axis=1), ATOMS)
    move_recv = jnp.stack([recv_low, recv_high], axis=1).astype(jnp.int32)
    shaped = lambda values: values.reshape((N_GX, N_YZ) + values.shape[1:]).astype(jnp.int32)
    return (site_order, neighbour_rows.astype(jnp.int32), live_rows.astype(jnp.int32), shaped(send_x), shaped(send_y), shaped(move_send), shaped(move_recv))


def draw_positions(key, part):
    world = lattice_world(key)
    key = jax.random.fold_in(key, 17)
    site_order = world[0]
    bricks = N_GX * N_YZ
    brick_ids = jnp.arange(bricks, dtype=jnp.int32)
    global_x = (brick_ids // N_YZ)[:, None] * PX + site_order // (PY * PZ)
    global_y = (brick_ids % N_YZ)[:, None] * PY + site_order // PZ % PY
    global_z = site_order % PZ
    lattice = jnp.stack([global_x, global_y, global_z], axis=1).astype(jnp.float32) * SPACING
    jitter = jnp.clip(0.1 * jax.random.normal(key, lattice.shape, jnp.float32), -0.4, 0.4)
    return (lattice + jitter).reshape(N_GX, N_YZ, 3, ATOMS).astype(jnp.float32)


def draw_neighbours(key, part):
    world = lattice_world(key)
    key = jax.random.fold_in(key, 23)
    return world[1]


def draw_slot_mask(key, part):
    world = lattice_world(key)
    key = jax.random.fold_in(key, 29)
    return world[2]


def draw_send_x(key, part):
    world = lattice_world(key)
    key = jax.random.fold_in(key, 31)
    return world[3]


def draw_send_y(key, part):
    world = lattice_world(key)
    key = jax.random.fold_in(key, 37)
    return world[4]


def draw_move_send(key, part):
    world = lattice_world(key)
    key = jax.random.fold_in(key, 41)
    return world[5]


def draw_move_recv(key, part):
    world = lattice_world(key)
    key = jax.random.fold_in(key, 43)
    return world[6]


def place_ends(values, own_key, low, largest):
    spot = [jax.random.randint(jax.random.fold_in(own_key, axis), (), 0, length) for axis, length in enumerate(values.shape)]
    main_axis = values.shape.index(max(values.shape))
    next_to = spot[:main_axis] + [(spot[main_axis] + 1) % values.shape[main_axis]] + spot[main_axis + 1:]
    return values.at[tuple(spot)].set(low).at[tuple(next_to)].set(largest)


def level_of(rng, shape, cuts, least, high):
    def one(position, blocks):
        draws = jax.random.uniform(jax.random.fold_in(jax.random.fold_in(rng, 6), position), (blocks,), jnp.float32, least / len(cuts), high / len(cuts))
        return jnp.repeat(jnp.exp(draws), shape[position] // blocks).reshape((-1,) + (1,) * (len(shape) - position - 1))

    factor_of = one(*cuts[0])
    for cut in cuts[1:]:
        factor_of = factor_of * one(*cut)
    return factor_of


def noise(rng, shape, spread, limit, shards=(), held_as=jnp.bfloat16):
    drawn = spread * jax.random.normal(rng, shape, jnp.float32)
    if shards:
        drawn = drawn * level_of(rng, shape, shards, -0.22, 0.18)
    return jnp.clip(drawn, -limit, limit).astype(held_as)


def setup_inputs(seed: int = 0) -> dict:
    streams_of = jax.random.split(jax.random.key(seed), 17)
    positions = draw_positions(jax.random.fold_in(streams_of[16], 71), 0)
    velocities = noise(streams_of[1], (N_GX, N_YZ, 3, ATOMS), 1.0, 4.0, ((0, 16), (1, 16)), jnp.float32)
    forces = noise(streams_of[2], (N_GX, N_YZ, 3, ATOMS), 1.0, 4.0, ((0, 16), (1, 16)), jnp.float32)
    species = place_ends(jax.random.randint(streams_of[3], (N_GX, N_YZ, ATOMS), 0, NSPEC), jax.random.fold_in(streams_of[3], 1), 0, NSPEC - 1).astype(jnp.int32)
    neighbours = draw_neighbours(jax.random.fold_in(streams_of[16], 71), 0)
    slot_mask = draw_slot_mask(jax.random.fold_in(streams_of[16], 71), 0)
    send_x = draw_send_x(jax.random.fold_in(streams_of[16], 71), 0)
    send_y = draw_send_y(jax.random.fold_in(streams_of[16], 71), 0)
    move_send = draw_move_send(jax.random.fold_in(streams_of[16], 71), 0)
    move_recv = draw_move_recv(jax.random.fold_in(streams_of[16], 71), 0)
    w_bessel = noise(streams_of[10], (NBASIS, CH), NBASIS ** -0.5, 2.0, (), jnp.float32)
    emb_center = noise(streams_of[11], (CH, NSPEC), 1.0, 4.0, (), jnp.float32)
    emb_neigh = noise(streams_of[12], (CH, NSPEC), 1.0, 4.0, (), jnp.float32)
    w_env = noise(streams_of[13], (CH, CH), CH ** -0.5, 1.0, (), jnp.float32)
    w_latent = noise(streams_of[14], (4 * CH, CH), (4 * CH) ** -0.5, 0.5, (), jnp.float32)
    w_out = noise(streams_of[15], (CH,), CH ** -0.5, 1.0, (), jnp.float32)
    return {"positions": positions, "velocities": velocities, "forces": forces, "species": species, "neighbours": neighbours, "slot_mask": slot_mask, "send_x": send_x, "send_y": send_y, "move_send": move_send, "move_recv": move_recv, "w_bessel": w_bessel, "emb_center": emb_center, "emb_neigh": emb_neigh, "w_env": w_env, "w_latent": w_latent, "w_out": w_out}


SPACING = 2.15
CUTOFF = 6.0
TIME_STEP = 0.05
ENV_SCALE = 0.125
MASSES = (1.008, 12.011, 14.007, 15.999, 32.06)
HIGHEST = lax.Precision.HIGHEST

def harmonics(unit_vec):
    unit_x, unit_y, unit_z = (unit_vec[0], unit_vec[1], unit_vec[2])
    root_three = 3.0 ** 0.5
    root_fifteen = 15.0 ** 0.5
    root_five = 5.0 ** 0.5
    return [jnp.ones_like(unit_x), root_three * unit_x, root_three * unit_y, root_three * unit_z, root_fifteen * unit_x * unit_y, root_fifteen * unit_y * unit_z, 0.5 * root_five * (3.0 * unit_z * unit_z - 1.0), root_fifteen * unit_x * unit_z, 0.5 * root_fifteen * (unit_x * unit_x - unit_y * unit_y)]

def brick_energy(table_coords, table_kinds, rows_in, slot_live, period, params):
    w_bessel, emb_center, emb_neigh, w_env, w_latent, w_out = params
    slot_count = rows_in.shape[0]
    atom_count = rows_in.shape[1]
    channels = w_env.shape[0]
    edge_count = slot_count * atom_count
    owned_rows = table_coords[:, :atom_count]
    nearby = jnp.take(table_coords, rows_in, axis=1)
    offset_vec = nearby - owned_rows[:, None, :]
    length_box = period[:, None, None]
    offset_vec = offset_vec - length_box * jnp.floor(offset_vec / length_box + 0.5)
    alive = slot_live > 0
    filler = jnp.stack([jnp.full(slot_live.shape, SPACING, jnp.float32), jnp.zeros(slot_live.shape, jnp.float32), jnp.zeros(slot_live.shape, jnp.float32)])
    offset_vec = jnp.where(alive[None], offset_vec, filler)
    radius = jnp.sqrt(lax.optimization_barrier(jnp.sum(offset_vec * offset_vec, axis=0)))
    unit_vec = offset_vec / radius[None]
    scaled = radius / CUTOFF
    polynomial = 1.0 - 28.0 * scaled ** 6 + 48.0 * scaled ** 7 - 21.0 * scaled ** 8
    envelope = jnp.where(scaled < 1.0, polynomial, 0.0) * slot_live
    orders = jnp.arange(1, w_bessel.shape[0] + 1).astype(jnp.float32)
    bessel = (2.0 / CUTOFF) ** 0.5 * jnp.sin(orders[:, None, None] * jnp.pi * radius[None] / CUTOFF) / radius[None]
    kind_ids = jnp.arange(emb_center.shape[1]).astype(jnp.float32)
    center_hot = (table_kinds[None, :atom_count] == kind_ids[:, None]).astype(jnp.float32)
    neigh_kinds = jnp.take(table_kinds, rows_in)
    neigh_hot = (neigh_kinds[None] == kind_ids[:, None, None]).astype(jnp.float32)
    preact = jnp.dot(w_bessel.T, bessel.reshape(-1, edge_count), precision=HIGHEST, preferred_element_type=jnp.float32)
    preact = preact + jnp.dot(emb_neigh, neigh_hot.reshape(-1, edge_count), precision=HIGHEST, preferred_element_type=jnp.float32)
    center_term = jnp.dot(emb_center, center_hot, precision=HIGHEST, preferred_element_type=jnp.float32)
    preact = preact.reshape(channels, slot_count, atom_count) + center_term[:, None, :]
    edge_feat = jax.nn.silu(preact) * envelope[None]
    weight = jnp.dot(w_env.T, edge_feat.reshape(channels, edge_count), precision=HIGHEST, preferred_element_type=jnp.float32).reshape(channels, slot_count, atom_count)
    harmonic = harmonics(unit_vec)
    env_sum = [ENV_SCALE * lax.optimization_barrier(jnp.sum(weight * harm_comp[None], axis=1)) for harm_comp in harmonic]
    scalars = []
    for first_m, stop_m in ((0, 1), (1, 4), (4, 9)):
        running = env_sum[first_m][:, None, :] * harmonic[first_m][None]
        for index_m in range(first_m + 1, stop_m):
            running = running + env_sum[index_m][:, None, :] * harmonic[index_m][None]
        scalars.append(running)
    joined = jnp.concatenate([edge_feat] + scalars, axis=0).reshape(4 * channels, edge_count)
    latent = jax.nn.silu(jnp.dot(w_latent.T, joined, precision=HIGHEST, preferred_element_type=jnp.float32))
    hidden = edge_feat.reshape(channels, edge_count) + latent
    pair_energy = jnp.dot(w_out, hidden, precision=HIGHEST, preferred_element_type=jnp.float32).reshape(slot_count, atom_count) * envelope
    return jnp.sum(pair_energy)

def select_rows(payload_rows, index_rows):
    return jax.vmap(jax.vmap(lambda block_rows, block_index: block_rows[:, block_index]))(payload_rows, index_rows)

def add_ghosts(payload_rows, outbound_messages, along):
    down_rows = select_rows(payload_rows, outbound_messages[:, :, 0])
    up_rows = select_rows(payload_rows, outbound_messages[:, :, 1])
    received_below = jnp.roll(up_rows, 1, axis=along)
    received_above = jnp.roll(down_rows, -1, axis=along)
    return jnp.concatenate([payload_rows, received_below, received_above], axis=3)

def add_into(kept_rows, index_rows, values):
    return jax.vmap(jax.vmap(lambda block_rows, block_index, block_values: block_rows.at[:, block_index].add(block_values)))(kept_rows, index_rows, values)

def return_ghosts(partial_energy_value, outbound_messages, along, total_row_count):
    ghost_width = outbound_messages.shape[3]
    kept_rows = partial_energy_value[..., :total_row_count]
    lower_portion = partial_energy_value[..., total_row_count:total_row_count + ghost_width]
    upper_portion = partial_energy_value[..., total_row_count + ghost_width:total_row_count + 2 * ghost_width]
    back_down = jnp.roll(upper_portion, 1, axis=along)
    back_up = jnp.roll(lower_portion, -1, axis=along)
    kept_rows = add_into(kept_rows, outbound_messages[:, :, 0], back_down)
    return add_into(kept_rows, outbound_messages[:, :, 1], back_up)

def settle_brick(padded, outgoing, incoming, received_below, received_above):
    leaving = jnp.zeros((padded.shape[1],), padded.dtype).at[outgoing[0]].set(1.0).at[outgoing[1]].set(1.0)
    settled = padded * (1.0 - leaving)[None]
    settled = settled.at[:, incoming[0]].set(received_below).at[:, incoming[1]].set(received_above)
    return settled[:, :-1]

def reference(positions, velocities, forces, species, neighbours, slot_mask, send_x, send_y, move_send, move_recv, w_bessel, emb_center, emb_neigh, w_env, w_latent, w_out):
    params = (w_bessel, emb_center, emb_neigh, w_env, w_latent, w_out)
    count_gx = positions.shape[0]
    count_yz = positions.shape[1]
    atom_count = positions.shape[3]
    bricks = count_gx * count_yz
    period = jnp.array([count_gx * PX * SPACING, count_yz * PY * SPACING, PZ * SPACING], jnp.float32)
    kinds_float = species.astype(jnp.float32)
    kind_ids = jnp.arange(len(MASSES)).astype(jnp.float32)
    one_hot = (kinds_float[:, :, None, :] == kind_ids[None, None, :, None]).astype(jnp.float32)
    mass_inverse = lax.optimization_barrier(jnp.sum(one_hot / jnp.array(MASSES, jnp.float32)[None, None, :, None], axis=2))[:, :, None, :]
    slot_live = slot_mask.astype(jnp.float32)
    flat_rows = neighbours.reshape(bricks, neighbours.shape[2], atom_count)
    flat_live = slot_live.reshape(bricks, neighbours.shape[2], atom_count)

    def brick_gradient(inputs):
        ghost_table, rows_in, live_in = inputs
        return jax.grad(brick_energy)(ghost_table[:3], ghost_table[3], rows_in, live_in, period, params)
    coords = positions
    velocity = velocities
    force_now = forces
    for repeat in range(STEPS):
        velocity = velocity + 0.5 * TIME_STEP * force_now * mass_inverse
        coords = coords + TIME_STEP * velocity
        owned_rows = jnp.concatenate([coords, kinds_float[:, :, None, :]], axis=2)
        extended = add_ghosts(owned_rows, send_x, 0)
        ghost_table = add_ghosts(extended, send_y, 1)
        table_rows = ghost_table.shape[3]
        gradient = lax.map(brick_gradient, (ghost_table.reshape(bricks, 4, table_rows), flat_rows, flat_live))
        partial_energy_value = -gradient.reshape(count_gx, count_yz, 3, table_rows)
        partial_energy_value = return_ghosts(partial_energy_value, send_y, 1, extended.shape[3])
        force_now = return_ghosts(partial_energy_value, send_x, 0, atom_count)
        velocity = velocity + 0.5 * TIME_STEP * force_now * mass_inverse
    travel = (coords - positions) / (STEPS * TIME_STEP)
    payload = jnp.concatenate([velocity, travel], axis=2)
    padded = jnp.concatenate([payload, jnp.zeros(payload.shape[:3] + (1,), jnp.float32)], axis=3)
    down_rows = select_rows(padded, move_send[:, :, 0])
    up_rows = select_rows(padded, move_send[:, :, 1])
    received_below = jnp.roll(up_rows, 1, axis=0)
    received_above = jnp.roll(down_rows, -1, axis=0)
    settled = jax.vmap(jax.vmap(settle_brick))(padded, move_send, move_recv, received_below, received_above)
    return (settled[:, :, :3], settled[:, :, 3:])
```

```python
import jax
import jax.numpy as jnp
from jax import lax
from jax.experimental import pallas as pl
from jax.experimental.pallas import tpu as pltpu
from jax.sharding import PartitionSpec as P

PX = 4
PY = 4
PZ = 5
STEPS = 1
SPACING = 2.15
CUTOFF = 6.0
TIME_STEP = 0.05
ENV_SCALE = 0.125
MASSES = (1.008, 12.011, 14.007, 15.999, 32.06)
HIGHEST = lax.Precision.HIGHEST
MESH = pl.DeviceIdType.MESH
F32 = jnp.float32
BF16 = jnp.bfloat16
I32 = jnp.int32

LANES = 128
GROUP = 16
PI = 3.141592653589793
R3 = 3.0**0.5
R5 = 5.0**0.5
R15 = 15.0**0.5

HALO = [(dx, dy) for dy in (-1, 0, 1) for dx in (-1, 0, 1)]
NEAR = [pos for pos in HALO if pos != (0, 0)]
TARGETS = [(dx, dy) for dy in (-1, 0, 1) for dx in (-2, -1, 0, 1, 2)]
FAR = [pos for pos in TARGETS if pos != (0, 0)]


def halo_slot(dx, dy):
    return (dy + 1) * 3 + dx + 1


def target_slot(dx, dy):
    return (dy + 1) * 5 + dx + 2


def nt_dot(a, b, precision=None):
    return lax.dot_general(
        a, b, (((1,), (1,)), ((), ())), precision=precision, preferred_element_type=F32
    )


def nn_dot(a, b, precision=None):
    return jnp.dot(a, b, precision=precision, preferred_element_type=F32)


def halves(x):
    high = x.astype(BF16)
    low = (x - high.astype(F32)).astype(BF16)
    return high, low


def left_parts(w):
    high, low = halves(w)
    return jnp.concatenate([high, high, low], axis=1)


def right_parts(x):
    high, low = halves(x)
    return jnp.concatenate([high, low, high], axis=0)


def pick(rows, index):
    return jnp.take_along_axis(rows, index, axis=1, mode="promise_in_bounds")


def sigmoid(x):
    return 1.0 / (1.0 + jnp.exp(-x))


def lanes_total(x):
    for shift in (64, 32, 16):
        x = x + pltpu.roll(x, shift, 1)
    return x


def kernel_body(
    period,
    atoms,
    slots,
    pos_ref,
    vel_ref,
    frc_ref,
    spc_ref,
    nbr_ref,
    msk_ref,
    sx_ref,
    sy_ref,
    ms_ref,
    mr_ref,
    wb_ref,
    ec_ref,
    en_ref,
    we_ref,
    wl_ref,
    wo_ref,
    nv_ref,
    ntr_ref,
    halo,
    load,
    ret_out,
    ret_in,
    nb_pad,
    rows_code,
    table,
    sc,
    zf,
    zy,
    zd,
    pt,
    cterm,
    mats,
    w1s,
    wcol,
    pre_s,
    sig_s,
    ef_s,
    dlp_s,
    hid_s,
    gs,
    dfs,
    g3,
    halo_send,
    halo_recv,
    load_send,
    load_recv,
    ret_send,
    ret_recv,
):
    gx = lax.axis_index("gx")
    yz = lax.axis_index("yz")
    n_gx = lax.axis_size("gx")
    n_yz = lax.axis_size("yz")
    blocks = atoms // GROUP
    per_block = slots // 8
    n_rows = blocks * per_block
    chunks = (n_rows + 7) // 8

    def device(dx, dy):
        return (lax.rem(gx + dx + n_gx, n_gx), lax.rem(yz + dy + n_yz, n_yz))

    barrier = pltpu.get_barrier_semaphore()
    for dx, dy in FAR:
        pl.semaphore_signal(barrier, inc=1, device_id=device(dx, dy), device_id_type=MESH)

    lane1 = lax.broadcasted_iota(I32, (1, LANES), 1)
    lane8 = lax.broadcasted_iota(I32, (8, LANES), 1)
    sub8 = lax.broadcasted_iota(I32, (8, LANES), 0)

    own = halo_slot(0, 0)
    kinds = spc_ref[0].astype(F32)
    minv = jnp.zeros_like(kinds)
    for kind, mass in enumerate(MASSES):
        minv = jnp.where(kinds == float(kind), 1.0 / jnp.float32(mass), minv)
    start = pos_ref[0, 0]
    velocity = vel_ref[0, 0] + 0.5 * TIME_STEP * frc_ref[0, 0] * minv
    coords = start + TIME_STEP * velocity
    travel = (coords - start) / (STEPS * TIME_STEP)
    halo[own] = jnp.zeros((8, LANES), F32)
    load[1] = jnp.zeros((8, LANES), F32)
    halo[own, 0:3, 0:atoms] = coords
    halo[own, 3:4, 0:atoms] = kinds
    code = lane1
    place = lane1
    source = lane1
    for side in (0, 1):
        for k in range(ms_ref.shape[3]):
            seat = atoms + 5 * (1 - side) + k
            code = jnp.where(lane1 == mr_ref[0, 0, side, k], LANES - 1, code)
    for side in (0, 1):
        for k in range(ms_ref.shape[3]):
            seat = atoms + 5 * (1 - side) + k
            gone = ms_ref[0, 0, side, k]
            code = jnp.where(lane1 == gone, (2 * side - 1) * LANES + seat, code)
            place = jnp.where(lane1 == seat, gone, place)
            source = jnp.where(lane1 == gone, LANES - 1, source)
    for side in (0, 1):
        for k in range(ms_ref.shape[3]):
            source = jnp.where(lane1 == mr_ref[0, 0, side, k], atoms + 5 * side + k, source)
    code = jnp.where(lane1 < atoms, code + LANES, 0)
    halo[own, 4:5, :] = code.astype(F32)
    halo[own, 6:8, 0:atoms] = sy_ref[0, 0].astype(F32)
    load[1, 0:3, 0:atoms] = velocity
    load[1, 3:6, 0:atoms] = travel
    load[1, 6:7, 0:atoms] = minv
    width_x = sx_ref.shape[3]
    g3[0] = jnp.zeros((64, LANES), F32)
    g3[0, 0:2, 0:width_x] = sx_ref[0, 0].astype(F32)
    lists = g3[0, 0:8, :]
    halo[own, 5:6, :] = lists[1:2] + pltpu.roll(lists, width_x, 1)[0:1]
    load[1] = pick(load[1], jnp.broadcast_to(place, (8, LANES)))

    pl.semaphore_wait(barrier, len(FAR))
    sends = []
    for dx, dy in NEAR:
        there = halo_slot(-dx, -dy)
        copy = pltpu.make_async_remote_copy(
            src_ref=halo.at[own],
            dst_ref=halo.at[there],
            send_sem=halo_send.at[there],
            recv_sem=halo_recv.at[there],
            device_id=device(dx, dy),
            device_id_type=MESH,
        )
        copy.start()
        sends.append(copy)
    for dx in (-1, 1):
        there = 1 - dx
        copy = pltpu.make_async_remote_copy(
            src_ref=load.at[1],
            dst_ref=load.at[there],
            send_sem=load_send.at[there],
            recv_sem=load_recv.at[there],
            device_id=device(dx, 0),
            device_id_type=MESH,
        )
        copy.start()
        sends.append(copy)

    nb_pad[...] = jnp.zeros((slots, LANES), F32)
    nb_pad[:, 0:atoms] = nbr_ref[0, 0].astype(F32) + 512.0 * msk_ref[0, 0].astype(F32)
    rows_code[...] = jnp.zeros((chunks * 8, LANES), F32)
    in_group = lane8 // GROUP == sub8
    for block in range(blocks):
        spread = (lane8 & (GROUP - 1)) + block * GROUP
        for jb in range(per_block):
            moved = pick(nb_pad[jb * 8 : jb * 8 + 8, :], spread)
            row = jnp.sum(jnp.where(in_group, moved, 0.0), axis=0, keepdims=True)
            r = block * per_block + jb
            rows_code[r : r + 1, :] = row

    ch = we_ref.shape[0]
    eye = (
        lax.broadcasted_iota(I32, (ch, ch), 0) == lax.broadcasted_iota(I32, (ch, ch), 1)
    ).astype(F32)
    for part in range(3):
        mixed = ENV_SCALE * nn_dot(we_ref[...], wl_ref[(part + 1) * ch : (part + 2) * ch, :], HIGHEST)
        mats[2 + part] = left_parts(nt_dot(eye, mixed, HIGHEST))
        mats[5 + part] = left_parts(mixed)
    mats[0] = left_parts(nt_dot(eye, wl_ref[0:ch, :], HIGHEST))
    mats[1] = left_parts(wl_ref[0:ch, :])
    n_basis = wb_ref.shape[0]
    n_kinds = en_ref.shape[1]
    w1f = jnp.concatenate(
        [
            nt_dot(eye, wb_ref[...], HIGHEST),
            en_ref[...],
            jnp.zeros((ch, 16 - n_basis - n_kinds), F32),
        ],
        axis=1,
    )
    w1s[...] = left_parts(w1f)
    w_basis = left_parts(wb_ref[...])
    wcol[...] = jnp.broadcast_to(
        jnp.sum(jnp.where(eye > 0, wo_ref[...], 0.0), axis=1, keepdims=True), (ch, LANES)
    )

    for copy in sends:
        copy.wait()

    def shifted(dx, dy):
        step = float(LANES * ((dy + 1) * 5 + dx + 1))
        return halo[halo_slot(dx, dy)] + jnp.where(sub8 == 4, step, 0.0)

    def row_index(rows, which):
        return jnp.broadcast_to(rows[which : which + 1, :], (8, LANES)).astype(I32)

    def x_ghosts(dy):
        low, high = shifted(-1, dy), shifted(1, dy)
        return jnp.where(
            lane8 < width_x,
            pick(low, row_index(low, 5)),
            pick(high, row_index(high, 5)),
        )

    def y_ghosts(dy):
        base = shifted(0, dy)
        index = row_index(base, 7 if dy < 0 else 6)
        outer = index >= atoms
        return jnp.where(
            outer,
            pick(x_ghosts(dy), jnp.where(outer, index - atoms, 0)),
            pick(base, jnp.where(outer, 0, index)),
        )

    table[0] = shifted(0, 0)
    table[1] = x_ghosts(0)
    table[2] = y_ghosts(-1)
    table[3] = y_ghosts(1)

    def whole(k, c):
        return jnp.broadcast_to(table[k, c : c + 1, :], (8, LANES))

    def forward_chunk(i, carry):
        word = rows_code[pl.ds(pl.multiple_of(i * 8, 8), 8), :]
        live = word >= 512.0
        n = jnp.where(live, word - 512.0, word).astype(I32)
        k = jnp.where(n >= atoms, 1, 0) + jnp.where(n >= 2 * atoms, 1, 0) + jnp.where(n >= 3 * atoms, 1, 0)
        n = n - atoms * k
        near = []
        for c in range(5):
            v = pick(whole(0, c), n)
            for part in (1, 2, 3):
                v = jnp.where(k == part, pick(whole(part, c), n), v)
            near.append(v)
        row = i * 8 + sub8
        block = jnp.zeros((8, LANES), I32)
        for b in range(1, blocks):
            block = block + jnp.where(row >= b * per_block, 1, 0)
        centre = block * GROUP + (lane8 & (GROUP - 1))
        off = []
        for c in range(3):
            d = near[c] - pick(whole(0, c), centre)
            d = d - period[c] * jnp.floor(d / period[c] + 0.5)
            off.append(jnp.where(live, d, SPACING if c == 0 else 0.0))
        radius = jnp.sqrt(off[0] * off[0] + off[1] * off[1] + off[2] * off[2])
        rinv = 1.0 / radius
        ux, uy, uz = (o * rinv for o in off)
        q = radius / CUTOFF
        valid = jnp.logical_and(live, q < 1.0)
        q2 = q * q
        q5 = q2 * q2 * q
        q6 = q5 * q
        env = jnp.where(valid, 1.0 + q6 * (-28.0 + q * (48.0 - 21.0 * q)), 0.0)
        denv = jnp.where(valid, (168.0 / CUTOFF) * q5 * (-1.0 + q * (2.0 - q)), 0.0)
        u = PI * jnp.minimum(q, 1.0) - 0.5 * PI
        w = u * u
        sin1 = 1.0 + w * (-1 / 2 + w * (1 / 24 + w * (-1 / 720 + w * (1 / 40320 + w * (-1 / 3628800 + w * (1 / 479001600))))))
        cos1 = -u * (1.0 + w * (-1 / 6 + w * (1 / 120 + w * (-1 / 5040 + w * (1 / 362880 + w * (-1 / 39916800 + w * (1 / 6227020800)))))))
        sc[0, i] = ux
        sc[1, i] = uy
        sc[2, i] = uz
        sc[3, i] = rinv
        sc[4, i] = denv
        zbase = i * 128
        scale = (2.0 / CUTOFF) ** 0.5 * rinv
        s_prev, s_now = jnp.zeros_like(sin1), sin1
        c_prev, c_now = jnp.ones_like(cos1), cos1
        for order in range(1, n_basis + 1):
            bes = scale * s_now
            zf[pl.ds(zbase + order - 1, 8, stride=16), :] = bes
            sc[4 + order, i] = scale * (order * PI / CUTOFF) * c_now - bes * rinv
            s_prev, s_now = s_now, 2.0 * cos1 * s_now - s_prev
            c_prev, c_now = c_now, 2.0 * cos1 * c_now - c_prev
        for kind in range(n_kinds):
            zf[pl.ds(zbase + n_basis + kind, 8, stride=16), :] = jnp.where(near[3] == float(kind), 1.0, 0.0)
        for extra in range(n_basis + n_kinds, 16):
            zf[pl.ds(zbase + extra, 8, stride=16), :] = jnp.zeros((8, LANES), F32)
        ys = (
            R3 * ux,
            R3 * uy,
            R3 * uz,
            R15 * ux * uy,
            R15 * uy * uz,
            0.5 * R5 * (3.0 * uz * uz - 1.0),
            R15 * ux * uz,
            0.5 * R15 * (ux * ux - uy * uy),
        )
        for m, y in enumerate(ys):
            zy[pl.ds(zbase + m, 8, stride=16), :] = y
        zy[pl.ds(zbase + 8, 8, stride=16), :] = env
        dest = near[4].astype(I32)
        tbase = i * 64
        pt[pl.ds(tbase + 6, 8, stride=8), :] = (dest >> 7).astype(F32)
        pt[pl.ds(tbase + 7, 8, stride=8), :] = (dest & (LANES - 1)).astype(F32)
        return carry

    lax.fori_loop(0, chunks, forward_chunk, 0)

    for block in range(blocks):
        spread = (lane8 & (GROUP - 1)) + block * GROUP
        kind_row = jnp.broadcast_to(pick(whole(0, 3), spread)[0:1], (ch, LANES))
        term = jnp.zeros((ch, LANES), F32)
        for kind in range(n_kinds):
            term = jnp.where(
                kind_row == float(kind),
                jnp.broadcast_to(ec_ref[:, kind : kind + 1], (ch, LANES)),
                term,
            )
        cterm[block] = term

    degrees = (0, 1, 1, 1, 2, 2, 2, 2, 2)

    def y_rows(row):
        return [zy[pl.ds(row * 16 + m, 1), :] for m in range(9)]

    def by_degree(first, parts):
        out = []
        for degree, (a, b) in enumerate(((0, 1), (1, 4), (4, 9))):
            joined = jnp.concatenate(parts[a:b], axis=1)
            got = nn_dot(mats[first + degree], right_parts(joined))
            out += [got[:, t * LANES : (t + 1) * LANES] for t in range(b - a)]
        return out

    def block_body(block, carry):
        base = block * per_block
        feats = jnp.concatenate(
            [zf[pl.ds(pl.multiple_of((base + jb) * 16, 16), 16), :] for jb in range(per_block)], axis=1
        )
        pre = nn_dot(w1s[...], right_parts(feats))
        centre_term = cterm[block]
        acc = None
        for jb in range(per_block):
            p = pre[:, jb * LANES : (jb + 1) * LANES] + centre_term
            *ys, env = y_rows(base + jb)
            sig = sigmoid(p)
            ef = p * sig * env
            pre_s[jb] = p
            sig_s[jb] = sig
            ef_s[jb] = ef
            new = [ef] + [ef * y for y in ys]
            acc = new if acc is None else [a + b for a, b in zip(acc, new)]
        sums = [lanes_total(a) for a in acc]
        grow = by_degree(2, sums)
        for m in range(9):
            gs[m] = grow[m]
        mixed = nn_dot(mats[0], right_parts(jnp.concatenate([ef_s[jb] for jb in range(per_block)], axis=1)))
        acc = None
        w_out = wcol[...]
        for jb in range(per_block):
            *ys, env = y_rows(base + jb)
            lp = mixed[:, jb * LANES : (jb + 1) * LANES] + gs[0]
            for m in range(8):
                lp = lp + gs[m + 1] * ys[m]
            sig = sigmoid(lp)
            lat = lp * sig
            hid_s[jb] = w_out * (ef_s[jb] + lat)
            dlp = (w_out * env) * (sig + lat * (1.0 - sig))
            dlp_s[jb] = dlp
            new = [dlp] + [dlp * y for y in ys]
            acc = new if acc is None else [a + b for a, b in zip(acc, new)]
        sums = [lanes_total(a) for a in acc]
        grow = by_degree(5, sums)
        for m in range(9):
            dfs[m] = grow[m]
        mixed = nn_dot(mats[1], right_parts(jnp.concatenate([dlp_s[jb] for jb in range(per_block)], axis=1)))
        dps = []
        for jb in range(per_block):
            *ys, env = y_rows(base + jb)
            de = mixed[:, jb * LANES : (jb + 1) * LANES] + w_out * env + dfs[0]
            for m in range(8):
                de = de + dfs[m + 1] * ys[m]
            sig = sig_s[jb]
            s1 = pre_s[jb] * sig
            dps.append(de * env * (sig + s1 * (1.0 - sig)))
            zbase = (base + jb) * 24
            zd[pl.ds(zbase + 16, 1), :] = jnp.sum(hid_s[jb] + de * s1, axis=0, keepdims=True)
            ef, dlp = ef_s[jb], dlp_s[jb]
            for m in range(8):
                zd[pl.ds(zbase + 8 + m, 1), :] = jnp.sum(
                    gs[m + 1] * dlp + dfs[m + 1] * ef, axis=0, keepdims=True
                )
        dbes = nn_dot(w_basis, right_parts(jnp.concatenate(dps, axis=1)))
        for jb in range(per_block):
            zd[pl.ds(pl.multiple_of((base + jb) * 24, 8), 8), :] = dbes[:, jb * LANES : (jb + 1) * LANES]
        return carry

    lax.fori_loop(0, blocks, block_body, 0)
    for row in range(n_rows, chunks * 8):
        zd[row * 24 : row * 24 + 24, :] = jnp.zeros((24, LANES), F32)

    def put_parts(store, values):
        for c in range(3):
            high = values[c].astype(BF16).astype(F32)
            store(c, high)
            store(c + 3, values[c] - high)

    def backward_chunk(i, carry):
        zbase = i * 192

        def d(which):
            return zd[pl.ds(zbase + which, 8, stride=24), :]

        ux, uy, uz, rinv, denv = (sc[t, i] for t in range(5))
        dr = d(16) * denv
        for order in range(n_basis):
            dr = dr + d(order) * sc[5 + order, i]
        d1, d2, d3, d4, d5, d6, d7, d8 = (d(8 + m) for m in range(8))
        dux = R3 * d1 + R15 * (uy * d4 + uz * d7 + ux * d8)
        duy = R3 * d2 + R15 * (ux * d4 + uz * d5 - uy * d8)
        duz = R3 * d3 + R15 * (uy * d5 + ux * d7) + (3.0 * R5) * uz * d6
        radial = dr - rinv * (dux * ux + duy * uy + duz * uz)
        forces = [-(radial * u + rinv * du) for u, du in ((ux, dux), (uy, duy), (uz, duz))]
        at = pl.ds(pl.multiple_of(i * 8, 8), 8)
        for c in range(3):
            g3[c, at, :] = forces[c]

        def store(which, value):
            pt[pl.ds(i * 64 + which, 8, stride=8), :] = value

        put_parts(store, forces)
        return carry

    lax.fori_loop(0, chunks, backward_chunk, 0)

    extra = chunks * 8
    pt[extra * 8 :, :] = jnp.zeros((8 * 8, LANES), F32)
    for block in range(blocks):
        at = (extra + block) * 8
        sums = [
            -jnp.sum(g3[c, block * per_block : (block + 1) * per_block, :], axis=0, keepdims=True)
            for c in range(3)
        ]

        def store(which, value):
            pt[at + which : at + which + 1, :] = value

        put_parts(store, sums)
        spread = (lane8 & (GROUP - 1)) + block * GROUP
        dest = pick(whole(0, 4), spread)[0:1].astype(I32)
        pt[at + 6 : at + 7, :] = (dest >> 7).astype(F32)
        pt[at + 7 : at + 8, :] = (dest & (LANES - 1)).astype(F32)

    n_targets = len(TARGETS)
    tall = 96
    sub_tall = lax.broadcasted_iota(I32, (tall, LANES), 0).astype(F32)

    def scatter_body(i, acc):
        lefts, rights = [], []
        for t in range(8):
            v = pt[pl.ds(pl.multiple_of((i * 8 + t) * 8, 8), 8), :]
            where_to, lo = v[6:7], v[7:8]
            lefts.append(
                jnp.concatenate([jnp.where(where_to == float(b), v, 0.0) for b in range(n_targets)], axis=0)
            )
            rights.append(jnp.where(lo == sub_tall, 1.0, 0.0))
        left = jnp.concatenate(lefts, axis=1).astype(BF16)
        right = jnp.concatenate(rights, axis=1).astype(BF16)
        return acc + nt_dot(left, right)

    spread_out = lax.fori_loop(
        0, chunks + 1, scatter_body, jnp.zeros((n_targets * 8, tall), F32)
    )
    for t in range(n_targets):
        ret_out[t] = jnp.zeros((8, LANES), F32)
        ret_out[t, :, 0:tall] = spread_out[t * 8 : t * 8 + 8, :]

    sends = []
    for dx, dy in FAR:
        there = target_slot(-dx, -dy)
        copy = pltpu.make_async_remote_copy(
            src_ref=ret_out.at[target_slot(dx, dy)],
            dst_ref=ret_in.at[there],
            send_sem=ret_send.at[there],
            recv_sem=ret_recv.at[there],
            device_id=device(dx, dy),
            device_id_type=MESH,
        )
        copy.start()
        sends.append(copy)

    settle = jnp.broadcast_to(source, (8, LANES))
    mine, low, high = load[1], load[0], load[2]
    held = jnp.where(lane8 < atoms, mine, jnp.where(lane8 < atoms + 5, low, high))
    held = jnp.where(lane8 < LANES - 1, held, 0.0)
    held = pick(held, settle)
    total = ret_out[target_slot(0, 0)]
    for copy, (dx, dy) in zip(sends, FAR):
        copy.wait()
    for dx, dy in FAR:
        total = total + ret_in[target_slot(dx, dy)]
    force = pick(total, settle)
    force = force[0:3] + force[3:6]
    fresh = held[0:3] + 0.5 * TIME_STEP * force * held[6:7]
    nv_ref[0, 0] = fresh[:, 0:atoms]
    ntr_ref[0, 0] = held[3:6, 0:atoms]


def on_device(*args):
    atoms = args[0].shape[3]
    slots = args[4].shape[2]
    ch = args[13].shape[0]
    chunks = (atoms // GROUP * (slots // 8) + 7) // 8
    n_gx, n_yz = lax.axis_size("gx"), lax.axis_size("yz")
    period = (n_gx * PX * SPACING, n_yz * PY * SPACING, PZ * SPACING)
    args = args[:15] + (args[15].reshape(1, ch),)

    def body(*refs):
        kernel_body(period, atoms, slots, *refs)

    vmem = pl.BlockSpec(memory_space=pltpu.VMEM)
    smem = pl.BlockSpec(memory_space=pltpu.SMEM)
    per_block = slots // 8
    dma = pltpu.SemaphoreType.DMA
    out = jax.ShapeDtypeStruct((1, 1, 3, atoms), F32)
    return pl.pallas_call(
        body,
        out_shape=(out, out),
        in_specs=[vmem] * 8 + [smem] * 2 + [vmem] * 6,
        out_specs=(vmem, vmem),
        scratch_shapes=[
            pltpu.VMEM((9, 8, LANES), F32),
            pltpu.VMEM((3, 8, LANES), F32),
            pltpu.VMEM((15, 8, LANES), F32),
            pltpu.VMEM((15, 8, LANES), F32),
            pltpu.VMEM((slots, LANES), F32),
            pltpu.VMEM((chunks * 8, LANES), F32),
            pltpu.VMEM((4, 8, LANES), F32),
            pltpu.VMEM((13, chunks, 8, LANES), F32),
            pltpu.VMEM((chunks * 128, LANES), F32),
            pltpu.VMEM((chunks * 128, LANES), F32),
            pltpu.VMEM((chunks * 192, LANES), F32),
            pltpu.VMEM((chunks * 64 + 64, LANES), F32),
            pltpu.VMEM((atoms // GROUP, ch, LANES), F32),
            pltpu.VMEM((8, ch, 3 * ch), BF16),
            pltpu.VMEM((ch, 48), BF16),
            pltpu.VMEM((ch, LANES), F32),
            pltpu.VMEM((per_block, ch, LANES), F32),
            pltpu.VMEM((per_block, ch, LANES), F32),
            pltpu.VMEM((per_block, ch, LANES), F32),
            pltpu.VMEM((per_block, ch, LANES), F32),
            pltpu.VMEM((per_block, ch, LANES), F32),
            pltpu.VMEM((9, ch, LANES), F32),
            pltpu.VMEM((9, ch, LANES), F32),
            pltpu.VMEM((3, 64, LANES), F32),
            dma((9,)),
            dma((9,)),
            dma((3,)),
            dma((3,)),
            dma((15,)),
            dma((15,)),
        ],
        compiler_params=pltpu.CompilerParams(
            collective_id=0, has_side_effects=True, vmem_limit_bytes=32 * 1024 * 1024
        ),
    )(*args)


def solution(mesh):
    block4 = P("gx", "yz", None, None)
    block3 = P("gx", "yz", None)
    return jax.shard_map(
        on_device,
        mesh=mesh,
        in_specs=(block4, block4, block4, block3) + (block4,) * 6 + (P(),) * 6,
        out_specs=(block4, block4),
        check_vma=False,
    )
```

```python
import jax
import jax.numpy as jnp
from jax import lax
from jax.experimental import pallas as pl
from jax.experimental.pallas import tpu as pltpu
from jax.sharding import PartitionSpec as P

PX = 4
PY = 4
PZ = 5
STEPS = 1
SPACING = 2.15
CUTOFF = 6.0
TIME_STEP = 0.05
ENV_SCALE = 0.125
MASSES = (1.008, 12.011, 14.007, 15.999, 32.06)
HIGHEST = lax.Precision.HIGHEST
MESH = pl.DeviceIdType.MESH
F32 = jnp.float32
BF16 = jnp.bfloat16
I32 = jnp.int32

LANES = 128
GROUP = 16
PI = 3.141592653589793
R3 = 3.0**0.5
R5 = 5.0**0.5
R15 = 15.0**0.5

HALO = [(dx, dy) for dy in (-1, 0, 1) for dx in (-1, 0, 1)]
NEAR = [pos for pos in HALO if pos != (0, 0)]
TARGETS = [(dx, dy) for dy in (-1, 0, 1) for dx in (-2, -1, 0, 1, 2)]
FAR = [pos for pos in TARGETS if pos != (0, 0)]


def halo_slot(dx, dy):
    return (dy + 1) * 3 + dx + 1


def target_slot(dx, dy):
    return (dy + 1) * 5 + dx + 2


def nt_dot(a, b, precision=None):
    return lax.dot_general(
        a, b, (((1,), (1,)), ((), ())), precision=precision, preferred_element_type=F32
    )


def nn_dot(a, b, precision=None):
    return jnp.dot(a, b, precision=precision, preferred_element_type=F32)


def halves(x):
    high = x.astype(BF16)
    low = (x - high.astype(F32)).astype(BF16)
    return high, low


def left_parts(w):
    high, low = halves(w)
    return jnp.concatenate([high, high, low], axis=1)


def right_parts(x):
    high, low = halves(x)
    return jnp.concatenate([high, low, high], axis=0)


def pick(rows, index):
    return jnp.take_along_axis(rows, index, axis=1, mode="promise_in_bounds")


def sigmoid(x):
    return 0.5 * jnp.tanh(0.5 * x) + 0.5


def kernel_body(
    period,
    atoms,
    slots,
    *refs,
):
    raw, refs = refs[:16], refs[16:]
    (
        nv_ref,
        ntr_ref,
        staged,
        halo,
        load,
        ret_out,
        ret_in,
        nb_pad,
        rows_code,
        table,
        sc,
        zf,
        zy,
        zd,
        pt,
        cterm,
        mats,
        w1s,
        wcol,
        w0pad,
        rhs,
        s1_s,
        ds_s,
        hid_s,
        dpt_s,
        g3,
        load_sems,
        halo_send,
        halo_recv,
        load_send,
        load_recv,
        ret_send,
        ret_recv,
    ) = refs
    gx = lax.axis_index("gx")
    yz = lax.axis_index("yz")
    n_gx = lax.axis_size("gx")
    n_yz = lax.axis_size("yz")
    blocks = atoms // GROUP
    per_block = slots // 8
    n_rows = blocks * per_block
    chunks = (n_rows + 7) // 8

    def device(dx, dy):
        return (lax.rem(gx + dx + n_gx, n_gx), lax.rem(yz + dy + n_yz, n_yz))

    barrier = pltpu.get_barrier_semaphore()
    for dx, dy in FAR:
        pl.semaphore_signal(barrier, inc=1, device_id=device(dx, dy), device_id_type=MESH)

    loads = []
    for at, (far, close) in enumerate(zip(raw, staged)):
        copy = pltpu.make_async_copy(far, close, load_sems.at[at])
        copy.start()
        loads.append(copy)
    (
        pos_ref,
        vel_ref,
        frc_ref,
        spc_ref,
        nbr_ref,
        msk_ref,
        sx_ref,
        sy_ref,
        ms_ref,
        mr_ref,
        wb_ref,
        ec_ref,
        en_ref,
        we_ref,
        wl_ref,
        wo_ref,
    ) = staged
    first = (0, 1, 2, 3, 6, 7, 8, 9)
    for at in first:
        loads[at].wait()

    lane1 = lax.broadcasted_iota(I32, (1, LANES), 1)
    lane8 = lax.broadcasted_iota(I32, (8, LANES), 1)
    sub8 = lax.broadcasted_iota(I32, (8, LANES), 0)

    own = halo_slot(0, 0)
    kinds = spc_ref[0].astype(F32)
    minv = jnp.zeros_like(kinds)
    for kind, mass in enumerate(MASSES):
        minv = jnp.where(kinds == float(kind), 1.0 / jnp.float32(mass), minv)
    halo[own] = jnp.zeros((8, LANES), F32)
    load[1] = jnp.zeros((8, LANES), F32)
    for c in range(3):
        start = pos_ref[0, c]
        velocity = vel_ref[0, c] + 0.5 * TIME_STEP * frc_ref[0, c] * minv
        coords = start + TIME_STEP * velocity
        halo[own, c : c + 1, 0:atoms] = coords
        load[1, c : c + 1, 0:atoms] = velocity
        load[1, c + 3 : c + 4, 0:atoms] = (coords - start) / (STEPS * TIME_STEP)
    halo[own, 3:4, 0:atoms] = kinds
    code = lane1
    place = lane1
    source = lane1
    for side in (0, 1):
        for k in range(ms_ref.shape[3]):
            seat = atoms + 5 * (1 - side) + k
            code = jnp.where(lane1 == mr_ref[0, 0, side, k], LANES - 1, code)
    for side in (0, 1):
        for k in range(ms_ref.shape[3]):
            seat = atoms + 5 * (1 - side) + k
            gone = ms_ref[0, 0, side, k]
            code = jnp.where(lane1 == gone, (2 * side - 1) * LANES + seat, code)
            place = jnp.where(lane1 == seat, gone, place)
            source = jnp.where(lane1 == gone, LANES - 1, source)
    for side in (0, 1):
        for k in range(ms_ref.shape[3]):
            source = jnp.where(lane1 == mr_ref[0, 0, side, k], atoms + 5 * side + k, source)
    code = jnp.where(lane1 < atoms, code + LANES, 0)
    halo[own, 4:5, :] = code.astype(F32)
    halo[own, 6:8, 0:atoms] = sy_ref[0, 0].astype(F32)
    load[1, 6:7, 0:atoms] = minv
    width_x = sx_ref.shape[3]
    g3[0] = jnp.zeros((64, LANES), F32)
    g3[0, 0:2, 0:width_x] = sx_ref[0, 0].astype(F32)
    lists = g3[0, 0:8, :]
    halo[own, 5:6, :] = lists[1:2] + pltpu.roll(lists, width_x, 1)[0:1]
    load[1] = pick(load[1], jnp.broadcast_to(place, (8, LANES)))

    pl.semaphore_wait(barrier, len(FAR))
    sends = []
    for dx, dy in NEAR:
        there = halo_slot(-dx, -dy)
        copy = pltpu.make_async_remote_copy(
            src_ref=halo.at[own],
            dst_ref=halo.at[there],
            send_sem=halo_send.at[there],
            recv_sem=halo_recv.at[there],
            device_id=device(dx, dy),
            device_id_type=MESH,
        )
        copy.start()
        sends.append(copy)
    for dx in (-1, 1):
        there = 1 - dx
        copy = pltpu.make_async_remote_copy(
            src_ref=load.at[1],
            dst_ref=load.at[there],
            send_sem=load_send.at[there],
            recv_sem=load_recv.at[there],
            device_id=device(dx, 0),
            device_id_type=MESH,
        )
        copy.start()
        sends.append(copy)

    for at in range(16):
        if at not in first:
            loads[at].wait()
    nb_pad[...] = jnp.zeros((atoms, LANES), F32)
    nb_pad[:, 0:slots] = nbr_ref[0, 0].astype(F32) + 512.0 * msk_ref[0, 0].astype(F32)
    rows_code[...] = jnp.zeros((chunks * 8, LANES), F32)
    atom_of_lane = lane8 & (GROUP - 1)
    in_row = (lane8 & 7) == sub8
    for block in range(blocks):
        upper = nb_pad[block * GROUP : block * GROUP + 8, :]
        lower = nb_pad[block * GROUP + 8 : block * GROUP + 16, :]
        for jb in range(per_block):
            slot = (lane8 >> 4) + jb * 8
            moved = jnp.where(atom_of_lane < 8, pick(upper, slot), pick(lower, slot))
            row = jnp.sum(jnp.where(in_row, moved, 0.0), axis=0, keepdims=True)
            r = block * per_block + jb
            rows_code[r : r + 1, :] = row

    ch = we_ref.shape[0]
    eye = (
        lax.broadcasted_iota(I32, (ch, ch), 0) == lax.broadcasted_iota(I32, (ch, ch), 1)
    ).astype(F32)
    n_basis = wb_ref.shape[0]
    n_kinds = en_ref.shape[0]
    wl_t = wl_ref[...]
    mixes = []
    for part in range(3):
        part_t = wl_t[:, (part + 1) * ch : (part + 2) * ch]
        mixes.append(ENV_SCALE * nt_dot(part_t, we_ref[...], HIGHEST))
    for part in range(3):
        turned = mixes[part]
        straight = nt_dot(eye, turned, HIGHEST)
        for which, m in enumerate((straight, turned)):
            m_high, m_low = halves(m)
            mats[which, 0, part] = m_high
            mats[which, 1, part] = m_low
    w0_t = wl_t[:, 0:ch]
    w0 = nt_dot(eye, w0_t, HIGHEST)
    ec = nt_dot(eye, ec_ref[...], HIGHEST)
    w0pad[...] = jnp.zeros((2, ch, LANES), F32)
    w0pad[0, :, GROUP : GROUP + ch] = w0_t
    w0pad[1, :, GROUP + ch : GROUP + 2 * ch] = w0
    w1f = jnp.concatenate(
        [
            nt_dot(eye, wb_ref[...], HIGHEST),
            nt_dot(eye, en_ref[...], HIGHEST),
            jnp.zeros((ch, 16 - n_basis - n_kinds), F32),
        ],
        axis=1,
    )
    w1s[...] = left_parts(w1f)
    row32 = lax.broadcasted_iota(I32, (32, LANES), 0)
    lane32 = lax.broadcasted_iota(I32, (32, LANES), 1)
    g3[1, 0:32, :] = jnp.zeros((32, LANES), F32)
    g3[1, 0:n_basis, 0:ch] = wb_ref[...]
    head = g3[1, 0:32, :] + jnp.where(
        (row32 == 8) & (lane32 >= ch) & (lane32 < 2 * ch), 1.0, 0.0
    ) + jnp.where((lane32 >= 2 * ch) & (row32 == 16 + ((lane32 - 2 * ch) >> 4)), 1.0, 0.0)
    rest = jnp.where(row32 == 16 + ((lane32 + LANES - 2 * ch) >> 4), 1.0, 0.0)
    w_last = jnp.concatenate([head, rest], axis=1).astype(BF16)[:, 0 : 2 * ch + LANES]
    wcol[...] = jnp.broadcast_to(
        jnp.sum(jnp.where(eye > 0, wo_ref[...], 0.0), axis=1, keepdims=True), (ch, LANES)
    )

    for copy in sends:
        copy.wait()

    def shifted(dx, dy):
        step = float(LANES * ((dy + 1) * 5 + dx + 1))
        return halo[halo_slot(dx, dy)] + jnp.where(sub8 == 4, step, 0.0)

    def row_index(rows, which):
        return jnp.broadcast_to(rows[which : which + 1, :], (8, LANES)).astype(I32)

    def x_ghosts(dy):
        low, high = shifted(-1, dy), shifted(1, dy)
        return jnp.where(
            lane8 < width_x,
            pick(low, row_index(low, 5)),
            pick(high, row_index(high, 5)),
        )

    def y_ghosts(dy):
        base = shifted(0, dy)
        index = row_index(base, 7 if dy < 0 else 6)
        outer = index >= atoms
        return jnp.where(
            outer,
            pick(x_ghosts(dy), jnp.where(outer, index - atoms, 0)),
            pick(base, jnp.where(outer, 0, index)),
        )

    table[0] = shifted(0, 0)
    table[1] = x_ghosts(0)
    table[2] = y_ghosts(-1)
    table[3] = y_ghosts(1)

    def whole(k, c):
        return jnp.broadcast_to(table[k, c : c + 1, :], (8, LANES))

    def forward_chunk(i, carry):
        word = rows_code[pl.ds(i * 8, 8), :]
        live = word >= 512.0
        n = jnp.where(live, word - 512.0, word).astype(I32)
        k = jnp.where(n >= atoms, 1, 0) + jnp.where(n >= 2 * atoms, 1, 0) + jnp.where(n >= 3 * atoms, 1, 0)
        n = n - atoms * k
        near = []
        for c in range(5):
            v = pick(whole(0, c), n)
            for part in (1, 2, 3):
                v = jnp.where(k == part, pick(whole(part, c), n), v)
            near.append(v)
        row = i * 8 + sub8
        block = jnp.zeros((8, LANES), I32)
        for b in range(1, blocks):
            block = block + jnp.where(row >= b * per_block, 1, 0)
        centre = block * GROUP + (lane8 & (GROUP - 1))
        off = []
        for c in range(3):
            d = near[c] - pick(whole(0, c), centre)
            d = d - period[c] * jnp.floor(d / period[c] + 0.5)
            off.append(jnp.where(live, d, SPACING if c == 0 else 0.0))
        radius = jnp.sqrt(off[0] * off[0] + off[1] * off[1] + off[2] * off[2])
        rinv = 1.0 / radius
        ux, uy, uz = (o * rinv for o in off)
        q = radius / CUTOFF
        valid = jnp.logical_and(live, q < 1.0)
        q2 = q * q
        q5 = q2 * q2 * q
        q6 = q5 * q
        env = jnp.where(valid, 1.0 + q6 * (-28.0 + q * (48.0 - 21.0 * q)), 0.0)
        denv = jnp.where(valid, (168.0 / CUTOFF) * q5 * (-1.0 + q * (2.0 - q)), 0.0)
        u = PI * jnp.minimum(q, 1.0) - 0.5 * PI
        w = u * u
        sin1 = 1.0 + w * (-1 / 2 + w * (1 / 24 + w * (-1 / 720 + w * (1 / 40320 + w * (-1 / 3628800 + w * (1 / 479001600))))))
        cos1 = -u * (1.0 + w * (-1 / 6 + w * (1 / 120 + w * (-1 / 5040 + w * (1 / 362880 + w * (-1 / 39916800 + w * (1 / 6227020800)))))))
        sc[0, i] = ux
        sc[1, i] = uy
        sc[2, i] = uz
        sc[3, i] = rinv
        sc[4, i] = denv
        zbase = i * 128
        scale = (2.0 / CUTOFF) ** 0.5 * rinv
        s_prev, s_now = jnp.zeros_like(sin1), sin1
        c_prev, c_now = jnp.ones_like(cos1), cos1
        for order in range(1, n_basis + 1):
            bes = scale * s_now
            zf[pl.ds(zbase + order - 1, 8, stride=16), :] = bes
            sc[4 + order, i] = scale * (order * PI / CUTOFF) * c_now - bes * rinv
            s_prev, s_now = s_now, 2.0 * cos1 * s_now - s_prev
            c_prev, c_now = c_now, 2.0 * cos1 * c_now - c_prev
        for kind in range(n_kinds):
            zf[pl.ds(zbase + n_basis + kind, 8, stride=16), :] = jnp.where(near[3] == float(kind), 1.0, 0.0)
        for extra in range(n_basis + n_kinds, 16):
            zf[pl.ds(zbase + extra, 8, stride=16), :] = jnp.zeros((8, LANES), F32)
        ys = (
            R3 * ux,
            R3 * uy,
            R3 * uz,
            R15 * ux * uy,
            R15 * uy * uz,
            0.5 * R5 * (3.0 * uz * uz - 1.0),
            R15 * ux * uz,
            0.5 * R15 * (ux * ux - uy * uy),
        )
        for m, y in enumerate(ys):
            zy[pl.ds(zbase + m, 8, stride=16), :] = y
        zy[pl.ds(zbase + 8, 8, stride=16), :] = env
        dest = near[4].astype(I32)
        tbase = i * 64
        pt[pl.ds(tbase + 6, 8, stride=8), :] = (dest >> 7).astype(F32)
        pt[pl.ds(tbase + 7, 8, stride=8), :] = (dest & (LANES - 1)).astype(F32)
        return carry

    for i in range(chunks):
        forward_chunk(i, 0)

    for block in range(blocks):
        spread = (lane8 & (GROUP - 1)) + block * GROUP
        kind_row = jnp.broadcast_to(pick(whole(0, 3), spread)[0:1], (ch, LANES))
        term = jnp.zeros((ch, LANES), F32)
        for kind in range(n_kinds):
            term = jnp.where(
                kind_row == float(kind),
                jnp.broadcast_to(ec[:, kind : kind + 1], (ch, LANES)),
                term,
            )
        cterm[block] = term

    n_harm = 8
    wide = n_harm * GROUP
    own_lane = lax.broadcasted_iota(I32, (GROUP, LANES), 0) == (
        lax.broadcasted_iota(I32, (GROUP, LANES), 1) & (GROUP - 1)
    )
    every = jnp.concatenate([own_lane] * n_harm, axis=0)
    ones_row = jnp.where(own_lane, 1.0, 0.0).astype(BF16)
    at_ef = wide + GROUP
    at_dlp = at_ef + ch

    def by_degree(which, sums):
        parts = []
        for degree, (a, b) in ((1, (0, 3)), (2, (3, n_harm)), (0, (n_harm, n_harm + 1))):
            rows = sums[a * GROUP : b * GROUP]
            parts.append(exact_dot(rows, which, degree))
        return jnp.concatenate(parts, axis=0)

    def exact_dot(rows, which, degree):
        high, low = halves(rows)
        m_high, m_low = mats[which, 0, degree], mats[which, 1, degree]
        return nn_dot(high, m_high) + nn_dot(low, m_high) + nn_dot(high, m_low)

    def as_left(turned, pad):
        tall_one = jnp.concatenate([turned, jnp.zeros((2 * LANES - wide - GROUP, ch), F32)], axis=0)
        left = tall_one.T
        return jnp.concatenate([left[:, 0:LANES], left[:, LANES:] + pad], axis=1).astype(BF16)

    w_out = wcol[...]
    kept = {}

    def env_row(row):
        return zy[row * 16 + 8 : row * 16 + 9, :]

    def stage_pre(b):
        base = b * per_block
        feats = jnp.concatenate(
            [zf[(base + jb) * 16 : (base + jb + 1) * 16, :] for jb in range(per_block)], axis=1
        )
        kept["pre", b] = nn_dot(w1s[...], right_parts(feats))

    def stage_feat(b):
        centre_term = cterm[b]
        pre = kept.pop(("pre", b))
        for jb in range(per_block):
            row = b * per_block + jb
            cols = slice(jb * LANES, (jb + 1) * LANES)
            z = zy[row * 16 : row * 16 + 16, :]
            env = z[8:9]
            p = pre[:, cols] + centre_term
            sig = sigmoid(p)
            s1 = p * sig
            s1_s[row] = s1
            ds_s[row] = (sig + s1 * (1.0 - sig)) * env
            rhs[b, at_ef : at_ef + ch, cols] = (s1 * env).astype(BF16)
            for m in range(n_harm):
                rhs[b, m * GROUP : (m + 1) * GROUP, cols] = jnp.where(own_lane, z[m : m + 1], 0.0).astype(BF16)
            rhs[b, wide : wide + GROUP, cols] = ones_row

    def stage_env(b):
        sums = nt_dot(rhs[b, 0:at_ef, :], rhs[b, at_ef : at_ef + ch, :])
        grown = by_degree(0, sums)
        kept["g", b] = grown[0:wide]
        left = as_left(grown, w0pad[0])
        kept["lp", b] = nn_dot(left[:, 0:at_dlp], rhs[b, 0:at_dlp, :])

    def stage_latent(b):
        lp_all = kept.pop(("lp", b))
        for jb in range(per_block):
            row = b * per_block + jb
            cols = slice(jb * LANES, (jb + 1) * LANES)
            env = env_row(row)
            lp = lp_all[:, cols]
            sig = sigmoid(lp)
            lat = lp * sig
            hid_s[row] = w_out * (s1_s[row] * env + lat)
            dlp = (w_out * env) * (sig + lat * (1.0 - sig))
            rhs[b, at_dlp : at_dlp + ch, cols] = dlp.astype(BF16)

    def stage_back(b):
        sums = nt_dot(rhs[b, 0:at_ef, :], rhs[b, at_dlp : at_dlp + ch, :])
        grown = by_degree(1, sums)
        left = as_left(grown, w0pad[1])
        kept["de", b] = nn_dot(left[:, 0 : at_dlp + ch], rhs[b])
        both = jnp.concatenate([grown[0:wide], kept.pop(("g", b))], axis=1).astype(BF16)
        kept["dy", b] = nn_dot(both, rhs[b, at_ef : at_dlp + ch, :])

    def stage_edge(b):
        de_all = kept.pop(("de", b))
        dy_all = kept.pop(("dy", b))
        for jb in range(per_block):
            row = b * per_block + jb
            cols = slice(jb * LANES, (jb + 1) * LANES)
            de = de_all[:, cols] + w_out * env_row(row)
            dpt_s[b, 0:ch, cols] = (de * ds_s[row]).astype(BF16)
            dpt_s[b, ch : 2 * ch, cols] = (hid_s[row] + de * s1_s[row]).astype(BF16)
            dpt_s[b, 2 * ch :, cols] = jnp.where(every, dy_all[:, cols], 0.0).astype(BF16)

    def stage_fold(b):
        got = nn_dot(w_last, dpt_s[b])
        for jb in range(per_block):
            row = b * per_block + jb
            zd[row * 24 : row * 24 + 24, :] = got[0:24, jb * LANES : (jb + 1) * LANES]

    stages = (stage_pre, stage_feat, stage_env, stage_latent, stage_back, stage_edge, stage_fold)
    for tick in range(len(stages) + blocks - 1):
        for b in range(blocks):
            if 0 <= tick - b < len(stages):
                stages[tick - b](b)
    for row in range(n_rows, chunks * 8):
        zd[row * 24 : row * 24 + 24, :] = jnp.zeros((24, LANES), F32)

    def put_parts(store, values):
        for c in range(3):
            high = values[c].astype(BF16).astype(F32)
            store(c, high)
            store(c + 3, values[c] - high)

    def backward_chunk(i, carry):
        zbase = i * 192

        def d(which):
            return zd[pl.ds(zbase + which, 8, stride=24), :]

        ux, uy, uz, rinv, denv = (sc[t, i] for t in range(5))
        dr = d(8) * denv
        for order in range(n_basis):
            dr = dr + d(order) * sc[5 + order, i]
        d1, d2, d3, d4, d5, d6, d7, d8 = (d(16 + m) for m in range(8))
        dux = R3 * d1 + R15 * (uy * d4 + uz * d7 + ux * d8)
        duy = R3 * d2 + R15 * (ux * d4 + uz * d5 - uy * d8)
        duz = R3 * d3 + R15 * (uy * d5 + ux * d7) + (3.0 * R5) * uz * d6
        radial = dr - rinv * (dux * ux + duy * uy + duz * uz)
        forces = [-(radial * u + rinv * du) for u, du in ((ux, dux), (uy, duy), (uz, duz))]
        at = pl.ds(i * 8, 8)
        for c in range(3):
            g3[c, at, :] = forces[c]

        def store(which, value):
            pt[pl.ds(i * 64 + which, 8, stride=8), :] = value

        put_parts(store, forces)
        return carry

    for i in range(chunks):
        backward_chunk(i, 0)

    extra = chunks * 8
    pt[extra * 8 :, :] = jnp.zeros((8 * 8, LANES), F32)
    for block in range(blocks):
        at = (extra + block) * 8
        sums = [
            -jnp.sum(g3[c, block * per_block : (block + 1) * per_block, :], axis=0, keepdims=True)
            for c in range(3)
        ]

        def store(which, value):
            pt[at + which : at + which + 1, :] = value

        put_parts(store, sums)
        spread = (lane8 & (GROUP - 1)) + block * GROUP
        dest = pick(whole(0, 4), spread)[0:1].astype(I32)
        pt[at + 6 : at + 7, :] = (dest >> 7).astype(F32)
        pt[at + 7 : at + 8, :] = (dest & (LANES - 1)).astype(F32)

    n_targets = len(TARGETS)
    tall = 96
    sub16 = lax.broadcasted_iota(I32, (16, LANES), 0)
    pair = jnp.where(sub16 >= 8, 1.0, 0.0)
    pairs = [(pair + 2.0 * b).astype(BF16) for b in range((n_targets + 1) // 2)]
    steps = [(sub16 + 16 * b).astype(F32).astype(BF16) for b in range(tall // 16)]
    zero16 = jnp.zeros((16, LANES), BF16)
    one16 = jnp.ones((16, LANES), BF16)

    def scatter_body(i, acc):
        lefts, rights = [], []
        for t in range(8):
            v = pt[pl.ds(pl.multiple_of((i * 8 + t) * 8, 8), 8), :]
            where_to = jnp.broadcast_to(v[6:7], (16, LANES)).astype(BF16)
            lo = jnp.broadcast_to(v[7:8], (16, LANES)).astype(BF16)
            twice = jnp.concatenate([v, v], axis=0).astype(BF16)
            lefts.append(jnp.concatenate([jnp.where(where_to == p, twice, zero16) for p in pairs], axis=0))
            rights.append(jnp.concatenate([jnp.where(lo == p, one16, zero16) for p in steps], axis=0))
        left = jnp.concatenate(lefts, axis=1)
        right = jnp.concatenate(rights, axis=1)
        return acc + nt_dot(left, right)

    spread_out = lax.fori_loop(
        0, chunks + 1, scatter_body, jnp.zeros((len(pairs) * 16, tall), F32)
    )
    for t in range(n_targets):
        ret_out[t] = jnp.zeros((8, LANES), F32)
        ret_out[t, :, 0:tall] = spread_out[t * 8 : t * 8 + 8, :]

    sends = []
    for dx, dy in FAR:
        there = target_slot(-dx, -dy)
        copy = pltpu.make_async_remote_copy(
            src_ref=ret_out.at[target_slot(dx, dy)],
            dst_ref=ret_in.at[there],
            send_sem=ret_send.at[there],
            recv_sem=ret_recv.at[there],
            device_id=device(dx, dy),
            device_id_type=MESH,
        )
        copy.start()
        sends.append(copy)

    settle = jnp.broadcast_to(source, (8, LANES))
    mine, low, high = load[1], load[0], load[2]
    held = jnp.where(lane8 < atoms, mine, jnp.where(lane8 < atoms + 5, low, high))
    held = jnp.where(lane8 < LANES - 1, held, 0.0)
    held = pick(held, settle)
    total = ret_out[target_slot(0, 0)]
    for copy, (dx, dy) in zip(sends, FAR):
        copy.wait()
    for dx, dy in FAR:
        total = total + ret_in[target_slot(dx, dy)]
    force = pick(total, settle)
    force = force[0:3] + force[3:6]
    fresh = held[0:3] + 0.5 * TIME_STEP * force * held[6:7]
    for c in range(3):
        nv_ref[0, c] = fresh[c : c + 1, 0:atoms]
        ntr_ref[0, c] = held[c + 3 : c + 4, 0:atoms]


def on_device(*args):
    atoms = args[0].shape[3]
    slots = args[4].shape[2]
    ch = args[13].shape[0]
    chunks = (atoms // GROUP * (slots // 8) + 7) // 8
    n_gx, n_yz = lax.axis_size("gx"), lax.axis_size("yz")
    period = (n_gx * PX * SPACING, n_yz * PY * SPACING, PZ * SPACING)
    pos, vel, frc, spc, nbr, msk, sx, sy, ms, mr, wb, ec, en, we, wl, wo = args
    pos, vel, frc = (x.transpose(0, 2, 1, 3) for x in (pos, vel, frc))
    nbr, msk = (x.transpose(0, 1, 3, 2) for x in (nbr, msk))
    args = (pos, vel, frc, spc, nbr, msk, sx, sy, ms, mr, wb, ec.T, en.T, we, wl.T, wo.reshape(1, ch))

    def body(*refs):
        kernel_body(period, atoms, slots, *refs)

    vmem = pl.BlockSpec(memory_space=pltpu.VMEM)
    per_block = slots // 8
    blocks = atoms // GROUP
    dma = pltpu.SemaphoreType.DMA
    out = jax.ShapeDtypeStruct((1, 3, 1, atoms), F32)
    staged = tuple(
        (pltpu.SMEM if at in (8, 9) else pltpu.VMEM)(x.shape, x.dtype) for at, x in enumerate(args)
    )
    velocity, travel = pl.pallas_call(
        body,
        out_shape=(out, out),
        in_specs=[pl.BlockSpec(memory_space=pl.ANY)] * 16,
        out_specs=(vmem, vmem),
        scratch_shapes=[
            staged,
            pltpu.VMEM((9, 8, LANES), F32),
            pltpu.VMEM((3, 8, LANES), F32),
            pltpu.VMEM((15, 8, LANES), F32),
            pltpu.VMEM((15, 8, LANES), F32),
            pltpu.VMEM((atoms, LANES), F32),
            pltpu.VMEM((chunks * 8, LANES), F32),
            pltpu.VMEM((4, 8, LANES), F32),
            pltpu.VMEM((13, chunks, 8, LANES), F32),
            pltpu.VMEM((chunks * 128, LANES), F32),
            pltpu.VMEM((chunks * 128, LANES), F32),
            pltpu.VMEM((chunks * 192, LANES), F32),
            pltpu.VMEM((chunks * 64 + 64, LANES), F32),
            pltpu.VMEM((atoms // GROUP, ch, LANES), F32),
            pltpu.VMEM((2, 2, 3, ch, ch), BF16),
            pltpu.VMEM((ch, 48), BF16),
            pltpu.VMEM((ch, LANES), F32),
            pltpu.VMEM((2, ch, LANES), F32),
            pltpu.VMEM((blocks, 9 * GROUP + 2 * ch, per_block * LANES), BF16),
            pltpu.VMEM((blocks * per_block, ch, LANES), F32),
            pltpu.VMEM((blocks * per_block, ch, LANES), F32),
            pltpu.VMEM((blocks * per_block, ch, LANES), F32),
            pltpu.VMEM((blocks, 2 * ch + 8 * GROUP, per_block * LANES), BF16),
            pltpu.VMEM((3, 64, LANES), F32),
            dma((16,)),
            dma((9,)),
            dma((9,)),
            dma((3,)),
            dma((3,)),
            dma((15,)),
            dma((15,)),
        ],
        compiler_params=pltpu.CompilerParams(
            collective_id=0, has_side_effects=True, vmem_limit_bytes=60 * 1024 * 1024
        ),
    )(*args)
    return velocity.transpose(0, 2, 1, 3), travel.transpose(0, 2, 1, 3)


def solution(mesh):
    block4 = P("gx", "yz", None, None)
    block3 = P("gx", "yz", None)
    return jax.shard_map(
        on_device,
        mesh=mesh,
        in_specs=(block4, block4, block4, block3) + (block4,) * 6 + (P(),) * 6,
        out_specs=(block4, block4),
        check_vma=False,
    )
```

```python
import jax
import jax.numpy as jnp
from jax import lax
from jax.experimental import pallas as pl
from jax.experimental.pallas import tpu as pltpu
from jax.sharding import PartitionSpec as P

PX = 4
PY = 4
PZ = 5
STEPS = 1
SPACING = 2.15
CUTOFF = 6.0
TIME_STEP = 0.05
ENV_SCALE = 0.125
MASSES = (1.008, 12.011, 14.007, 15.999, 32.06)
HIGHEST = lax.Precision.HIGHEST
MESH = pl.DeviceIdType.MESH
F32 = jnp.float32
BF16 = jnp.bfloat16
I32 = jnp.int32

LANES = 128
GROUP = 8
PI = 3.141592653589793
R3 = 3.0**0.5
R5 = 5.0**0.5
R15 = 15.0**0.5

HALO = [(dx, dy) for dy in (-1, 0, 1) for dx in (-1, 0, 1)]
NEAR = [pos for pos in HALO if pos != (0, 0)]
TARGETS = [(dx, dy) for dy in (-1, 0, 1) for dx in (-2, -1, 0, 1, 2)]
FAR = [pos for pos in TARGETS if pos != (0, 0)]


def halo_slot(dx, dy):
    return (dy + 1) * 3 + dx + 1


def target_slot(dx, dy):
    return (dy + 1) * 5 + dx + 2


def nt_dot(a, b, precision=None):
    return lax.dot_general(
        a, b, (((1,), (1,)), ((), ())), precision=precision, preferred_element_type=F32
    )


def nn_dot(a, b, precision=None):
    return jnp.dot(a, b, precision=precision, preferred_element_type=F32)


def halves(x):
    high = x.astype(BF16)
    low = (x - high.astype(F32)).astype(BF16)
    return high, low


def pick(rows, index):
    return jnp.take_along_axis(rows, index, axis=1, mode="promise_in_bounds")


def turn(eye, x):
    high, low = halves(x)
    return nt_dot(eye, high) + nt_dot(eye, low)


def split_dot(left, right):
    high, low = halves(left)
    return nn_dot(high, right) + nn_dot(low, right)


def sigmoid(x):
    return 0.5 * jnp.tanh(0.5 * x) + 0.5


def kernel_body(
    period,
    atoms,
    slots,
    *refs,
):
    raw, refs = refs[:16], refs[16:]
    (
        both_ref,
        staged,
        halo,
        load,
        ret_out,
        ret_in,
        nb_pad,
        rows_code,
        table,
        sc,
        zf,
        zy,
        zd,
        pt,
        cterm,
        mats,
        w1s,
        wcol,
        w0pad,
        rhs,
        s1_s,
        ds_s,
        hid_s,
        dpt_s,
        g3,
        load_sems,
        halo_send,
        halo_recv,
        load_send,
        load_recv,
        ret_send,
        ret_recv,
    ) = refs
    gx = lax.axis_index("gx")
    yz = lax.axis_index("yz")
    n_gx = lax.axis_size("gx")
    n_yz = lax.axis_size("yz")
    blocks = atoms // GROUP
    per_block = slots // 16
    n_rows = blocks * per_block
    chunks = (n_rows + 7) // 8

    def device(dx, dy):
        return (lax.rem(gx + dx + n_gx, n_gx), lax.rem(yz + dy + n_yz, n_yz))

    barrier = pltpu.get_barrier_semaphore()
    loads = []
    first = (0, 1, 2, 3, 6, 7, 8, 9)
    for at, (far, close) in enumerate(zip(raw, staged)):
        loads.append(pltpu.make_async_copy(far, close, load_sems.at[at]))
    for at in first:
        loads[at].start()
    for dx, dy in FAR:
        pl.semaphore_signal(barrier, inc=1, device_id=device(dx, dy), device_id_type=MESH)

    for at in range(16):
        if at not in first:
            loads[at].start()
    (
        pos_ref,
        vel_ref,
        frc_ref,
        spc_ref,
        nbr_ref,
        msk_ref,
        sx_ref,
        sy_ref,
        ms_ref,
        mr_ref,
        wb_ref,
        ec_ref,
        en_ref,
        we_ref,
        wl_ref,
        wo_ref,
    ) = staged
    for at in first:
        loads[at].wait()

    lane1 = lax.broadcasted_iota(I32, (1, LANES), 1)
    lane8 = lax.broadcasted_iota(I32, (8, LANES), 1)
    sub8 = lax.broadcasted_iota(I32, (8, LANES), 0)

    own = halo_slot(0, 0)
    kinds = spc_ref[0].astype(F32)
    minv = jnp.zeros_like(kinds)
    for kind, mass in enumerate(MASSES):
        minv = jnp.where(kinds == float(kind), 1.0 / jnp.float32(mass), minv)
    halo[own] = jnp.zeros((8, LANES), F32)
    load[1] = jnp.zeros((8, LANES), F32)
    for c in range(3):
        start = pos_ref[0, c]
        velocity = vel_ref[0, c] + 0.5 * TIME_STEP * frc_ref[0, c] * minv
        coords = start + TIME_STEP * velocity
        halo[own, c : c + 1, 0:atoms] = coords
        load[1, c : c + 1, 0:atoms] = velocity
        load[1, c + 3 : c + 4, 0:atoms] = (coords - start) / (STEPS * TIME_STEP)
    halo[own, 3:4, 0:atoms] = kinds
    code = lane1
    place = lane1
    source = lane1
    for side in (0, 1):
        for k in range(ms_ref.shape[3]):
            seat = atoms + 5 * (1 - side) + k
            code = jnp.where(lane1 == mr_ref[0, 0, side, k], LANES - 1, code)
    for side in (0, 1):
        for k in range(ms_ref.shape[3]):
            seat = atoms + 5 * (1 - side) + k
            gone = ms_ref[0, 0, side, k]
            code = jnp.where(lane1 == gone, (2 * side - 1) * LANES + seat, code)
            place = jnp.where(lane1 == seat, gone, place)
            source = jnp.where(lane1 == gone, LANES - 1, source)
    for side in (0, 1):
        for k in range(ms_ref.shape[3]):
            source = jnp.where(lane1 == mr_ref[0, 0, side, k], atoms + 5 * side + k, source)
    code = jnp.where(lane1 < atoms, code + LANES, 0)
    halo[own, 4:5, :] = code.astype(F32)
    halo[own, 6:8, 0:atoms] = sy_ref[0, 0].astype(F32)
    load[1, 6:7, 0:atoms] = minv
    width_x = sx_ref.shape[3]
    g3[0] = jnp.zeros((64, LANES), F32)
    g3[0, 0:2, 0:width_x] = sx_ref[0, 0].astype(F32)
    lists = g3[0, 0:8, :]
    halo[own, 5:6, :] = lists[1:2] + pltpu.roll(lists, width_x, 1)[0:1]
    load[1] = pick(load[1], jnp.broadcast_to(place, (8, LANES)))

    pl.semaphore_wait(barrier, len(FAR))
    sends = []
    for dx, dy in NEAR:
        there = halo_slot(-dx, -dy)
        copy = pltpu.make_async_remote_copy(
            src_ref=halo.at[own],
            dst_ref=halo.at[there],
            send_sem=halo_send.at[there],
            recv_sem=halo_recv.at[there],
            device_id=device(dx, dy),
            device_id_type=MESH,
        )
        copy.start()
        sends.append(copy)
    for dx in (-1, 1):
        there = 1 - dx
        copy = pltpu.make_async_remote_copy(
            src_ref=load.at[1],
            dst_ref=load.at[there],
            send_sem=load_send.at[there],
            recv_sem=load_recv.at[there],
            device_id=device(dx, 0),
            device_id_type=MESH,
        )
        copy.start()
        sends.append(copy)

    for at in range(16):
        if at not in first:
            loads[at].wait()
    nb_pad[...] = jnp.zeros((atoms, LANES), F32)
    nb_pad[:, 0:slots] = nbr_ref[0, 0].astype(F32) + 512.0 * msk_ref[0, 0].astype(F32)
    rows_code[...] = jnp.zeros((chunks * 8, LANES), F32)
    in_row = (lane8 & (GROUP - 1)) == sub8
    for block in range(blocks):
        group = nb_pad[block * GROUP : (block + 1) * GROUP, :]
        for jb in range(per_block):
            moved = pick(group, (lane8 >> 3) + jb * 16)
            row = jnp.sum(jnp.where(in_row, moved, 0.0), axis=0, keepdims=True)
            r = block * per_block + jb
            rows_code[r : r + 1, :] = row

    ch = we_ref.shape[0]
    eye = (
        lax.broadcasted_iota(I32, (ch, ch), 0) == lax.broadcasted_iota(I32, (ch, ch), 1)
    ).astype(F32)
    n_basis = wb_ref.shape[0]
    n_kinds = en_ref.shape[0]
    wl_t = wl_ref[...]
    mixes = []
    eye16 = eye.astype(BF16)
    we_h, we_l = halves(we_ref[...])
    for part in range(3):
        part_t = wl_t[:, (part + 1) * ch : (part + 2) * ch]
        part_h, part_l = halves(part_t)
        mixes.append(ENV_SCALE * (nt_dot(part_h, we_h) + nt_dot(part_l, we_h) + nt_dot(part_h, we_l)))
    for part in range(3):
        turned = mixes[part]
        straight = turn(eye16, turned)
        for which, m in enumerate((straight, turned)):
            m_high, m_low = halves(m)
            mats[which, part] = jnp.concatenate([m_high, m_high, m_low], axis=0)
    w0_t = wl_t[:, 0:ch]
    w0 = turn(eye16, w0_t)
    ec = turn(eye16, ec_ref[...])
    w0pad[...] = jnp.zeros((2, ch, LANES), F32)
    w0pad[0, :, 80 : 80 + ch] = w0_t
    w0pad[1, :, 80 : 80 + ch] = w0
    w1f = jnp.concatenate(
        [
            nt_dot(eye16, wb_ref[...].astype(BF16)),
            nt_dot(eye16, en_ref[...].astype(BF16)),
            jnp.zeros((ch, 16 - n_basis - n_kinds), F32),
        ],
        axis=1,
    )
    w1s[...] = w1f.astype(BF16)
    row32 = lax.broadcasted_iota(I32, (32, LANES), 0)
    lane32 = lax.broadcasted_iota(I32, (32, LANES), 1)
    g3[1, 0:32, :] = jnp.zeros((32, LANES), F32)
    g3[1, 0:n_basis, 0:ch] = wb_ref[...]
    head = g3[1, 0:32, :] + jnp.where(
        (row32 == 8) & (lane32 >= ch) & (lane32 < 2 * ch), 1.0, 0.0
    ) + jnp.where((lane32 >= 2 * ch) & (row32 == 16 + ((lane32 - 2 * ch) >> 3)), 1.0, 0.0)
    w_last = head
    wcol[...] = jnp.broadcast_to(
        jnp.sum(jnp.where(eye > 0, wo_ref[...], 0.0), axis=1, keepdims=True), (ch, LANES)
    )

    for copy in sends:
        copy.wait()

    def shifted(dx, dy):
        step = float(LANES * ((dy + 1) * 5 + dx + 1))
        return halo[halo_slot(dx, dy)] + jnp.where(sub8 == 4, step, 0.0)

    def row_index(rows, which):
        return jnp.broadcast_to(rows[which : which + 1, :], (8, LANES)).astype(I32)

    def x_ghosts(dy):
        low, high = shifted(-1, dy), shifted(1, dy)
        return jnp.where(
            lane8 < width_x,
            pick(low, row_index(low, 5)),
            pick(high, row_index(high, 5)),
        )

    def y_ghosts(dy):
        base = shifted(0, dy)
        index = row_index(base, 7 if dy < 0 else 6)
        outer = index >= atoms
        return jnp.where(
            outer,
            pick(x_ghosts(dy), jnp.where(outer, index - atoms, 0)),
            pick(base, jnp.where(outer, 0, index)),
        )

    table[0] = shifted(0, 0)
    table[1] = x_ghosts(0)
    table[2] = y_ghosts(-1)
    table[3] = y_ghosts(1)

    def whole(k, c):
        return jnp.broadcast_to(table[k, c : c + 1, :], (8, LANES))

    def forward_chunk(i, carry):
        word = rows_code[pl.ds(i * 8, 8), :]
        live = word >= 512.0
        n = jnp.where(live, word - 512.0, word).astype(I32)
        k = jnp.where(n >= atoms, 1, 0) + jnp.where(n >= 2 * atoms, 1, 0) + jnp.where(n >= 3 * atoms, 1, 0)
        n = n - atoms * k
        near = []
        for c in range(5):
            v = pick(whole(0, c), n)
            for part in (1, 2, 3):
                v = jnp.where(k == part, pick(whole(part, c), n), v)
            near.append(v)
        row = i * 8 + sub8
        block = jnp.zeros((8, LANES), I32)
        for b in range(1, blocks):
            block = block + jnp.where(row >= b * per_block, 1, 0)
        centre = block * GROUP + (lane8 & (GROUP - 1))
        off = []
        for c in range(3):
            d = near[c] - pick(whole(0, c), centre)
            d = d - period[c] * jnp.floor(d / period[c] + 0.5)
            off.append(jnp.where(live, d, SPACING if c == 0 else 0.0))
        radius = jnp.sqrt(off[0] * off[0] + off[1] * off[1] + off[2] * off[2])
        rinv = 1.0 / radius
        ux, uy, uz = (o * rinv for o in off)
        q = radius / CUTOFF
        valid = jnp.logical_and(live, q < 1.0)
        q2 = q * q
        q5 = q2 * q2 * q
        q6 = q5 * q
        env = jnp.where(valid, 1.0 + q6 * (-28.0 + q * (48.0 - 21.0 * q)), 0.0)
        denv = jnp.where(valid, (168.0 / CUTOFF) * q5 * (-1.0 + q * (2.0 - q)), 0.0)
        u = PI * jnp.minimum(q, 1.0) - 0.5 * PI
        w = u * u
        sin1 = 1.0 + w * (-1 / 2 + w * (1 / 24 + w * (-1 / 720 + w * (1 / 40320 + w * (-1 / 3628800 + w * (1 / 479001600))))))
        cos1 = -u * (1.0 + w * (-1 / 6 + w * (1 / 120 + w * (-1 / 5040 + w * (1 / 362880 + w * (-1 / 39916800 + w * (1 / 6227020800)))))))
        sc[0, i] = ux
        sc[1, i] = uy
        sc[2, i] = uz
        sc[3, i] = rinv
        sc[4, i] = denv
        zbase = i * 128
        scale = (2.0 / CUTOFF) ** 0.5 * rinv
        s_prev, s_now = jnp.zeros_like(sin1), sin1
        c_prev, c_now = jnp.ones_like(cos1), cos1
        for order in range(1, n_basis + 1):
            bes = scale * s_now
            zf[pl.ds(zbase + order - 1, 8, stride=16), :] = bes
            sc[4 + order, i] = scale * (order * PI / CUTOFF) * c_now - bes * rinv
            s_prev, s_now = s_now, 2.0 * cos1 * s_now - s_prev
            c_prev, c_now = c_now, 2.0 * cos1 * c_now - c_prev
        for kind in range(n_kinds):
            zf[pl.ds(zbase + n_basis + kind, 8, stride=16), :] = jnp.where(near[3] == float(kind), 1.0, 0.0)
        for extra in range(n_basis + n_kinds, 16):
            zf[pl.ds(zbase + extra, 8, stride=16), :] = jnp.zeros((8, LANES), F32)
        ys = (
            R3 * ux,
            R3 * uy,
            R3 * uz,
            R15 * ux * uy,
            R15 * uy * uz,
            0.5 * R5 * (3.0 * uz * uz - 1.0),
            R15 * ux * uz,
            0.5 * R15 * (ux * ux - uy * uy),
        )
        for m, y in enumerate(ys):
            zy[pl.ds(zbase + m, 8, stride=16), :] = y
        zy[pl.ds(zbase + 8, 8, stride=16), :] = env
        dest = near[4].astype(I32)
        tbase = i * 64
        pt[pl.ds(tbase + 6, 8, stride=8), :] = (dest >> 7).astype(F32)
        pt[pl.ds(tbase + 7, 8, stride=8), :] = (dest & (LANES - 1)).astype(F32)
        return carry

    for i in range(chunks):
        forward_chunk(i, 0)

    for block in range(blocks):
        spread = (lane8 & (GROUP - 1)) + block * GROUP
        kind_row = jnp.broadcast_to(pick(whole(0, 3), spread)[0:1], (ch, LANES))
        term = jnp.zeros((ch, LANES), F32)
        for kind in range(n_kinds):
            term = jnp.where(
                kind_row == float(kind),
                jnp.broadcast_to(ec[:, kind : kind + 1], (ch, LANES)),
                term,
            )
        cterm[block] = term

    n_harm = 8
    wide = n_harm * GROUP
    own_lane = (lane8 & (GROUP - 1)) == sub8
    every = jnp.concatenate([own_lane] * n_harm, axis=0)
    ones_row = jnp.concatenate([jnp.where(own_lane, 1.0, 0.0), jnp.zeros((8, LANES), F32)], axis=0).astype(BF16)
    at_ef = wide + 2 * GROUP
    at_dlp = at_ef + ch

    degree_rows = ((1, 0, 3 * GROUP), (2, 3 * GROUP, wide), (0, wide, wide + 2 * GROUP))

    def by_degree(which, sums):
        parts = []
        for degree, a, b in degree_rows:
            grown = exact_dot(jnp.concatenate([x[a:b] for x in sums], axis=0), which, degree)
            parts.append([grown[t * (b - a) : (t + 1) * (b - a)] for t in range(blocks)])
        return [jnp.concatenate([p[t] for p in parts], axis=0) for t in range(blocks)]

    def exact_dot(rows, which, degree):
        high = rows.astype(BF16).astype(F32)
        joined = jnp.concatenate([high, rows - high, high], axis=1).astype(BF16)
        return nn_dot(joined, mats[which, degree])

    def as_left(turned, pad):
        tall_one = jnp.concatenate([turned, jnp.zeros((LANES - at_ef, ch), F32)], axis=0)
        return (tall_one.T + pad)[:, 0:at_dlp]

    w_out = wcol[...]
    kept = {}

    def env_row(row):
        return zy[row * 16 + 8 : row * 16 + 9, :]

    def stage_pre(b):
        base = b * per_block
        feats = jnp.concatenate(
            [zf[(base + jb) * 16 : (base + jb + 1) * 16, :] for jb in range(per_block)], axis=1
        )
        kept["pre", b] = nn_dot(w1s[...], feats.astype(BF16))

    def stage_feat(b):
        centre_term = cterm[b]
        pre = kept.pop(("pre", b))
        for jb in range(per_block):
            row = b * per_block + jb
            cols = slice(jb * LANES, (jb + 1) * LANES)
            z = zy[row * 16 : row * 16 + 16, :]
            env = z[8:9]
            p = pre[:, cols] + centre_term
            sig = sigmoid(p)
            s1 = p * sig
            s1_s[row] = s1
            ds_s[row] = (sig + s1 * (1.0 - sig)) * env
            rhs[b, at_ef : at_ef + ch, cols] = (s1 * env).astype(BF16)
            for m in range(0, n_harm, 2):
                two = [jnp.where(own_lane, z[t : t + 1], 0.0) for t in (m, m + 1)]
                rhs[b, m * GROUP : (m + 2) * GROUP, cols] = jnp.concatenate(two, axis=0).astype(BF16)
            rhs[b, wide : wide + 2 * GROUP, cols] = ones_row

    def stage_env(b):
        kept["f", b] = nt_dot(rhs[b, 0:at_ef, :], rhs[b, at_ef : at_ef + ch, :])

    def stage_grow(b):
        if b == 0:
            grown = by_degree(0, [kept.pop(("f", t)) for t in range(blocks)])
            for t in range(blocks):
                kept["g", t] = grown[t]

    def stage_lp(b):
        left = as_left(kept["g", b], w0pad[0])
        kept["lp", b] = split_dot(left, rhs[b, 0:at_dlp, :])

    def stage_latent(b):
        lp_all = kept.pop(("lp", b))
        for jb in range(per_block):
            row = b * per_block + jb
            cols = slice(jb * LANES, (jb + 1) * LANES)
            env = env_row(row)
            lp = lp_all[:, cols]
            sig = sigmoid(lp)
            lat = lp * sig
            hid_s[row] = w_out * (s1_s[row] * env + lat)
            dlp = (w_out * env) * (sig + lat * (1.0 - sig))
            rhs[b, at_dlp : at_dlp + ch, cols] = dlp.astype(BF16)

    def stage_back(b):
        kept["f", b] = nt_dot(rhs[b, 0:at_ef, :], rhs[b, at_dlp : at_dlp + ch, :])

    def stage_shrink(b):
        if b == 0:
            grown = by_degree(1, [kept.pop(("f", t)) for t in range(blocks)])
            for t in range(blocks):
                kept["d", t] = grown[t]

    def stage_de(b):
        grown = kept.pop(("d", b))
        left = as_left(grown, w0pad[1])
        kept["de", b] = split_dot(left, jnp.concatenate([rhs[b, 0:at_ef, :], rhs[b, at_dlp : at_dlp + ch, :]], axis=0))
        both = jnp.concatenate([grown[0:wide], kept.pop(("g", b))[0:wide]], axis=1)
        kept["dy", b] = nn_dot(both.astype(BF16), rhs[b, at_ef : at_dlp + ch, :])

    def stage_edge(b):
        de_all = kept.pop(("de", b))
        dy_all = kept.pop(("dy", b))
        for jb in range(per_block):
            row = b * per_block + jb
            cols = slice(jb * LANES, (jb + 1) * LANES)
            de = de_all[:, cols] + w_out * env_row(row)
            dpt_s[b, 0:ch, cols] = (de * ds_s[row]).astype(BF16)
            dpt_s[b, ch : 2 * ch, cols] = (hid_s[row] + de * s1_s[row]).astype(BF16)
            dpt_s[b, 2 * ch :, cols] = jnp.where(every, dy_all[:, cols], 0.0).astype(BF16)

    def stage_fold(b):
        got = split_dot(w_last, dpt_s[b])
        for jb in range(per_block):
            row = b * per_block + jb
            zd[row * 24 : row * 24 + 24, :] = got[0:24, jb * LANES : (jb + 1) * LANES]

    stages = (
        stage_pre,
        stage_feat,
        stage_env,
        stage_grow,
        stage_lp,
        stage_latent,
        stage_back,
        stage_shrink,
        stage_de,
        stage_edge,
        stage_fold,
    )
    for stage in stages:
        for b in range(blocks):
            stage(b)
    for row in range(n_rows, chunks * 8):
        zd[row * 24 : row * 24 + 24, :] = jnp.zeros((24, LANES), F32)

    def put_parts(store, values):
        for c in range(3):
            high = values[c].astype(BF16).astype(F32)
            store(c, high)
            store(c + 3, values[c] - high)

    def backward_chunk(i, carry):
        zbase = i * 192

        def d(which):
            return zd[pl.ds(zbase + which, 8, stride=24), :]

        ux, uy, uz, rinv, denv = (sc[t, i] for t in range(5))
        dr = d(8) * denv
        for order in range(n_basis):
            dr = dr + d(order) * sc[5 + order, i]
        d1, d2, d3, d4, d5, d6, d7, d8 = (d(16 + m) for m in range(8))
        dux = R3 * d1 + R15 * (uy * d4 + uz * d7 + ux * d8)
        duy = R3 * d2 + R15 * (ux * d4 + uz * d5 - uy * d8)
        duz = R3 * d3 + R15 * (uy * d5 + ux * d7) + (3.0 * R5) * uz * d6
        radial = dr - rinv * (dux * ux + duy * uy + duz * uz)
        forces = [-(radial * u + rinv * du) for u, du in ((ux, dux), (uy, duy), (uz, duz))]
        at = pl.ds(i * 8, 8)
        for c in range(3):
            g3[c, at, :] = forces[c]

        def store(which, value):
            pt[pl.ds(i * 64 + which, 8, stride=8), :] = value

        put_parts(store, forces)
        return carry

    for i in range(chunks):
        backward_chunk(i, 0)

    halfway = blocks // 2
    pt[chunks * 64 :, :] = jnp.zeros((64, LANES), F32)
    sums = []
    for c in range(3):
        rows = jnp.concatenate(
            [
                jnp.sum(g3[c, b * per_block : (b + 1) * per_block, :], axis=0, keepdims=True)
                for b in range(blocks)
            ],
            axis=0,
        )
        rows = -(rows + pltpu.roll(rows, LANES // 2, 1))
        sums.append(jnp.where(lane1 < LANES // 2, rows[0:halfway], rows[halfway:]))
    for b in range(halfway):
        at = (n_rows + b) * 8

        def store(which, value):
            pt[at + which : at + which + 1, :] = value[b : b + 1]

        put_parts(store, sums)
        spread = (lane8 & (GROUP - 1)) + jnp.where(lane8 < LANES // 2, b, b + halfway) * GROUP
        dest = pick(whole(0, 4), spread)[0:1].astype(I32)
        pt[at + 6 : at + 7, :] = (dest >> 7).astype(F32)
        pt[at + 7 : at + 8, :] = (dest & (LANES - 1)).astype(F32)

    n_targets = len(TARGETS)
    tall = 96
    sub16 = lax.broadcasted_iota(I32, (16, LANES), 0)
    pair = jnp.where(sub16 >= 8, 1.0, 0.0)
    pairs = [(pair + 2.0 * b).astype(BF16) for b in range((n_targets + 1) // 2)]
    steps = [(sub16 + 16 * b).astype(F32).astype(BF16) for b in range(tall // 16)]
    zero16 = jnp.zeros((16, LANES), BF16)
    one16 = jnp.ones((16, LANES), BF16)

    spread_out = None
    rows_left = n_rows + halfway + (n_rows + halfway) % 2
    for first_row in range(0, rows_left, 8):
        lefts, rights = [], []
        for row in range(first_row, min(first_row + 8, rows_left)):
            v = pt[row * 8 : row * 8 + 8, :]
            where_to = jnp.broadcast_to(v[6:7], (16, LANES)).astype(BF16)
            lo = jnp.broadcast_to(v[7:8], (16, LANES)).astype(BF16)
            twice = jnp.concatenate([v, v], axis=0).astype(BF16)
            lefts.append(jnp.concatenate([jnp.where(where_to == p, twice, zero16) for p in pairs], axis=0))
            rights.append(jnp.concatenate([jnp.where(lo == p, one16, zero16) for p in steps], axis=0))
        part = nt_dot(jnp.concatenate(lefts, axis=1), jnp.concatenate(rights, axis=1))
        spread_out = part if spread_out is None else spread_out + part
    for t in range(n_targets):
        ret_out[t] = jnp.zeros((8, LANES), F32)
        ret_out[t, :, 0:tall] = spread_out[t * 8 : t * 8 + 8, :]

    sends = []
    for dx, dy in FAR:
        there = target_slot(-dx, -dy)
        copy = pltpu.make_async_remote_copy(
            src_ref=ret_out.at[target_slot(dx, dy)],
            dst_ref=ret_in.at[there],
            send_sem=ret_send.at[there],
            recv_sem=ret_recv.at[there],
            device_id=device(dx, dy),
            device_id_type=MESH,
        )
        copy.start()
        sends.append(copy)

    settle = jnp.broadcast_to(source, (8, LANES))
    mine, low, high = load[1], load[0], load[2]
    held = jnp.where(lane8 < atoms, mine, jnp.where(lane8 < atoms + 5, low, high))
    held = jnp.where(lane8 < LANES - 1, held, 0.0)
    held = pick(held, settle)
    total = ret_out[target_slot(0, 0)]
    for copy, (dx, dy) in zip(sends, FAR):
        copy.wait()
    for dx, dy in FAR:
        total = total + ret_in[target_slot(dx, dy)]
    force = pick(total, settle)
    force = force[0:3] + force[3:6]
    fresh = held[0:3] + 0.5 * TIME_STEP * force * held[6:7]
    for c in range(3):
        both_ref[0, c] = fresh[c : c + 1, 0:atoms]
        both_ref[0, c + 3] = held[c + 3 : c + 4, 0:atoms]


def on_device(*args):
    atoms = args[0].shape[3]
    slots = args[4].shape[2]
    ch = args[13].shape[0]
    chunks = (atoms // GROUP * (slots // 16) + 7) // 8
    n_gx, n_yz = lax.axis_size("gx"), lax.axis_size("yz")
    period = (n_gx * PX * SPACING, n_yz * PY * SPACING, PZ * SPACING)
    pos, vel, frc, spc, nbr, msk, sx, sy, ms, mr, wb, ec, en, we, wl, wo = args
    pos, vel, frc = (x.transpose(0, 2, 1, 3) for x in (pos, vel, frc))
    nbr, msk = (x.transpose(0, 1, 3, 2) for x in (nbr, msk))
    args = (pos, vel, frc, spc, nbr, msk, sx, sy, ms, mr, wb, ec.T, en.T, we, wl.T, wo.reshape(1, ch))

    def body(*refs):
        kernel_body(period, atoms, slots, *refs)

    vmem = pl.BlockSpec(memory_space=pltpu.VMEM)
    per_block = slots // 16
    blocks = atoms // GROUP
    dma = pltpu.SemaphoreType.DMA
    out = jax.ShapeDtypeStruct((1, 6, 1, atoms), F32)
    staged = tuple(
        (pltpu.SMEM if at in (8, 9) else pltpu.VMEM)(x.shape, x.dtype) for at, x in enumerate(args)
    )
    both = pl.pallas_call(
        body,
        out_shape=out,
        in_specs=[pl.BlockSpec(memory_space=pl.ANY)] * 16,
        out_specs=vmem,
        scratch_shapes=[
            staged,
            pltpu.VMEM((9, 8, LANES), F32),
            pltpu.VMEM((3, 8, LANES), F32),
            pltpu.VMEM((15, 8, LANES), F32),
            pltpu.VMEM((15, 8, LANES), F32),
            pltpu.VMEM((atoms, LANES), F32),
            pltpu.VMEM((chunks * 8, LANES), F32),
            pltpu.VMEM((4, 8, LANES), F32),
            pltpu.VMEM((13, chunks, 8, LANES), F32),
            pltpu.VMEM((chunks * 128, LANES), F32),
            pltpu.VMEM((chunks * 128, LANES), F32),
            pltpu.VMEM((chunks * 192, LANES), F32),
            pltpu.VMEM((chunks * 64 + 64, LANES), F32),
            pltpu.VMEM((atoms // GROUP, ch, LANES), F32),
            pltpu.VMEM((2, 3, 3 * ch, ch), BF16),
            pltpu.VMEM((ch, 16), BF16),
            pltpu.VMEM((ch, LANES), F32),
            pltpu.VMEM((2, ch, LANES), F32),
            pltpu.VMEM((blocks, 10 * GROUP + 2 * ch, per_block * LANES), BF16),
            pltpu.VMEM((blocks * per_block, ch, LANES), F32),
            pltpu.VMEM((blocks * per_block, ch, LANES), F32),
            pltpu.VMEM((blocks * per_block, ch, LANES), F32),
            pltpu.VMEM((blocks, 2 * ch + 8 * GROUP, per_block * LANES), BF16),
            pltpu.VMEM((3, 64, LANES), F32),
            dma((16,)),
            dma((9,)),
            dma((9,)),
            dma((3,)),
            dma((3,)),
            dma((15,)),
            dma((15,)),
        ],
        compiler_params=pltpu.CompilerParams(
            collective_id=0, has_side_effects=True, vmem_limit_bytes=60 * 1024 * 1024
        ),
    )(*args)
    return both[:, 0:3].transpose(0, 2, 1, 3), both[:, 3:6].transpose(0, 2, 1, 3)


def solution(mesh):
    block4 = P("gx", "yz", None, None)
    block3 = P("gx", "yz", None)
    return jax.shard_map(
        on_device,
        mesh=mesh,
        in_specs=(block4, block4, block4, block3) + (block4,) * 6 + (P(),) * 6,
        out_specs=(block4, block4),
        check_vma=False,
    )
```

```python
import jax
import jax.numpy as jnp
from jax import lax
from jax.experimental import pallas as pl
from jax.experimental.pallas import tpu as pltpu
from jax.sharding import PartitionSpec as P

PX = 4
PY = 4
PZ = 5
STEPS = 1
SPACING = 2.15
CUTOFF = 6.0
TIME_STEP = 0.05
ENV_SCALE = 0.125
MASSES = (1.008, 12.011, 14.007, 15.999, 32.06)
HIGHEST = lax.Precision.HIGHEST
MESH = pl.DeviceIdType.MESH
F32 = jnp.float32
BF16 = jnp.bfloat16
I32 = jnp.int32

LANES = 128
GROUP = 8
PI = 3.141592653589793
R3 = 3.0**0.5
R5 = 5.0**0.5
R15 = 15.0**0.5

HALO = [(dx, dy) for dy in (-1, 0, 1) for dx in (-1, 0, 1)]
NEAR = sorted((pos for pos in HALO if pos != (0, 0)), key=lambda pos: -abs(pos[0]) - 2 * abs(pos[1]))
TARGETS = [(dx, dy) for dy in (-1, 0, 1) for dx in (-2, -1, 0, 1, 2)]
FAR = sorted((pos for pos in TARGETS if pos != (0, 0)), key=lambda pos: -(abs(pos[0]) % 2) - 2 * abs(pos[1]))


def halo_slot(dx, dy):
    return (dy + 1) * 3 + dx + 1


def target_slot(dx, dy):
    return (dy + 1) * 5 + dx + 2


def nt_dot(a, b, precision=None):
    return lax.dot_general(
        a, b, (((1,), (1,)), ((), ())), precision=precision, preferred_element_type=F32
    )


def nn_dot(a, b, precision=None):
    return jnp.dot(a, b, precision=precision, preferred_element_type=F32)


def halves(x):
    high = x.astype(BF16)
    low = (x - high.astype(F32)).astype(BF16)
    return high, low


def pick(rows, index):
    return jnp.take_along_axis(rows, index, axis=1, mode="promise_in_bounds")


def turn(eye, x):
    high, low = halves(x)
    return nt_dot(eye, high) + nt_dot(eye, low)


def split_dot(left, right):
    high, low = halves(left)
    return nn_dot(high, right) + nn_dot(low, right)


def sigmoid(x):
    return 0.5 * jnp.tanh(0.5 * x) + 0.5


def kernel_body(
    period,
    atoms,
    slots,
    *refs,
):
    raw, refs = refs[:16], refs[16:]
    (
        both_ref,
        staged,
        halo,
        load,
        ret_out,
        ret_in,
        nb_pad,
        rows_code,
        table,
        sc,
        zf,
        zy,
        zd,
        pt,
        cterm,
        mats,
        w1s,
        wcol,
        w0pad,
        rhs,
        s1_s,
        ds_s,
        hid_s,
        dpt_s,
        g3,
        load_sems,
        halo_send,
        halo_recv,
        load_send,
        load_recv,
        ret_send,
        ret_recv,
    ) = refs
    gx = lax.axis_index("gx")
    yz = lax.axis_index("yz")
    n_gx = lax.axis_size("gx")
    n_yz = lax.axis_size("yz")
    blocks = atoms // GROUP
    per_block = slots // 16
    n_rows = blocks * per_block
    chunks = (n_rows + 7) // 8

    def device(dx, dy):
        return (lax.rem(gx + dx + n_gx, n_gx), lax.rem(yz + dy + n_yz, n_yz))

    barrier = pltpu.get_barrier_semaphore()
    loads = []
    first = (0, 1, 2, 3, 6, 7, 8, 9)
    for at, (far, close) in enumerate(zip(raw, staged)):
        loads.append(pltpu.make_async_copy(far, close, load_sems.at[at]))
    for dx, dy in FAR:
        pl.semaphore_signal(barrier, inc=1, device_id=device(dx, dy), device_id_type=MESH)

    for at in first:
        loads[at].start()
    for at in range(16):
        if at not in first:
            loads[at].start()
    (
        pos_ref,
        vel_ref,
        frc_ref,
        spc_ref,
        nbr_ref,
        msk_ref,
        sx_ref,
        sy_ref,
        ms_ref,
        mr_ref,
        wb_ref,
        ec_ref,
        en_ref,
        we_ref,
        wl_ref,
        wo_ref,
    ) = staged
    for at in first:
        loads[at].wait()

    lane1 = lax.broadcasted_iota(I32, (1, LANES), 1)
    lane8 = lax.broadcasted_iota(I32, (8, LANES), 1)
    sub8 = lax.broadcasted_iota(I32, (8, LANES), 0)

    own = halo_slot(0, 0)
    kinds = spc_ref[0].astype(F32)
    minv = jnp.zeros_like(kinds)
    for kind, mass in enumerate(MASSES):
        minv = jnp.where(kinds == float(kind), 1.0 / jnp.float32(mass), minv)
    halo[own] = jnp.zeros((8, LANES), F32)
    load[1] = jnp.zeros((8, LANES), F32)
    for c in range(3):
        start = pos_ref[0, c]
        velocity = vel_ref[0, c] + 0.5 * TIME_STEP * frc_ref[0, c] * minv
        coords = start + TIME_STEP * velocity
        halo[own, c : c + 1, 0:atoms] = coords
        load[1, c : c + 1, 0:atoms] = velocity
        load[1, c + 3 : c + 4, 0:atoms] = (coords - start) / (STEPS * TIME_STEP)
    halo[own, 3:4, 0:atoms] = kinds
    code = lane1
    place = lane1
    source = lane1
    for side in (0, 1):
        for k in range(ms_ref.shape[3]):
            seat = atoms + 5 * (1 - side) + k
            code = jnp.where(lane1 == mr_ref[0, 0, side, k], LANES - 1, code)
    for side in (0, 1):
        for k in range(ms_ref.shape[3]):
            seat = atoms + 5 * (1 - side) + k
            gone = ms_ref[0, 0, side, k]
            code = jnp.where(lane1 == gone, (2 * side - 1) * LANES + seat, code)
            place = jnp.where(lane1 == seat, gone, place)
            source = jnp.where(lane1 == gone, LANES - 1, source)
    for side in (0, 1):
        for k in range(ms_ref.shape[3]):
            source = jnp.where(lane1 == mr_ref[0, 0, side, k], atoms + 5 * side + k, source)
    code = jnp.where(lane1 < atoms, code + LANES, 0)
    halo[own, 4:5, :] = code.astype(F32)
    halo[own, 6:8, 0:atoms] = sy_ref[0, 0].astype(F32)
    load[1, 6:7, 0:atoms] = minv
    width_x = sx_ref.shape[3]
    g3[0] = jnp.zeros((64, LANES), F32)
    g3[0, 0:2, 0:width_x] = sx_ref[0, 0].astype(F32)
    lists = g3[0, 0:8, :]
    halo[own, 5:6, :] = lists[1:2] + pltpu.roll(lists, width_x, 1)[0:1]
    load[1] = pick(load[1], jnp.broadcast_to(place, (8, LANES)))

    pl.semaphore_wait(barrier, len(FAR))
    sends, carried = [], []
    for dx, dy in NEAR:
        there = halo_slot(-dx, -dy)
        copy = pltpu.make_async_remote_copy(
            src_ref=halo.at[own],
            dst_ref=halo.at[there],
            send_sem=halo_send.at[there],
            recv_sem=halo_recv.at[there],
            device_id=device(dx, dy),
            device_id_type=MESH,
        )
        copy.start()
        sends.append(copy)
    for dx in (-1, 1):
        there = 1 - dx
        copy = pltpu.make_async_remote_copy(
            src_ref=load.at[1],
            dst_ref=load.at[there],
            send_sem=load_send.at[there],
            recv_sem=load_recv.at[there],
            device_id=device(dx, 0),
            device_id_type=MESH,
        )
        copy.start()
        carried.append(copy)

    for at in range(16):
        if at not in first:
            loads[at].wait()
    nb_pad[...] = jnp.zeros((atoms, LANES), F32)
    nb_pad[:, 0:slots] = nbr_ref[0, 0].astype(F32) + 512.0 * msk_ref[0, 0].astype(F32)
    rows_code[...] = jnp.zeros((chunks * 8, LANES), F32)
    in_row = (lane8 & (GROUP - 1)) == sub8
    for block in range(blocks):
        group = nb_pad[block * GROUP : (block + 1) * GROUP, :]
        for jb in range(per_block):
            moved = pick(group, (lane8 >> 3) + jb * 16)
            row = jnp.sum(jnp.where(in_row, moved, 0.0), axis=0, keepdims=True)
            r = block * per_block + jb
            rows_code[r : r + 1, :] = row

    ch = we_ref.shape[0]
    eye = (
        lax.broadcasted_iota(I32, (ch, ch), 0) == lax.broadcasted_iota(I32, (ch, ch), 1)
    ).astype(F32)
    n_basis = wb_ref.shape[0]
    n_kinds = en_ref.shape[0]
    wl_t = wl_ref[...]
    mixes = []
    eye16 = eye.astype(BF16)
    we_h, we_l = halves(we_ref[...])
    for part in range(3):
        part_t = wl_t[:, (part + 1) * ch : (part + 2) * ch]
        part_h, part_l = halves(part_t)
        mixes.append(ENV_SCALE * (nt_dot(part_h, we_h) + nt_dot(part_l, we_h) + nt_dot(part_h, we_l)))
    for part in range(3):
        turned = mixes[part]
        straight = turn(eye16, turned)
        for which, m in enumerate((straight, turned)):
            m_high, m_low = halves(m)
            mats[which, part] = jnp.concatenate([m_high, m_high, m_low], axis=0)
    w0_t = wl_t[:, 0:ch]
    w0 = turn(eye16, w0_t)
    ec = turn(eye16, ec_ref[...])
    w0pad[...] = jnp.zeros((2, ch, LANES), F32)
    w0pad[0, :, 80 : 80 + ch] = w0_t
    w0pad[1, :, 80 : 80 + ch] = w0
    w1f = jnp.concatenate(
        [
            nt_dot(eye16, wb_ref[...].astype(BF16)),
            nt_dot(eye16, en_ref[...].astype(BF16)),
            jnp.zeros((ch, 16 - n_basis - n_kinds), F32),
        ],
        axis=1,
    )
    w1s[...] = w1f.astype(BF16)
    row32 = lax.broadcasted_iota(I32, (32, LANES), 0)
    lane32 = lax.broadcasted_iota(I32, (32, LANES), 1)
    g3[1, 0:32, :] = jnp.zeros((32, LANES), F32)
    g3[1, 0:n_basis, 0:ch] = wb_ref[...]
    head = g3[1, 0:32, :] + jnp.where(
        (row32 == 8) & (lane32 >= ch) & (lane32 < 2 * ch), 1.0, 0.0
    ) + jnp.where((lane32 >= 2 * ch) & (row32 == 16 + ((lane32 - 2 * ch) >> 3)), 1.0, 0.0)
    w_last = head
    wcol[...] = jnp.broadcast_to(
        jnp.sum(jnp.where(eye > 0, wo_ref[...], 0.0), axis=1, keepdims=True), (ch, LANES)
    )

    kind_rows = jnp.broadcast_to(halo[own, 3:4, :], (8, LANES))
    for block in range(blocks):
        spread = (lane8 & (GROUP - 1)) + block * GROUP
        kind_row = jnp.broadcast_to(pick(kind_rows, spread)[0:1], (ch, LANES))
        term = jnp.zeros((ch, LANES), F32)
        for kind in range(n_kinds):
            term = jnp.where(
                kind_row == float(kind),
                jnp.broadcast_to(ec[:, kind : kind + 1], (ch, LANES)),
                term,
            )
        cterm[block] = term

    for copy in sends:
        copy.wait_recv()

    def shifted(dx, dy):
        step = float(LANES * ((dy + 1) * 5 + dx + 1))
        return halo[halo_slot(dx, dy)] + jnp.where(sub8 == 4, step, 0.0)

    def row_index(rows, which):
        return jnp.broadcast_to(rows[which : which + 1, :], (8, LANES)).astype(I32)

    def x_ghosts(dy):
        low, high = shifted(-1, dy), shifted(1, dy)
        return jnp.where(
            lane8 < width_x,
            pick(low, row_index(low, 5)),
            pick(high, row_index(high, 5)),
        )

    def y_ghosts(dy):
        base = shifted(0, dy)
        index = row_index(base, 7 if dy < 0 else 6)
        outer = index >= atoms
        return jnp.where(
            outer,
            pick(x_ghosts(dy), jnp.where(outer, index - atoms, 0)),
            pick(base, jnp.where(outer, 0, index)),
        )

    table[0] = shifted(0, 0)
    table[1] = x_ghosts(0)
    table[2] = y_ghosts(-1)
    table[3] = y_ghosts(1)

    def whole(k, c):
        return jnp.broadcast_to(table[k, c : c + 1, :], (8, LANES))

    def forward_chunk(i, carry):
        word = rows_code[pl.ds(i * 8, 8), :]
        live = word >= 512.0
        n = jnp.where(live, word - 512.0, word).astype(I32)
        k = jnp.where(n >= atoms, 1, 0) + jnp.where(n >= 2 * atoms, 1, 0) + jnp.where(n >= 3 * atoms, 1, 0)
        n = n - atoms * k
        near = []
        for c in range(5):
            v = pick(whole(0, c), n)
            for part in (1, 2, 3):
                v = jnp.where(k == part, pick(whole(part, c), n), v)
            near.append(v)
        row = i * 8 + sub8
        block = jnp.zeros((8, LANES), I32)
        for b in range(1, blocks):
            block = block + jnp.where(row >= b * per_block, 1, 0)
        centre = block * GROUP + (lane8 & (GROUP - 1))
        off = []
        for c in range(3):
            d = near[c] - pick(whole(0, c), centre)
            d = d - period[c] * jnp.floor(d / period[c] + 0.5)
            off.append(jnp.where(live, d, SPACING if c == 0 else 0.0))
        radius = jnp.sqrt(off[0] * off[0] + off[1] * off[1] + off[2] * off[2])
        rinv = 1.0 / radius
        ux, uy, uz = (o * rinv for o in off)
        q = radius / CUTOFF
        valid = jnp.logical_and(live, q < 1.0)
        q2 = q * q
        q5 = q2 * q2 * q
        q6 = q5 * q
        env = jnp.where(valid, 1.0 + q6 * (-28.0 + q * (48.0 - 21.0 * q)), 0.0)
        denv = jnp.where(valid, (168.0 / CUTOFF) * q5 * (-1.0 + q * (2.0 - q)), 0.0)
        u = PI * jnp.minimum(q, 1.0) - 0.5 * PI
        w = u * u
        sin1 = 1.0 + w * (-1 / 2 + w * (1 / 24 + w * (-1 / 720 + w * (1 / 40320 + w * (-1 / 3628800 + w * (1 / 479001600))))))
        cos1 = -u * (1.0 + w * (-1 / 6 + w * (1 / 120 + w * (-1 / 5040 + w * (1 / 362880 + w * (-1 / 39916800 + w * (1 / 6227020800)))))))
        sc[0, i] = ux
        sc[1, i] = uy
        sc[2, i] = uz
        sc[3, i] = rinv
        sc[4, i] = denv
        zbase = i * 128
        scale = (2.0 / CUTOFF) ** 0.5 * rinv
        s_prev, s_now = jnp.zeros_like(sin1), sin1
        c_prev, c_now = jnp.ones_like(cos1), cos1
        for order in range(1, n_basis + 1):
            bes = scale * s_now
            zf[pl.ds(zbase + order - 1, 8, stride=16), :] = bes
            sc[4 + order, i] = scale * (order * PI / CUTOFF) * c_now - bes * rinv
            s_prev, s_now = s_now, 2.0 * cos1 * s_now - s_prev
            c_prev, c_now = c_now, 2.0 * cos1 * c_now - c_prev
        for kind in range(n_kinds):
            zf[pl.ds(zbase + n_basis + kind, 8, stride=16), :] = jnp.where(near[3] == float(kind), 1.0, 0.0)
        for extra in range(n_basis + n_kinds, 16):
            zf[pl.ds(zbase + extra, 8, stride=16), :] = jnp.zeros((8, LANES), F32)
        ys = (
            R3 * ux,
            R3 * uy,
            R3 * uz,
            R15 * ux * uy,
            R15 * uy * uz,
            0.5 * R5 * (3.0 * uz * uz - 1.0),
            R15 * ux * uz,
            0.5 * R15 * (ux * ux - uy * uy),
        )
        for m, y in enumerate(ys):
            zy[pl.ds(zbase + m, 8, stride=16), :] = y
        zy[pl.ds(zbase + 8, 8, stride=16), :] = env
        dest = near[4].astype(I32)
        tbase = i * 64
        pt[pl.ds(tbase + 6, 8, stride=8), :] = (dest >> 7).astype(F32)
        pt[pl.ds(tbase + 7, 8, stride=8), :] = (dest & (LANES - 1)).astype(F32)
        return carry

    for i in range(chunks):
        forward_chunk(i, 0)

    n_harm = 8
    wide = n_harm * GROUP
    own_lane = (lane8 & (GROUP - 1)) == sub8
    every = jnp.concatenate([jnp.where(own_lane, 1.0, 0.0)] * n_harm, axis=0).astype(BF16)
    ones_row = jnp.concatenate([jnp.where(own_lane, 1.0, 0.0), jnp.zeros((8, LANES), F32)], axis=0).astype(BF16)
    at_ef = wide + 2 * GROUP
    at_dlp = at_ef + ch

    degree_rows = ((1, 0, 3 * GROUP), (2, 3 * GROUP, wide), (0, wide, wide + 2 * GROUP))

    def by_degree(which, sums):
        parts = []
        for degree, a, b in degree_rows:
            grown = exact_dot(jnp.concatenate([x[a:b] for x in sums], axis=0), which, degree)
            parts.append([grown[t * (b - a) : (t + 1) * (b - a)] for t in range(len(sums))])
        return [jnp.concatenate([p[t] for p in parts], axis=0) for t in range(len(sums))]

    def exact_dot(rows, which, degree):
        high = rows.astype(BF16).astype(F32)
        joined = jnp.concatenate([high, rows - high, high], axis=1).astype(BF16)
        return nn_dot(joined, mats[which, degree])

    def as_left(turned, pad):
        tall_one = jnp.concatenate([turned, jnp.zeros((LANES - at_ef, ch), F32)], axis=0)
        return (tall_one.T + pad)[:, 0:at_dlp]

    w_out = wcol[...]
    kept = {}

    def env_row(row):
        return zy[row * 16 + 8 : row * 16 + 9, :]

    def stage_pre(b):
        base = b * per_block
        feats = jnp.concatenate(
            [zf[(base + jb) * 16 : (base + jb + 1) * 16, :] for jb in range(per_block)], axis=1
        )
        kept["pre", b] = nn_dot(w1s[...], feats.astype(BF16))

    def stage_feat(b):
        centre_term = cterm[b]
        pre = kept.pop(("pre", b))
        for jb in range(per_block):
            row = b * per_block + jb
            cols = slice(jb * LANES, (jb + 1) * LANES)
            z = zy[row * 16 : row * 16 + 16, :]
            env = z[8:9]
            p = pre[:, cols] + centre_term
            sig = sigmoid(p)
            s1 = p * sig
            s1_s[row] = s1
            ds_s[row] = (sig + s1 * (1.0 - sig)) * env
            rhs[b, at_ef : at_ef + ch, cols] = (s1 * env).astype(BF16)
            for m in range(0, n_harm, 2):
                two = [jnp.where(own_lane, z[t : t + 1], 0.0) for t in (m, m + 1)]
                rhs[b, m * GROUP : (m + 2) * GROUP, cols] = jnp.concatenate(two, axis=0).astype(BF16)
            rhs[b, wide : wide + 2 * GROUP, cols] = ones_row

    def stage_env(b):
        kept["f", b] = nt_dot(rhs[b, 0:at_ef, :], rhs[b, at_ef : at_ef + ch, :])

    def stage_grow(b):
        half = blocks // 2
        if b % half == 0:
            grown = by_degree(0, [kept.pop(("f", t)) for t in range(b, b + half)])
            for t in range(half):
                kept["g", b + t] = grown[t]

    def stage_lp(b):
        left = as_left(kept["g", b], w0pad[0])
        kept["lp", b] = split_dot(left, rhs[b, 0:at_dlp, :])

    def stage_latent(b):
        lp_all = kept.pop(("lp", b))
        for jb in range(per_block):
            row = b * per_block + jb
            cols = slice(jb * LANES, (jb + 1) * LANES)
            env = env_row(row)
            lp = lp_all[:, cols]
            sig = sigmoid(lp)
            lat = lp * sig
            hid_s[row] = w_out * (s1_s[row] * env + lat)
            dlp = (w_out * env) * (sig + lat * (1.0 - sig))
            rhs[b, at_dlp : at_dlp + ch, cols] = dlp.astype(BF16)

    def stage_back(b):
        kept["f", b] = nt_dot(rhs[b, 0:at_ef, :], rhs[b, at_dlp : at_dlp + ch, :])

    def stage_shrink(b):
        half = blocks // 2
        if b % half == 0:
            grown = by_degree(1, [kept.pop(("f", t)) for t in range(b, b + half)])
            for t in range(half):
                kept["d", b + t] = grown[t]

    def stage_de(b):
        grown = kept.pop(("d", b))
        left = as_left(grown, w0pad[1])
        kept["de", b] = split_dot(left, jnp.concatenate([rhs[b, 0:at_ef, :], rhs[b, at_dlp : at_dlp + ch, :]], axis=0))
        both = jnp.concatenate([grown[0:wide], kept.pop(("g", b))[0:wide]], axis=1)
        kept["dy", b] = nn_dot(both.astype(BF16), rhs[b, at_ef : at_dlp + ch, :])

    def stage_edge(b):
        de_all = kept.pop(("de", b))
        dy_all = kept.pop(("dy", b))
        for jb in range(per_block):
            row = b * per_block + jb
            cols = slice(jb * LANES, (jb + 1) * LANES)
            de = de_all[:, cols] + w_out * env_row(row)
            dpt_s[b, 0:ch, cols] = (de * ds_s[row]).astype(BF16)
            dpt_s[b, ch : 2 * ch, cols] = (hid_s[row] + de * s1_s[row]).astype(BF16)
            dpt_s[b, 2 * ch :, cols] = dy_all[:, cols].astype(BF16) * every

    def stage_fold(b):
        got = split_dot(w_last, dpt_s[b])
        for jb in range(per_block):
            row = b * per_block + jb
            zd[row * 24 : row * 24 + 24, :] = got[0:24, jb * LANES : (jb + 1) * LANES]

    stages = (
        stage_pre,
        stage_feat,
        stage_env,
        stage_grow,
        stage_lp,
        stage_latent,
        stage_back,
        stage_shrink,
        stage_de,
        stage_edge,
        stage_fold,
    )
    teams = (range(0, blocks // 2), range(blocks // 2, blocks))
    for tick in range(len(stages) + 3):
        for late, team in enumerate(teams):
            if 0 <= tick - 3 * late < len(stages):
                for b in team:
                    stages[tick - 3 * late](b)
    for row in range(n_rows, chunks * 8):
        zd[row * 24 : row * 24 + 24, :] = jnp.zeros((24, LANES), F32)

    def put_parts(store, values):
        for c in range(3):
            high = values[c].astype(BF16).astype(F32)
            store(c, high)
            store(c + 3, values[c] - high)

    def backward_chunk(i, carry):
        zbase = i * 192

        def d(which):
            return zd[pl.ds(zbase + which, 8, stride=24), :]

        ux, uy, uz, rinv, denv = (sc[t, i] for t in range(5))
        dr = d(8) * denv
        for order in range(n_basis):
            dr = dr + d(order) * sc[5 + order, i]
        d1, d2, d3, d4, d5, d6, d7, d8 = (d(16 + m) for m in range(8))
        dux = R3 * d1 + R15 * (uy * d4 + uz * d7 + ux * d8)
        duy = R3 * d2 + R15 * (ux * d4 + uz * d5 - uy * d8)
        duz = R3 * d3 + R15 * (uy * d5 + ux * d7) + (3.0 * R5) * uz * d6
        radial = dr - rinv * (dux * ux + duy * uy + duz * uz)
        forces = [-(radial * u + rinv * du) for u, du in ((ux, dux), (uy, duy), (uz, duz))]
        at = pl.ds(i * 8, 8)
        for c in range(3):
            g3[c, at, :] = forces[c]

        def store(which, value):
            pt[pl.ds(i * 64 + which, 8, stride=8), :] = value

        put_parts(store, forces)
        return carry

    for i in range(chunks):
        backward_chunk(i, 0)

    halfway = blocks // 2
    pt[chunks * 64 :, :] = jnp.zeros((64, LANES), F32)
    sums = []
    for c in range(3):
        rows = jnp.concatenate(
            [
                jnp.sum(g3[c, b * per_block : (b + 1) * per_block, :], axis=0, keepdims=True)
                for b in range(blocks)
            ],
            axis=0,
        )
        rows = -(rows + pltpu.roll(rows, LANES // 2, 1))
        sums.append(jnp.where(lane1 < LANES // 2, rows[0:halfway], rows[halfway:]))
    for b in range(halfway):
        at = (n_rows + b) * 8

        def store(which, value):
            pt[at + which : at + which + 1, :] = value[b : b + 1]

        put_parts(store, sums)
        spread = (lane8 & (GROUP - 1)) + jnp.where(lane8 < LANES // 2, b, b + halfway) * GROUP
        dest = pick(whole(0, 4), spread)[0:1].astype(I32)
        pt[at + 6 : at + 7, :] = (dest >> 7).astype(F32)
        pt[at + 7 : at + 8, :] = (dest & (LANES - 1)).astype(F32)

    n_targets = len(TARGETS)
    tall = 96
    sub16 = lax.broadcasted_iota(I32, (16, LANES), 0)
    pair = jnp.where(sub16 >= 8, 1.0, 0.0)
    pairs = [(pair + 2.0 * b).astype(BF16) for b in range((n_targets + 1) // 2)]
    steps = [(sub16 + 16 * b).astype(F32).astype(BF16) for b in range(tall // 16)]
    zero16 = jnp.zeros((16, LANES), BF16)
    one16 = jnp.ones((16, LANES), BF16)

    spread_out = None
    rows_left = n_rows + halfway + (n_rows + halfway) % 2
    for first_row in range(0, rows_left, 8):
        lefts, rights = [], []
        for row in range(first_row, min(first_row + 8, rows_left)):
            v = pt[row * 8 : row * 8 + 8, :]
            where_to = jnp.broadcast_to(v[6:7], (16, LANES)).astype(BF16)
            lo = jnp.broadcast_to(v[7:8], (16, LANES)).astype(BF16)
            twice = jnp.concatenate([v, v], axis=0).astype(BF16)
            lefts.append(jnp.concatenate([jnp.where(where_to == p, twice, zero16) for p in pairs], axis=0))
            rights.append(jnp.concatenate([jnp.where(lo == p, one16, zero16) for p in steps], axis=0))
        part = nt_dot(jnp.concatenate(lefts, axis=1), jnp.concatenate(rights, axis=1))
        spread_out = part if spread_out is None else spread_out + part
    for t in range(n_targets):
        ret_out[t] = jnp.zeros((8, LANES), F32)
        ret_out[t, :, 0:tall] = spread_out[t * 8 : t * 8 + 8, :]

    returns = []
    for dx, dy in FAR:
        there = target_slot(-dx, -dy)
        copy = pltpu.make_async_remote_copy(
            src_ref=ret_out.at[target_slot(dx, dy)],
            dst_ref=ret_in.at[there],
            send_sem=ret_send.at[there],
            recv_sem=ret_recv.at[there],
            device_id=device(dx, dy),
            device_id_type=MESH,
        )
        copy.start()
        returns.append(copy)

    for copy in carried:
        copy.wait_recv()
    settle = jnp.broadcast_to(source, (8, LANES))
    mine, low, high = load[1], load[0], load[2]
    held = jnp.where(lane8 < atoms, mine, jnp.where(lane8 < atoms + 5, low, high))
    held = jnp.where(lane8 < LANES - 1, held, 0.0)
    held = pick(held, settle)
    total = ret_out[target_slot(0, 0)]
    for copy in returns:
        copy.wait_recv()
    for dx, dy in FAR:
        total = total + ret_in[target_slot(dx, dy)]
    force = pick(total, settle)
    force = force[0:3] + force[3:6]
    fresh = held[0:3] + 0.5 * TIME_STEP * force * held[6:7]
    for c in range(3):
        both_ref[0, c] = fresh[c : c + 1, 0:atoms]
        both_ref[0, c + 3] = held[c + 3 : c + 4, 0:atoms]
    for copy in sends + carried + returns:
        copy.wait_send()


def on_device(*args):
    atoms = args[0].shape[3]
    slots = args[4].shape[2]
    ch = args[13].shape[0]
    chunks = (atoms // GROUP * (slots // 16) + 7) // 8
    n_gx, n_yz = lax.axis_size("gx"), lax.axis_size("yz")
    period = (n_gx * PX * SPACING, n_yz * PY * SPACING, PZ * SPACING)
    pos, vel, frc, spc, nbr, msk, sx, sy, ms, mr, wb, ec, en, we, wl, wo = args
    pos, vel, frc = (x.transpose(0, 2, 1, 3) for x in (pos, vel, frc))
    nbr, msk = (x.transpose(0, 1, 3, 2) for x in (nbr, msk))
    args = (pos, vel, frc, spc, nbr, msk, sx, sy, ms, mr, wb, ec.T, en.T, we, wl.T, wo.reshape(1, ch))

    def body(*refs):
        kernel_body(period, atoms, slots, *refs)

    vmem = pl.BlockSpec(memory_space=pltpu.VMEM)
    per_block = slots // 16
    blocks = atoms // GROUP
    dma = pltpu.SemaphoreType.DMA
    out = jax.ShapeDtypeStruct((1, 6, 1, atoms), F32)
    staged = tuple(
        (pltpu.SMEM if at in (8, 9) else pltpu.VMEM)(x.shape, x.dtype) for at, x in enumerate(args)
    )
    both = pl.pallas_call(
        body,
        out_shape=out,
        in_specs=[pl.BlockSpec(memory_space=pl.ANY)] * 16,
        out_specs=vmem,
        scratch_shapes=[
            staged,
            pltpu.VMEM((9, 8, LANES), F32),
            pltpu.VMEM((3, 8, LANES), F32),
            pltpu.VMEM((15, 8, LANES), F32),
            pltpu.VMEM((15, 8, LANES), F32),
            pltpu.VMEM((atoms, LANES), F32),
            pltpu.VMEM((chunks * 8, LANES), F32),
            pltpu.VMEM((4, 8, LANES), F32),
            pltpu.VMEM((13, chunks, 8, LANES), F32),
            pltpu.VMEM((chunks * 128, LANES), F32),
            pltpu.VMEM((chunks * 128, LANES), F32),
            pltpu.VMEM((chunks * 192, LANES), F32),
            pltpu.VMEM((chunks * 64 + 64, LANES), F32),
            pltpu.VMEM((atoms // GROUP, ch, LANES), F32),
            pltpu.VMEM((2, 3, 3 * ch, ch), BF16),
            pltpu.VMEM((ch, 16), BF16),
            pltpu.VMEM((ch, LANES), F32),
            pltpu.VMEM((2, ch, LANES), F32),
            pltpu.VMEM((blocks, 10 * GROUP + 2 * ch, per_block * LANES), BF16),
            pltpu.VMEM((blocks * per_block, ch, LANES), F32),
            pltpu.VMEM((blocks * per_block, ch, LANES), F32),
            pltpu.VMEM((blocks * per_block, ch, LANES), F32),
            pltpu.VMEM((blocks, 2 * ch + 8 * GROUP, per_block * LANES), BF16),
            pltpu.VMEM((3, 64, LANES), F32),
            dma((16,)),
            dma((9,)),
            dma((9,)),
            dma((3,)),
            dma((3,)),
            dma((15,)),
            dma((15,)),
        ],
        compiler_params=pltpu.CompilerParams(
            collective_id=0, has_side_effects=True, vmem_limit_bytes=60 * 1024 * 1024
        ),
    )(*args)
    return both[:, 0:3].transpose(0, 2, 1, 3), both[:, 3:6].transpose(0, 2, 1, 3)


def solution(mesh):
    block4 = P("gx", "yz", None, None)
    block3 = P("gx", "yz", None)
    return jax.shard_map(
        on_device,
        mesh=mesh,
        in_specs=(block4, block4, block4, block3) + (block4,) * 6 + (P(),) * 6,
        out_specs=(block4, block4),
        check_vma=False,
    )
```

```python
import jax
import jax.numpy as jnp
from jax import lax
from jax.experimental import pallas as pl
from jax.experimental.pallas import tpu as pltpu
from jax.sharding import PartitionSpec as P

PX = 4
PY = 4
PZ = 5
STEPS = 1
SPACING = 2.15
CUTOFF = 6.0
TIME_STEP = 0.05
ENV_SCALE = 0.125
MASSES = (1.008, 12.011, 14.007, 15.999, 32.06)
HIGHEST = lax.Precision.HIGHEST
MESH = pl.DeviceIdType.MESH
F32 = jnp.float32
BF16 = jnp.bfloat16
I32 = jnp.int32

LANES = 128
GROUP = 8
PI = 3.141592653589793
R3 = 3.0**0.5
R5 = 5.0**0.5
R15 = 15.0**0.5

HALO = [(dx, dy) for dy in (-1, 0, 1) for dx in (-1, 0, 1)]
NEAR = sorted((pos for pos in HALO if pos != (0, 0)), key=lambda pos: -abs(pos[0]) - 2 * abs(pos[1]))
TARGETS = [(dx, dy) for dy in (-1, 0, 1) for dx in (-2, -1, 0, 1, 2)]
REST = sorted((pos for pos in TARGETS if pos != (0, 0)), key=lambda pos: -(abs(pos[0]) % 2) - 2 * abs(pos[1]))


FAR = [pos for pos in REST if abs(pos[0]) == 2]
NIGH = [pos for pos in REST if abs(pos[0]) < 2]
DROPPED = 127
EMPTY = 95


def far_slot(dx, dy):
    return (dy + 1) * 2 + (dx + 2) // 4


def halo_slot(dx, dy):
    return (dy + 1) * 3 + dx + 1


def target_slot(dx, dy):
    return (dy + 1) * 5 + dx + 2


def nt_dot(a, b, precision=None):
    return lax.dot_general(
        a, b, (((1,), (1,)), ((), ())), precision=precision, preferred_element_type=F32
    )


def nn_dot(a, b, precision=None):
    return jnp.dot(a, b, precision=precision, preferred_element_type=F32)


def halves(x):
    high = x.astype(BF16)
    low = (x - high.astype(F32)).astype(BF16)
    return high, low


def pick(rows, index):
    return jnp.take_along_axis(rows, index, axis=1, mode="promise_in_bounds")


def turn(eye, x):
    high, low = halves(x)
    return nt_dot(eye, high) + nt_dot(eye, low)


def split_dot(left, right):
    high, low = halves(left)
    return nn_dot(high, right) + nn_dot(low, right)


def sigmoid(x):
    return 0.5 * jnp.tanh(0.5 * x) + 0.5


def kernel_body(
    period,
    atoms,
    slots,
    *refs,
):
    raw, refs = refs[:16], refs[16:]
    (
        both_ref,
        staged,
        halo,
        load,
        ret_out,
        ret_in,
        far_out,
        far_in,
        nb_pad,
        rows_code,
        table,
        sc,
        zf,
        zy,
        zd,
        pt,
        cterm,
        mats,
        w1s,
        wcol,
        w0pad,
        rhs,
        s1_s,
        ds_s,
        hid_s,
        dpt_s,
        g3,
        load_sems,
        halo_send,
        halo_recv,
        load_send,
        load_recv,
        ret_send,
        ret_recv,
        far_send,
        far_recv,
    ) = refs
    gx = lax.axis_index("gx")
    yz = lax.axis_index("yz")
    n_gx = lax.axis_size("gx")
    n_yz = lax.axis_size("yz")
    blocks = atoms // GROUP
    per_block = slots // 16
    n_rows = blocks * per_block
    chunks = (n_rows + 7) // 8

    def device(dx, dy):
        return (lax.rem(gx + dx + n_gx, n_gx), lax.rem(yz + dy + n_yz, n_yz))

    barrier = pltpu.get_barrier_semaphore()
    loads = []
    first = (0, 1, 2, 3, 6, 7, 8, 9)
    for at, (far, close) in enumerate(zip(raw, staged)):
        loads.append(pltpu.make_async_copy(far, close, load_sems.at[at]))
    for dx, dy in REST:
        pl.semaphore_signal(barrier, inc=1, device_id=device(dx, dy), device_id_type=MESH)

    for at in first:
        loads[at].start()
    for at in range(16):
        if at not in first:
            loads[at].start()
    (
        pos_ref,
        vel_ref,
        frc_ref,
        spc_ref,
        nbr_ref,
        msk_ref,
        sx_ref,
        sy_ref,
        ms_ref,
        mr_ref,
        wb_ref,
        ec_ref,
        en_ref,
        we_ref,
        wl_ref,
        wo_ref,
    ) = staged
    for at in first:
        loads[at].wait()

    lane1 = lax.broadcasted_iota(I32, (1, LANES), 1)
    lane8 = lax.broadcasted_iota(I32, (8, LANES), 1)
    sub8 = lax.broadcasted_iota(I32, (8, LANES), 0)

    own = halo_slot(0, 0)
    kinds = spc_ref[0].astype(F32)
    minv = jnp.zeros_like(kinds)
    for kind, mass in enumerate(MASSES):
        minv = jnp.where(kinds == float(kind), 1.0 / jnp.float32(mass), minv)
    halo[own] = jnp.zeros((8, LANES), F32)
    load[1] = jnp.zeros((8, LANES), F32)
    for c in range(3):
        start = pos_ref[0, c]
        velocity = vel_ref[0, c] + 0.5 * TIME_STEP * frc_ref[0, c] * minv
        coords = start + TIME_STEP * velocity
        halo[own, c : c + 1, 0:atoms] = coords
        load[1, c : c + 1, 0:atoms] = velocity
        load[1, c + 3 : c + 4, 0:atoms] = (coords - start) / (STEPS * TIME_STEP)
    halo[own, 3:4, 0:atoms] = kinds
    code = lane1
    place = lane1
    source = lane1
    for side in (0, 1):
        for k in range(ms_ref.shape[3]):
            seat = atoms + 5 * (1 - side) + k
            code = jnp.where(lane1 == mr_ref[0, 0, side, k], DROPPED, code)
    for side in (0, 1):
        for k in range(ms_ref.shape[3]):
            seat = atoms + 5 * (1 - side) + k
            gone = ms_ref[0, 0, side, k]
            code = jnp.where(lane1 == gone, (2 * side - 1) * LANES + seat, code)
            place = jnp.where(lane1 == seat, gone, place)
            source = jnp.where(lane1 == gone, EMPTY, source)
    for side in (0, 1):
        for k in range(ms_ref.shape[3]):
            source = jnp.where(lane1 == mr_ref[0, 0, side, k], atoms + 5 * side + k, source)
    code = jnp.where(lane1 < atoms, code + LANES, 0)
    halo[own, 4:5, :] = code.astype(F32)
    halo[own, 6:8, 0:atoms] = sy_ref[0, 0].astype(F32)
    load[1, 6:7, 0:atoms] = minv
    width_x = sx_ref.shape[3]
    g3[0] = jnp.zeros((64, LANES), F32)
    g3[0, 0:2, 0:width_x] = sx_ref[0, 0].astype(F32)
    lists = g3[0, 0:8, :]
    halo[own, 5:6, :] = lists[1:2] + pltpu.roll(lists, width_x, 1)[0:1]
    load[1] = pick(load[1], jnp.broadcast_to(place, (8, LANES)))

    pl.semaphore_wait(barrier, len(REST))
    sends, carried = [], []
    for dx, dy in NEAR:
        there = halo_slot(-dx, -dy)
        copy = pltpu.make_async_remote_copy(
            src_ref=halo.at[own],
            dst_ref=halo.at[there],
            send_sem=halo_send.at[there],
            recv_sem=halo_recv.at[there],
            device_id=device(dx, dy),
            device_id_type=MESH,
        )
        copy.start()
        sends.append(copy)
    for dx in (-1, 1):
        there = 1 - dx
        copy = pltpu.make_async_remote_copy(
            src_ref=load.at[1],
            dst_ref=load.at[there],
            send_sem=load_send.at[there],
            recv_sem=load_recv.at[there],
            device_id=device(dx, 0),
            device_id_type=MESH,
        )
        copy.start()
        carried.append(copy)

    for t in range(len(TARGETS)):
        ret_out[t] = jnp.zeros((4, LANES), F32)

    for at in range(16):
        if at not in first:
            loads[at].wait()
    nb_pad[...] = jnp.zeros((atoms, LANES), F32)
    nb_pad[:, 0:slots] = nbr_ref[0, 0].astype(F32) + 512.0 * msk_ref[0, 0].astype(F32)
    rows_code[...] = jnp.zeros((chunks * 8, LANES), F32)
    in_row = (lane8 & (GROUP - 1)) == sub8
    for block in range(blocks):
        group = nb_pad[block * GROUP : (block + 1) * GROUP, :]
        for jb in range(per_block):
            moved = pick(group, (lane8 >> 3) + jb * 16)
            row = jnp.sum(jnp.where(in_row, moved, 0.0), axis=0, keepdims=True)
            r = block * per_block + jb
            rows_code[r : r + 1, :] = row

    ch = we_ref.shape[0]
    eye = (
        lax.broadcasted_iota(I32, (ch, ch), 0) == lax.broadcasted_iota(I32, (ch, ch), 1)
    ).astype(F32)
    n_basis = wb_ref.shape[0]
    n_kinds = en_ref.shape[0]
    wl_t = wl_ref[...]
    mixes = []
    eye16 = eye.astype(BF16)
    we_h, we_l = halves(we_ref[...])
    for part in range(3):
        part_t = wl_t[:, (part + 1) * ch : (part + 2) * ch]
        part_h, part_l = halves(part_t)
        mixes.append(ENV_SCALE * (nt_dot(part_h, we_h) + nt_dot(part_l, we_h) + nt_dot(part_h, we_l)))
    for part in range(3):
        turned = mixes[part]
        straight = turn(eye16, turned)
        for which, m in enumerate((straight, turned)):
            m_high, m_low = halves(m)
            mats[which, part] = jnp.concatenate([m_high, m_high, m_low], axis=0)
    w0_t = wl_t[:, 0:ch]
    w0 = turn(eye16, w0_t)
    ec = turn(eye16, ec_ref[...])
    w0pad[...] = jnp.zeros((2, ch, LANES), F32)
    w0pad[0, :, 80 : 80 + ch] = w0_t
    w0pad[1, :, 80 : 80 + ch] = w0
    w1f = jnp.concatenate(
        [
            nt_dot(eye16, wb_ref[...].astype(BF16)),
            nt_dot(eye16, en_ref[...].astype(BF16)),
            jnp.zeros((ch, 16 - n_basis - n_kinds), F32),
        ],
        axis=1,
    )
    w1s[...] = w1f.astype(BF16)
    row32 = lax.broadcasted_iota(I32, (32, LANES), 0)
    lane32 = lax.broadcasted_iota(I32, (32, LANES), 1)
    g3[1, 0:32, :] = jnp.zeros((32, LANES), F32)
    g3[1, 0:n_basis, 0:ch] = wb_ref[...]
    head = g3[1, 0:32, :] + jnp.where(
        (row32 == 8) & (lane32 >= ch) & (lane32 < 2 * ch), 1.0, 0.0
    ) + jnp.where((lane32 >= 2 * ch) & (row32 == 16 + ((lane32 - 2 * ch) >> 3)), 1.0, 0.0)
    w_last = head
    wcol[...] = jnp.broadcast_to(
        jnp.sum(jnp.where(eye > 0, wo_ref[...], 0.0), axis=1, keepdims=True), (ch, LANES)
    )

    kind_rows = jnp.broadcast_to(halo[own, 3:4, :], (8, LANES))
    for block in range(blocks):
        spread = (lane8 & (GROUP - 1)) + block * GROUP
        kind_row = jnp.broadcast_to(pick(kind_rows, spread)[0:1], (ch, LANES))
        term = jnp.zeros((ch, LANES), F32)
        for kind in range(n_kinds):
            term = jnp.where(
                kind_row == float(kind),
                jnp.broadcast_to(ec[:, kind : kind + 1], (ch, LANES)),
                term,
            )
        cterm[block] = term

    for copy in sends:
        copy.wait_recv()

    def shifted(dx, dy):
        step = float(LANES * ((dy + 1) * 5 + dx + 1))
        return halo[halo_slot(dx, dy)] + jnp.where(sub8 == 4, step, 0.0)

    def row_index(rows, which):
        return jnp.broadcast_to(rows[which : which + 1, :], (8, LANES)).astype(I32)

    def x_ghosts(dy):
        low, high = shifted(-1, dy), shifted(1, dy)
        return jnp.where(
            lane8 < width_x,
            pick(low, row_index(low, 5)),
            pick(high, row_index(high, 5)),
        )

    def y_ghosts(dy):
        base = shifted(0, dy)
        index = row_index(base, 7 if dy < 0 else 6)
        outer = index >= atoms
        return jnp.where(
            outer,
            pick(x_ghosts(dy), jnp.where(outer, index - atoms, 0)),
            pick(base, jnp.where(outer, 0, index)),
        )

    table[0] = shifted(0, 0)
    table[1] = x_ghosts(0)
    table[2] = y_ghosts(-1)
    table[3] = y_ghosts(1)

    def whole(k, c):
        return jnp.broadcast_to(table[k, c : c + 1, :], (8, LANES))

    def forward_chunk(i, carry):
        word = rows_code[pl.ds(i * 8, 8), :]
        live = word >= 512.0
        n = jnp.where(live, word - 512.0, word).astype(I32)
        k = jnp.where(n >= atoms, 1, 0) + jnp.where(n >= 2 * atoms, 1, 0) + jnp.where(n >= 3 * atoms, 1, 0)
        n = n - atoms * k
        near = []
        for c in range(5):
            v = pick(whole(0, c), n)
            for part in (1, 2, 3):
                v = jnp.where(k == part, pick(whole(part, c), n), v)
            near.append(v)
        row = i * 8 + sub8
        block = jnp.zeros((8, LANES), I32)
        for b in range(1, blocks):
            block = block + jnp.where(row >= b * per_block, 1, 0)
        centre = block * GROUP + (lane8 & (GROUP - 1))
        off = []
        for c in range(3):
            d = near[c] - pick(whole(0, c), centre)
            d = d - period[c] * jnp.floor(d / period[c] + 0.5)
            off.append(jnp.where(live, d, SPACING if c == 0 else 0.0))
        radius = jnp.sqrt(off[0] * off[0] + off[1] * off[1] + off[2] * off[2])
        rinv = 1.0 / radius
        ux, uy, uz = (o * rinv for o in off)
        q = radius / CUTOFF
        valid = jnp.logical_and(live, q < 1.0)
        q2 = q * q
        q5 = q2 * q2 * q
        q6 = q5 * q
        env = jnp.where(valid, 1.0 + q6 * (-28.0 + q * (48.0 - 21.0 * q)), 0.0)
        denv = jnp.where(valid, (168.0 / CUTOFF) * q5 * (-1.0 + q * (2.0 - q)), 0.0)
        u = PI * jnp.minimum(q, 1.0) - 0.5 * PI
        w = u * u
        sin1 = 1.0 + w * (-1 / 2 + w * (1 / 24 + w * (-1 / 720 + w * (1 / 40320 + w * (-1 / 3628800 + w * (1 / 479001600))))))
        cos1 = -u * (1.0 + w * (-1 / 6 + w * (1 / 120 + w * (-1 / 5040 + w * (1 / 362880 + w * (-1 / 39916800 + w * (1 / 6227020800)))))))
        sc[0, i] = ux
        sc[1, i] = uy
        sc[2, i] = uz
        sc[3, i] = rinv
        sc[4, i] = denv
        zbase = i * 128
        scale = (2.0 / CUTOFF) ** 0.5 * rinv
        s_prev, s_now = jnp.zeros_like(sin1), sin1
        c_prev, c_now = jnp.ones_like(cos1), cos1
        for order in range(1, n_basis + 1):
            bes = scale * s_now
            zf[pl.ds(zbase + order - 1, 8, stride=16), :] = bes
            sc[4 + order, i] = scale * (order * PI / CUTOFF) * c_now - bes * rinv
            s_prev, s_now = s_now, 2.0 * cos1 * s_now - s_prev
            c_prev, c_now = c_now, 2.0 * cos1 * c_now - c_prev
        for kind in range(n_kinds):
            zf[pl.ds(zbase + n_basis + kind, 8, stride=16), :] = jnp.where(near[3] == float(kind), 1.0, 0.0)
        for extra in range(n_basis + n_kinds, 16):
            zf[pl.ds(zbase + extra, 8, stride=16), :] = jnp.zeros((8, LANES), F32)
        ys = (
            R3 * ux,
            R3 * uy,
            R3 * uz,
            R15 * ux * uy,
            R15 * uy * uz,
            0.5 * R5 * (3.0 * uz * uz - 1.0),
            R15 * ux * uz,
            0.5 * R15 * (ux * ux - uy * uy),
        )
        for m, y in enumerate(ys):
            zy[pl.ds(zbase + m, 8, stride=16), :] = y
        zy[pl.ds(zbase + 8, 8, stride=16), :] = env
        dest = near[4].astype(I32)
        tbase = i * 64
        pt[pl.ds(tbase + 6, 8, stride=8), :] = (dest >> 7).astype(F32)
        pt[pl.ds(tbase + 7, 8, stride=8), :] = (dest & (LANES - 1)).astype(F32)
        return carry

    for i in range(chunks):
        forward_chunk(i, 0)

    n_harm = 8
    wide = n_harm * GROUP
    own_lane = (lane8 & (GROUP - 1)) == sub8
    every = jnp.concatenate([jnp.where(own_lane, 1.0, 0.0)] * n_harm, axis=0).astype(BF16)
    ones_row = jnp.concatenate([jnp.where(own_lane, 1.0, 0.0), jnp.zeros((8, LANES), F32)], axis=0).astype(BF16)
    at_ef = wide + 2 * GROUP
    at_dlp = at_ef + ch

    degree_rows = ((1, 0, 3 * GROUP), (2, 3 * GROUP, wide), (0, wide, wide + 2 * GROUP))

    def by_degree(which, sums):
        parts = []
        for degree, a, b in degree_rows:
            grown = exact_dot(jnp.concatenate([x[a:b] for x in sums], axis=0), which, degree)
            parts.append([grown[t * (b - a) : (t + 1) * (b - a)] for t in range(len(sums))])
        return [jnp.concatenate([p[t] for p in parts], axis=0) for t in range(len(sums))]

    def exact_dot(rows, which, degree):
        high = rows.astype(BF16).astype(F32)
        joined = jnp.concatenate([high, rows - high, high], axis=1).astype(BF16)
        return nn_dot(joined, mats[which, degree])

    def as_left(turned, pad):
        tall_one = jnp.concatenate([turned, jnp.zeros((LANES - at_ef, ch), F32)], axis=0)
        return (tall_one.T + pad)[:, 0:at_dlp]

    w_out = wcol[...]
    kept = {}

    def env_row(row):
        return zy[row * 16 + 8 : row * 16 + 9, :]

    def stage_pre(b):
        base = b * per_block
        feats = jnp.concatenate(
            [zf[(base + jb) * 16 : (base + jb + 1) * 16, :] for jb in range(per_block)], axis=1
        )
        kept["pre", b] = nn_dot(w1s[...], feats.astype(BF16))

    def stage_feat(b):
        centre_term = cterm[b]
        pre = kept.pop(("pre", b))
        for jb in range(per_block):
            row = b * per_block + jb
            cols = slice(jb * LANES, (jb + 1) * LANES)
            z = zy[row * 16 : row * 16 + 16, :]
            env = z[8:9]
            p = pre[:, cols] + centre_term
            sig = sigmoid(p)
            s1 = p * sig
            s1_s[row] = s1
            ds_s[row] = (sig + s1 * (1.0 - sig)) * env
            rhs[b, at_ef : at_ef + ch, cols] = (s1 * env).astype(BF16)
            for m in range(0, n_harm, 2):
                two = [jnp.where(own_lane, z[t : t + 1], 0.0) for t in (m, m + 1)]
                rhs[b, m * GROUP : (m + 2) * GROUP, cols] = jnp.concatenate(two, axis=0).astype(BF16)
            rhs[b, wide : wide + 2 * GROUP, cols] = ones_row

    def stage_env(b):
        kept["f", b] = nt_dot(rhs[b, 0:at_ef, :], rhs[b, at_ef : at_ef + ch, :])

    def stage_grow(b):
        half = blocks // 2
        if b % half == 0:
            grown = by_degree(0, [kept.pop(("f", t)) for t in range(b, b + half)])
            for t in range(half):
                kept["g", b + t] = grown[t]

    def stage_lp(b):
        left = as_left(kept["g", b], w0pad[0])
        kept["lp", b] = split_dot(left, rhs[b, 0:at_dlp, :])

    def stage_latent(b):
        lp_all = kept.pop(("lp", b))
        for jb in range(per_block):
            row = b * per_block + jb
            cols = slice(jb * LANES, (jb + 1) * LANES)
            env = env_row(row)
            lp = lp_all[:, cols]
            sig = sigmoid(lp)
            lat = lp * sig
            hid_s[row] = w_out * (s1_s[row] * env + lat)
            dlp = (w_out * env) * (sig + lat * (1.0 - sig))
            rhs[b, at_dlp : at_dlp + ch, cols] = dlp.astype(BF16)

    def stage_back(b):
        kept["f", b] = nt_dot(rhs[b, 0:at_ef, :], rhs[b, at_dlp : at_dlp + ch, :])

    def stage_shrink(b):
        half = blocks // 2
        if b % half == 0:
            grown = by_degree(1, [kept.pop(("f", t)) for t in range(b, b + half)])
            for t in range(half):
                kept["d", b + t] = grown[t]

    def stage_de(b):
        grown = kept.pop(("d", b))
        left = as_left(grown, w0pad[1])
        kept["de", b] = split_dot(left, jnp.concatenate([rhs[b, 0:at_ef, :], rhs[b, at_dlp : at_dlp + ch, :]], axis=0))
        both = jnp.concatenate([grown[0:wide], kept.pop(("g", b))[0:wide]], axis=1)
        kept["dy", b] = nn_dot(both.astype(BF16), rhs[b, at_ef : at_dlp + ch, :])

    def stage_edge(b):
        de_all = kept.pop(("de", b))
        dy_all = kept.pop(("dy", b))
        for jb in range(per_block):
            row = b * per_block + jb
            cols = slice(jb * LANES, (jb + 1) * LANES)
            de = de_all[:, cols] + w_out * env_row(row)
            dpt_s[b, 0:ch, cols] = (de * ds_s[row]).astype(BF16)
            dpt_s[b, ch : 2 * ch, cols] = (hid_s[row] + de * s1_s[row]).astype(BF16)
            dpt_s[b, 2 * ch :, cols] = dy_all[:, cols].astype(BF16) * every

    def stage_fold(b):
        got = split_dot(w_last, dpt_s[b])
        for jb in range(per_block):
            row = b * per_block + jb
            zd[row * 24 : row * 24 + 24, :] = got[0:24, jb * LANES : (jb + 1) * LANES]

    stages = (
        stage_pre,
        stage_feat,
        stage_env,
        stage_grow,
        stage_lp,
        stage_latent,
        stage_back,
        stage_shrink,
        stage_de,
        stage_edge,
        stage_fold,
    )
    teams = (range(0, blocks // 2), range(blocks // 2, blocks))
    for tick in range(len(stages) + 3):
        for late, team in enumerate(teams):
            if 0 <= tick - 3 * late < len(stages):
                for b in team:
                    stages[tick - 3 * late](b)
    for row in range(n_rows, chunks * 8):
        zd[row * 24 : row * 24 + 24, :] = jnp.zeros((24, LANES), F32)

    def put_parts(store, values):
        for c in range(3):
            high = values[c].astype(BF16).astype(F32)
            store(c, high)
            store(c + 3, values[c] - high)

    def backward_chunk(i, carry):
        zbase = i * 192

        def d(which):
            return zd[pl.ds(zbase + which, 8, stride=24), :]

        ux, uy, uz, rinv, denv = (sc[t, i] for t in range(5))
        dr = d(8) * denv
        for order in range(n_basis):
            dr = dr + d(order) * sc[5 + order, i]
        d1, d2, d3, d4, d5, d6, d7, d8 = (d(16 + m) for m in range(8))
        dux = R3 * d1 + R15 * (uy * d4 + uz * d7 + ux * d8)
        duy = R3 * d2 + R15 * (ux * d4 + uz * d5 - uy * d8)
        duz = R3 * d3 + R15 * (uy * d5 + ux * d7) + (3.0 * R5) * uz * d6
        radial = dr - rinv * (dux * ux + duy * uy + duz * uz)
        forces = [-(radial * u + rinv * du) for u, du in ((ux, dux), (uy, duy), (uz, duz))]
        at = pl.ds(i * 8, 8)
        for c in range(3):
            g3[c, at, :] = forces[c]

        def store(which, value):
            pt[pl.ds(i * 64 + which, 8, stride=8), :] = value

        put_parts(store, forces)
        return carry

    for i in range(chunks):
        backward_chunk(i, 0)

    halfway = blocks // 2
    pt[chunks * 64 :, :] = jnp.zeros((64, LANES), F32)
    sums = []
    for c in range(3):
        rows = jnp.concatenate(
            [
                jnp.sum(g3[c, b * per_block : (b + 1) * per_block, :], axis=0, keepdims=True)
                for b in range(blocks)
            ],
            axis=0,
        )
        rows = -(rows + pltpu.roll(rows, LANES // 2, 1))
        sums.append(jnp.where(lane1 < LANES // 2, rows[0:halfway], rows[halfway:]))
    for b in range(halfway):
        at = (n_rows + b) * 8

        def store(which, value):
            pt[at + which : at + which + 1, :] = value[b : b + 1]

        put_parts(store, sums)
        spread = (lane8 & (GROUP - 1)) + jnp.where(lane8 < LANES // 2, b, b + halfway) * GROUP
        dest = pick(whole(0, 4), spread)[0:1].astype(I32)
        pt[at + 6 : at + 7, :] = (dest >> 7).astype(F32)
        pt[at + 7 : at + 8, :] = (dest & (LANES - 1)).astype(F32)

    n_targets = len(TARGETS)
    tall = 96
    sub16 = lax.broadcasted_iota(I32, (16, LANES), 0)
    pair = jnp.where(sub16 >= 8, 1.0, 0.0)
    pairs = [(pair + 2.0 * b).astype(BF16) for b in range((n_targets + 1) // 2)]
    steps = [(sub16 + 16 * b).astype(F32).astype(BF16) for b in range(tall // 16)]
    zero16 = jnp.zeros((16, LANES), BF16)
    one16 = jnp.ones((16, LANES), BF16)

    spread_out = None
    rows_left = n_rows + halfway + (n_rows + halfway) % 2
    for first_row in range(0, rows_left, 8):
        lefts, rights = [], []
        for row in range(first_row, min(first_row + 8, rows_left)):
            v = pt[row * 8 : row * 8 + 8, :]
            where_to = jnp.broadcast_to(v[6:7], (16, LANES)).astype(BF16)
            lo = jnp.broadcast_to(v[7:8], (16, LANES)).astype(BF16)
            twice = jnp.concatenate([v, v], axis=0).astype(BF16)
            lefts.append(jnp.concatenate([jnp.where(where_to == p, twice, zero16) for p in pairs], axis=0))
            rights.append(jnp.concatenate([jnp.where(lo == p, one16, zero16) for p in steps], axis=0))
        part = nt_dot(jnp.concatenate(lefts, axis=1), jnp.concatenate(rights, axis=1))
        spread_out = part if spread_out is None else spread_out + part
    for t in range(n_targets):
        tile = spread_out[t * 8 : t * 8 + 8, :]
        ret_out[t, 0:3, 0:tall] = tile[0:3] + tile[3:6]
    for dx, dy in FAR:
        tile = jnp.concatenate([ret_out[target_slot(dx, dy)], jnp.zeros((4, LANES), F32)], axis=0)
        far_out[far_slot(dx, dy)] = jnp.where(
            lane1 < atoms + 10,
            tile[0:1],
            jnp.where(lane1 < atoms + 20, pltpu.roll(tile, 10, 1)[1:2], pltpu.roll(tile, 20, 1)[2:3]),
        )

    returns = []
    for group, slot, out, into, send_sems, recv_sems in (
        (NIGH, target_slot, ret_out, ret_in, ret_send, ret_recv),
        (FAR, far_slot, far_out, far_in, far_send, far_recv),
    ):
        for dx, dy in group:
            there = slot(-dx, -dy)
            copy = pltpu.make_async_remote_copy(
                src_ref=out.at[slot(dx, dy)],
                dst_ref=into.at[there],
                send_sem=send_sems.at[there],
                recv_sem=recv_sems.at[there],
                device_id=device(dx, dy),
                device_id_type=MESH,
            )
            copy.start()
            returns.append(copy)

    for copy in carried:
        copy.wait_recv()
    settle = jnp.broadcast_to(source, (8, LANES))
    mine, low, high = load[1], load[0], load[2]
    held = jnp.where(lane8 < atoms, mine, jnp.where(lane8 < atoms + 5, low, high))
    held = jnp.where(lane8 < LANES - 1, held, 0.0)
    held = pick(held, settle)
    total = ret_out[target_slot(0, 0)]
    for copy in returns:
        copy.wait_recv()
    for dx, dy in NIGH:
        total = total + ret_in[target_slot(dx, dy)]
    far = far_in[0]
    for t in range(1, len(FAR)):
        far = far + far_in[t]
    far = jnp.broadcast_to(far, (8, LANES))
    seats = jnp.logical_and(lane8 >= atoms, lane8 < atoms + 10)
    moved = jnp.where(sub8 == 0, far, jnp.where(sub8 == 1, pltpu.roll(far, LANES - 10, 1), pltpu.roll(far, LANES - 20, 1)))
    total = jnp.concatenate([total, jnp.zeros((4, LANES), F32)], axis=0) + jnp.where(seats, moved, 0.0)
    force = pick(total, settle)[0:3]
    fresh = held[0:3] + 0.5 * TIME_STEP * force * held[6:7]
    for c in range(3):
        both_ref[0, c] = fresh[c : c + 1, 0:atoms]
        both_ref[0, c + 3] = held[c + 3 : c + 4, 0:atoms]
    for copy in sends + carried + returns:
        copy.wait_send()


def on_device(*args):
    atoms = args[0].shape[3]
    slots = args[4].shape[2]
    ch = args[13].shape[0]
    chunks = (atoms // GROUP * (slots // 16) + 7) // 8
    n_gx, n_yz = lax.axis_size("gx"), lax.axis_size("yz")
    period = (n_gx * PX * SPACING, n_yz * PY * SPACING, PZ * SPACING)
    pos, vel, frc, spc, nbr, msk, sx, sy, ms, mr, wb, ec, en, we, wl, wo = args
    pos, vel, frc = (x.transpose(0, 2, 1, 3) for x in (pos, vel, frc))
    nbr, msk = (x.transpose(0, 1, 3, 2) for x in (nbr, msk))
    args = (pos, vel, frc, spc, nbr, msk, sx, sy, ms, mr, wb, ec.T, en.T, we, wl.T, wo.reshape(1, ch))

    def body(*refs):
        kernel_body(period, atoms, slots, *refs)

    vmem = pl.BlockSpec(memory_space=pltpu.VMEM)
    per_block = slots // 16
    blocks = atoms // GROUP
    dma = pltpu.SemaphoreType.DMA
    out = jax.ShapeDtypeStruct((1, 6, 1, atoms), F32)
    staged = tuple(
        (pltpu.SMEM if at in (8, 9) else pltpu.VMEM)(x.shape, x.dtype) for at, x in enumerate(args)
    )
    both = pl.pallas_call(
        body,
        out_shape=out,
        in_specs=[pl.BlockSpec(memory_space=pl.ANY)] * 16,
        out_specs=vmem,
        scratch_shapes=[
            staged,
            pltpu.VMEM((9, 8, LANES), F32),
            pltpu.VMEM((3, 8, LANES), F32),
            pltpu.VMEM((15, 4, LANES), F32),
            pltpu.VMEM((15, 4, LANES), F32),
            pltpu.VMEM((6, 1, LANES), F32),
            pltpu.VMEM((6, 1, LANES), F32),
            pltpu.VMEM((atoms, LANES), F32),
            pltpu.VMEM((chunks * 8, LANES), F32),
            pltpu.VMEM((4, 8, LANES), F32),
            pltpu.VMEM((13, chunks, 8, LANES), F32),
            pltpu.VMEM((chunks * 128, LANES), F32),
            pltpu.VMEM((chunks * 128, LANES), F32),
            pltpu.VMEM((chunks * 192, LANES), F32),
            pltpu.VMEM((chunks * 64 + 64, LANES), F32),
            pltpu.VMEM((atoms // GROUP, ch, LANES), F32),
            pltpu.VMEM((2, 3, 3 * ch, ch), BF16),
            pltpu.VMEM((ch, 16), BF16),
            pltpu.VMEM((ch, LANES), F32),
            pltpu.VMEM((2, ch, LANES), F32),
            pltpu.VMEM((blocks, 10 * GROUP + 2 * ch, per_block * LANES), BF16),
            pltpu.VMEM((blocks * per_block, ch, LANES), F32),
            pltpu.VMEM((blocks * per_block, ch, LANES), F32),
            pltpu.VMEM((blocks * per_block, ch, LANES), F32),
            pltpu.VMEM((blocks, 2 * ch + 8 * GROUP, per_block * LANES), BF16),
            pltpu.VMEM((3, 64, LANES), F32),
            dma((16,)),
            dma((9,)),
            dma((9,)),
            dma((3,)),
            dma((3,)),
            dma((15,)),
            dma((15,)),
            dma((6,)),
            dma((6,)),
        ],
        compiler_params=pltpu.CompilerParams(
            collective_id=0, has_side_effects=True, vmem_limit_bytes=60 * 1024 * 1024
        ),
    )(*args)
    return both[:, 0:3].transpose(0, 2, 1, 3), both[:, 3:6].transpose(0, 2, 1, 3)


def solution(mesh):
    block4 = P("gx", "yz", None, None)
    block3 = P("gx", "yz", None)
    return jax.shard_map(
        on_device,
        mesh=mesh,
        in_specs=(block4, block4, block4, block3) + (block4,) * 6 + (P(),) * 6,
        out_specs=(block4, block4),
        check_vma=False,
    )
```

```python
import jax
import jax.numpy as jnp
from jax import lax
from jax.experimental import pallas as pl
from jax.experimental.pallas import tpu as pltpu
from jax.sharding import PartitionSpec as P

PX = 4
PY = 4
PZ = 5
STEPS = 1
SPACING = 2.15
CUTOFF = 6.0
TIME_STEP = 0.05
ENV_SCALE = 0.125
MASSES = (1.008, 12.011, 14.007, 15.999, 32.06)
HIGHEST = lax.Precision.HIGHEST
MESH = pl.DeviceIdType.MESH
F32 = jnp.float32
BF16 = jnp.bfloat16
I32 = jnp.int32

LANES = 128
GROUP = 8
PI = 3.141592653589793
R3 = 3.0**0.5
R5 = 5.0**0.5
R15 = 15.0**0.5

HALO = [(dx, dy) for dy in (-1, 0, 1) for dx in (-1, 0, 1)]
NEAR = sorted((pos for pos in HALO if pos != (0, 0)), key=lambda pos: -abs(pos[0]) - 2 * abs(pos[1]))
TARGETS = [(dx, dy) for dy in (-1, 0, 1) for dx in (-2, -1, 0, 1, 2)]
REST = sorted((pos for pos in TARGETS if pos != (0, 0)), key=lambda pos: -(abs(pos[0]) % 2) - 2 * abs(pos[1]))


FAR = [pos for pos in REST if abs(pos[0]) == 2]
NIGH = [pos for pos in REST if abs(pos[0]) < 2]
DROPPED = 127
EMPTY = 95


def far_slot(dx, dy):
    return (dy + 1) * 2 + (dx + 2) // 4


def halo_slot(dx, dy):
    return (dy + 1) * 3 + dx + 1


def target_slot(dx, dy):
    return (dy + 1) * 5 + dx + 2


def nt_dot(a, b, precision=None):
    return lax.dot_general(
        a, b, (((1,), (1,)), ((), ())), precision=precision, preferred_element_type=F32
    )


def nn_dot(a, b, precision=None):
    return jnp.dot(a, b, precision=precision, preferred_element_type=F32)


def halves(x):
    high = x.astype(BF16)
    low = (x - high.astype(F32)).astype(BF16)
    return high, low


def pick(rows, index):
    return jnp.take_along_axis(rows, index, axis=1, mode="promise_in_bounds")


def turn(eye, x):
    high, low = halves(x)
    return nt_dot(eye, high) + nt_dot(eye, low)


def split_dot(left, right):
    high, low = halves(left)
    return nn_dot(high, right) + nn_dot(low, right)


def sigmoid(x):
    return 0.5 * jnp.tanh(0.5 * x) + 0.5


def kernel_body(
    period,
    atoms,
    slots,
    *refs,
):
    raw, refs = refs[:16], refs[16:]
    (
        both_ref,
        staged,
        halo,
        edge,
        load,
        ret_out,
        ret_in,
        far_out,
        far_in,
        nb_pad,
        rows_code,
        table,
        sc,
        zf,
        zy,
        zd,
        pt,
        cterm,
        mats,
        w1s,
        wcol,
        w0pad,
        rhs,
        s1_s,
        ds_s,
        hid_s,
        dpt_s,
        g3,
        spot,
        early,
        load_sems,
        halo_send,
        halo_recv,
        load_send,
        load_recv,
        ret_send,
        ret_recv,
        far_send,
        far_recv,
    ) = refs
    gx = lax.axis_index("gx")
    yz = lax.axis_index("yz")
    n_gx = lax.axis_size("gx")
    n_yz = lax.axis_size("yz")
    blocks = atoms // GROUP
    per_block = slots // 16
    n_rows = blocks * per_block
    chunks = (n_rows + 7) // 8

    def device(dx, dy):
        return (lax.rem(gx + dx + n_gx, n_gx), lax.rem(yz + dy + n_yz, n_yz))

    barrier = pltpu.get_barrier_semaphore()
    loads = []
    first = (0, 1, 2, 3, 6, 7, 8, 9)
    for at, (far, close) in enumerate(zip(raw, staged)):
        loads.append(pltpu.make_async_copy(far, close, load_sems.at[at]))
    for dx, dy in REST:
        pl.semaphore_signal(barrier, inc=1, device_id=device(dx, dy), device_id_type=MESH)

    for at in first:
        loads[at].start()
    for at in range(16):
        if at not in first:
            loads[at].start()
    (
        pos_ref,
        vel_ref,
        frc_ref,
        spc_ref,
        nbr_ref,
        msk_ref,
        sx_ref,
        sy_ref,
        ms_ref,
        mr_ref,
        wb_ref,
        ec_ref,
        en_ref,
        we_ref,
        wl_ref,
        wo_ref,
    ) = staged
    for at in first:
        loads[at].wait()

    lane1 = lax.broadcasted_iota(I32, (1, LANES), 1)
    lane8 = lax.broadcasted_iota(I32, (8, LANES), 1)
    sub8 = lax.broadcasted_iota(I32, (8, LANES), 0)

    own = halo_slot(0, 0)
    kinds = spc_ref[0].astype(F32)
    minv = jnp.zeros_like(kinds)
    for kind, mass in enumerate(MASSES):
        minv = jnp.where(kinds == float(kind), 1.0 / jnp.float32(mass), minv)
    halo[own] = jnp.zeros((8, LANES), F32)
    load[1] = jnp.zeros((8, LANES), F32)
    for c in range(3):
        start = pos_ref[0, c]
        velocity = vel_ref[0, c] + 0.5 * TIME_STEP * frc_ref[0, c] * minv
        coords = start + TIME_STEP * velocity
        halo[own, c : c + 1, 0:atoms] = coords
        load[1, c : c + 1, 0:atoms] = velocity
        load[1, c + 3 : c + 4, 0:atoms] = (coords - start) / (STEPS * TIME_STEP)
    halo[own, 3:4, 0:atoms] = kinds
    code = lane1
    place = lane1
    source = lane1
    for side in (0, 1):
        for k in range(ms_ref.shape[3]):
            seat = atoms + 5 * (1 - side) + k
            code = jnp.where(lane1 == mr_ref[0, 0, side, k], DROPPED, code)
    for side in (0, 1):
        for k in range(ms_ref.shape[3]):
            seat = atoms + 5 * (1 - side) + k
            gone = ms_ref[0, 0, side, k]
            code = jnp.where(lane1 == gone, (2 * side - 1) * LANES + seat, code)
            place = jnp.where(lane1 == seat, gone, place)
            source = jnp.where(lane1 == gone, EMPTY, source)
    for side in (0, 1):
        for k in range(ms_ref.shape[3]):
            source = jnp.where(lane1 == mr_ref[0, 0, side, k], atoms + 5 * side + k, source)
    code = jnp.where(lane1 < atoms, code + LANES, 0)
    halo[own, 4:5, :] = code.astype(F32)
    halo[own, 6:8, 0:atoms] = sy_ref[0, 0].astype(F32)
    load[1, 6:7, 0:atoms] = minv
    width_x = sx_ref.shape[3]
    g3[0] = jnp.zeros((64, LANES), F32)
    g3[0, 0:2, 0:width_x] = sx_ref[0, 0].astype(F32)
    lists = g3[0, 0:8, :]
    outward = lists[1:2] + pltpu.roll(lists, width_x, 1)[0:1]
    edge[...] = pick(halo[own], jnp.broadcast_to(outward, (8, LANES)).astype(I32))
    load[1] = pick(load[1], jnp.broadcast_to(place, (8, LANES)))

    pl.semaphore_wait(barrier, len(REST))
    sends, carried = [], []
    for dx, dy in NEAR:
        there = halo_slot(-dx, -dy)
        copy = pltpu.make_async_remote_copy(
            src_ref=edge if dx else halo.at[own],
            dst_ref=halo.at[there],
            send_sem=halo_send.at[there],
            recv_sem=halo_recv.at[there],
            device_id=device(dx, dy),
            device_id_type=MESH,
        )
        copy.start()
        sends.append(copy)
    for dx in (-1, 1):
        there = 1 - dx
        copy = pltpu.make_async_remote_copy(
            src_ref=load.at[1],
            dst_ref=load.at[there],
            send_sem=load_send.at[there],
            recv_sem=load_recv.at[there],
            device_id=device(dx, 0),
            device_id_type=MESH,
        )
        copy.start()
        carried.append(copy)

    for t in range(len(TARGETS)):
        ret_out[t] = jnp.zeros((4, LANES), F32)

    for at in range(16):
        if at not in first:
            loads[at].wait()
    nb_pad[...] = jnp.zeros((atoms, LANES), F32)
    nb_pad[:, 0:slots] = nbr_ref[0, 0].astype(F32) + 512.0 * msk_ref[0, 0].astype(F32)
    rows_code[...] = jnp.zeros((chunks * 8, LANES), F32)
    in_row = (lane8 & (GROUP - 1)) == sub8
    for block in range(blocks):
        group = nb_pad[block * GROUP : (block + 1) * GROUP, :]
        for jb in range(per_block):
            moved = pick(group, (lane8 >> 3) + jb * 16)
            row = jnp.sum(jnp.where(in_row, moved, 0.0), axis=0, keepdims=True)
            r = block * per_block + jb
            rows_code[r : r + 1, :] = row

    ch = we_ref.shape[0]
    eye = (
        lax.broadcasted_iota(I32, (ch, ch), 0) == lax.broadcasted_iota(I32, (ch, ch), 1)
    ).astype(F32)
    n_basis = wb_ref.shape[0]
    n_kinds = en_ref.shape[0]
    wl_t = wl_ref[...]
    mixes = []
    eye16 = eye.astype(BF16)
    we_h, we_l = halves(we_ref[...])
    for part in range(3):
        part_t = wl_t[:, (part + 1) * ch : (part + 2) * ch]
        part_h, part_l = halves(part_t)
        mixes.append(ENV_SCALE * (nt_dot(part_h, we_h) + nt_dot(part_l, we_h) + nt_dot(part_h, we_l)))
    for part in range(3):
        turned = mixes[part]
        straight = turn(eye16, turned)
        for which, m in enumerate((straight, turned)):
            m_high, m_low = halves(m)
            mats[which, part] = jnp.concatenate([m_high, m_high, m_low], axis=0)
    w0_t = wl_t[:, 0:ch]
    w0 = turn(eye16, w0_t)
    ec = turn(eye16, ec_ref[...])
    w0pad[...] = jnp.zeros((2, ch, LANES), F32)
    w0pad[0, :, 80 : 80 + ch] = w0_t
    w0pad[1, :, 80 : 80 + ch] = w0
    w1f = jnp.concatenate(
        [
            nt_dot(eye16, wb_ref[...].astype(BF16)),
            nt_dot(eye16, en_ref[...].astype(BF16)),
            jnp.zeros((ch, 16 - n_basis - n_kinds), F32),
        ],
        axis=1,
    )
    w1s[...] = w1f.astype(BF16)
    row32 = lax.broadcasted_iota(I32, (32, LANES), 0)
    lane32 = lax.broadcasted_iota(I32, (32, LANES), 1)
    g3[1, 0:32, :] = jnp.zeros((32, LANES), F32)
    g3[1, 0:n_basis, 0:ch] = wb_ref[...]
    head = g3[1, 0:32, :] + jnp.where(
        (row32 == 8) & (lane32 >= ch) & (lane32 < 2 * ch), 1.0, 0.0
    ) + jnp.where((lane32 >= 2 * ch) & (row32 == 16 + ((lane32 - 2 * ch) >> 3)), 1.0, 0.0)
    w_last = head
    wcol[...] = jnp.broadcast_to(
        jnp.sum(jnp.where(eye > 0, wo_ref[...], 0.0), axis=1, keepdims=True), (ch, LANES)
    )

    def shifted(dx, dy):
        step = float(LANES * ((dy + 1) * 5 + dx + 1))
        return halo[halo_slot(dx, dy)] + jnp.where(sub8 == 4, step, 0.0)

    def whole(k, c):
        return jnp.broadcast_to(table[k, c : c + 1, :], (8, LANES))

    table[0] = shifted(0, 0)
    for i in range(chunks):
        word = rows_code[i * 8 : i * 8 + 8, :]
        n = jnp.where(word >= 512.0, word - 512.0, word).astype(I32)
        k = jnp.where(n >= atoms, 1, 0) + jnp.where(n >= 2 * atoms, 1, 0) + jnp.where(n >= 3 * atoms, 1, 0)
        n = n - atoms * k
        spot[0, i] = n
        spot[1, i] = k
        for c in range(5):
            early[c, i] = pick(whole(0, c), n)
        row = i * 8 + sub8
        block = jnp.zeros((8, LANES), I32)
        for b in range(1, blocks):
            block = block + jnp.where(row >= b * per_block, 1, 0)
        centre = block * GROUP + (lane8 & (GROUP - 1))
        for c in range(3):
            early[5 + c, i] = pick(whole(0, c), centre)

    kind_rows = jnp.broadcast_to(halo[own, 3:4, :], (8, LANES))
    for block in range(blocks):
        spread = (lane8 & (GROUP - 1)) + block * GROUP
        kind_row = jnp.broadcast_to(pick(kind_rows, spread)[0:1], (ch, LANES))
        term = jnp.zeros((ch, LANES), F32)
        for kind in range(n_kinds):
            term = jnp.where(
                kind_row == float(kind),
                jnp.broadcast_to(ec[:, kind : kind + 1], (ch, LANES)),
                term,
            )
        cterm[block] = term

    for copy in sends:
        copy.wait_recv()

    def row_index(rows, which):
        return jnp.broadcast_to(rows[which : which + 1, :], (8, LANES)).astype(I32)

    def x_ghosts(dy):
        return jnp.where(lane8 < width_x, shifted(-1, dy), shifted(1, dy))

    def y_ghosts(dy):
        base = shifted(0, dy)
        index = row_index(base, 7 if dy < 0 else 6)
        outer = index >= atoms
        return jnp.where(
            outer,
            pick(x_ghosts(dy), jnp.where(outer, index - atoms, 0)),
            pick(base, jnp.where(outer, 0, index)),
        )

    table[1] = x_ghosts(0)
    table[2] = y_ghosts(-1)
    table[3] = y_ghosts(1)

    def forward_chunk(i, carry):
        word = rows_code[pl.ds(i * 8, 8), :]
        live = word >= 512.0
        n, k = spot[0, i], spot[1, i]
        near = []
        for c in range(5):
            v = early[c, i]
            for part in (1, 2, 3):
                v = jnp.where(k == part, pick(whole(part, c), n), v)
            near.append(v)
        off = []
        for c in range(3):
            d = near[c] - early[5 + c, i]
            d = d - period[c] * jnp.floor(d / period[c] + 0.5)
            off.append(jnp.where(live, d, SPACING if c == 0 else 0.0))
        radius = jnp.sqrt(off[0] * off[0] + off[1] * off[1] + off[2] * off[2])
        rinv = 1.0 / radius
        ux, uy, uz = (o * rinv for o in off)
        q = radius / CUTOFF
        valid = jnp.logical_and(live, q < 1.0)
        q2 = q * q
        q5 = q2 * q2 * q
        q6 = q5 * q
        env = jnp.where(valid, 1.0 + q6 * (-28.0 + q * (48.0 - 21.0 * q)), 0.0)
        denv = jnp.where(valid, (168.0 / CUTOFF) * q5 * (-1.0 + q * (2.0 - q)), 0.0)
        u = PI * jnp.minimum(q, 1.0) - 0.5 * PI
        w = u * u
        sin1 = 1.0 + w * (-1 / 2 + w * (1 / 24 + w * (-1 / 720 + w * (1 / 40320 + w * (-1 / 3628800 + w * (1 / 479001600))))))
        cos1 = -u * (1.0 + w * (-1 / 6 + w * (1 / 120 + w * (-1 / 5040 + w * (1 / 362880 + w * (-1 / 39916800 + w * (1 / 6227020800)))))))
        sc[0, i] = ux
        sc[1, i] = uy
        sc[2, i] = uz
        sc[3, i] = rinv
        sc[4, i] = denv
        zbase = i * 128
        scale = (2.0 / CUTOFF) ** 0.5 * rinv
        s_prev, s_now = jnp.zeros_like(sin1), sin1
        c_prev, c_now = jnp.ones_like(cos1), cos1
        for order in range(1, n_basis + 1):
            bes = scale * s_now
            zf[pl.ds(zbase + order - 1, 8, stride=16), :] = bes
            sc[4 + order, i] = scale * (order * PI / CUTOFF) * c_now - bes * rinv
            s_prev, s_now = s_now, 2.0 * cos1 * s_now - s_prev
            c_prev, c_now = c_now, 2.0 * cos1 * c_now - c_prev
        for kind in range(n_kinds):
            zf[pl.ds(zbase + n_basis + kind, 8, stride=16), :] = jnp.where(near[3] == float(kind), 1.0, 0.0)
        for extra in range(n_basis + n_kinds, 16):
            zf[pl.ds(zbase + extra, 8, stride=16), :] = jnp.zeros((8, LANES), F32)
        ys = (
            R3 * ux,
            R3 * uy,
            R3 * uz,
            R15 * ux * uy,
            R15 * uy * uz,
            0.5 * R5 * (3.0 * uz * uz - 1.0),
            R15 * ux * uz,
            0.5 * R15 * (ux * ux - uy * uy),
        )
        for m, y in enumerate(ys):
            zy[pl.ds(zbase + m, 8, stride=16), :] = y
        zy[pl.ds(zbase + 8, 8, stride=16), :] = env
        dest = near[4].astype(I32)
        tbase = i * 64
        pt[pl.ds(tbase + 6, 8, stride=8), :] = (dest >> 7).astype(F32)
        pt[pl.ds(tbase + 7, 8, stride=8), :] = (dest & (LANES - 1)).astype(F32)
        return carry

    for i in range(chunks):
        forward_chunk(i, 0)

    n_harm = 8
    wide = n_harm * GROUP
    own_lane = (lane8 & (GROUP - 1)) == sub8
    every = jnp.concatenate([jnp.where(own_lane, 1.0, 0.0)] * n_harm, axis=0).astype(BF16)
    ones_row = jnp.concatenate([jnp.where(own_lane, 1.0, 0.0), jnp.zeros((8, LANES), F32)], axis=0).astype(BF16)
    at_ef = wide + 2 * GROUP
    at_dlp = at_ef + ch

    degree_rows = ((1, 0, 3 * GROUP), (2, 3 * GROUP, wide), (0, wide, wide + 2 * GROUP))

    def by_degree(which, sums):
        parts = []
        for degree, a, b in degree_rows:
            grown = exact_dot(jnp.concatenate([x[a:b] for x in sums], axis=0), which, degree)
            parts.append([grown[t * (b - a) : (t + 1) * (b - a)] for t in range(len(sums))])
        return [jnp.concatenate([p[t] for p in parts], axis=0) for t in range(len(sums))]

    def exact_dot(rows, which, degree):
        high = rows.astype(BF16).astype(F32)
        joined = jnp.concatenate([high, rows - high, high], axis=1).astype(BF16)
        return nn_dot(joined, mats[which, degree])

    def as_left(turned, pad):
        tall_one = jnp.concatenate([turned, jnp.zeros((LANES - at_ef, ch), F32)], axis=0)
        return (tall_one.T + pad)[:, 0:at_dlp]

    w_out = wcol[...]
    kept = {}

    def env_row(row):
        return zy[row * 16 + 8 : row * 16 + 9, :]

    def stage_pre(b):
        base = b * per_block
        feats = jnp.concatenate(
            [zf[(base + jb) * 16 : (base + jb + 1) * 16, :] for jb in range(per_block)], axis=1
        )
        kept["pre", b] = nn_dot(w1s[...], feats.astype(BF16))

    def stage_feat(b):
        centre_term = cterm[b]
        pre = kept.pop(("pre", b))
        for jb in range(per_block):
            row = b * per_block + jb
            cols = slice(jb * LANES, (jb + 1) * LANES)
            z = zy[row * 16 : row * 16 + 16, :]
            env = z[8:9]
            p = pre[:, cols] + centre_term
            sig = sigmoid(p)
            s1 = p * sig
            s1_s[row] = s1
            ds_s[row] = (sig + s1 * (1.0 - sig)) * env
            rhs[b, at_ef : at_ef + ch, cols] = (s1 * env).astype(BF16)
            for m in range(0, n_harm, 2):
                two = [jnp.where(own_lane, z[t : t + 1], 0.0) for t in (m, m + 1)]
                rhs[b, m * GROUP : (m + 2) * GROUP, cols] = jnp.concatenate(two, axis=0).astype(BF16)
            rhs[b, wide : wide + 2 * GROUP, cols] = ones_row

    def stage_env(b):
        kept["f", b] = nt_dot(rhs[b, 0:at_ef, :], rhs[b, at_ef : at_ef + ch, :])

    def stage_grow(b):
        half = blocks // 2
        if b % half == 0:
            grown = by_degree(0, [kept.pop(("f", t)) for t in range(b, b + half)])
            for t in range(half):
                kept["g", b + t] = grown[t]

    def stage_lp(b):
        left = as_left(kept["g", b], w0pad[0])
        kept["lp", b] = split_dot(left, rhs[b, 0:at_dlp, :])

    def stage_latent(b):
        lp_all = kept.pop(("lp", b))
        for jb in range(per_block):
            row = b * per_block + jb
            cols = slice(jb * LANES, (jb + 1) * LANES)
            env = env_row(row)
            lp = lp_all[:, cols]
            sig = sigmoid(lp)
            lat = lp * sig
            hid_s[row] = w_out * (s1_s[row] * env + lat)
            dlp = (w_out * env) * (sig + lat * (1.0 - sig))
            rhs[b, at_dlp : at_dlp + ch, cols] = dlp.astype(BF16)

    def stage_back(b):
        kept["f", b] = nt_dot(rhs[b, 0:at_ef, :], rhs[b, at_dlp : at_dlp + ch, :])

    def stage_shrink(b):
        half = blocks // 2
        if b % half == 0:
            grown = by_degree(1, [kept.pop(("f", t)) for t in range(b, b + half)])
            for t in range(half):
                kept["d", b + t] = grown[t]

    def stage_de(b):
        grown = kept.pop(("d", b))
        left = as_left(grown, w0pad[1])
        kept["de", b] = split_dot(left, jnp.concatenate([rhs[b, 0:at_ef, :], rhs[b, at_dlp : at_dlp + ch, :]], axis=0))
        both = jnp.concatenate([grown[0:wide], kept.pop(("g", b))[0:wide]], axis=1)
        kept["dy", b] = nn_dot(both.astype(BF16), rhs[b, at_ef : at_dlp + ch, :])

    def stage_edge(b):
        de_all = kept.pop(("de", b))
        dy_all = kept.pop(("dy", b))
        for jb in range(per_block):
            row = b * per_block + jb
            cols = slice(jb * LANES, (jb + 1) * LANES)
            de = de_all[:, cols] + w_out * env_row(row)
            dpt_s[b, 0:ch, cols] = (de * ds_s[row]).astype(BF16)
            dpt_s[b, ch : 2 * ch, cols] = (hid_s[row] + de * s1_s[row]).astype(BF16)
            dpt_s[b, 2 * ch :, cols] = dy_all[:, cols].astype(BF16) * every

    def stage_fold(b):
        got = split_dot(w_last, dpt_s[b])
        for jb in range(per_block):
            row = b * per_block + jb
            zd[row * 24 : row * 24 + 24, :] = got[0:24, jb * LANES : (jb + 1) * LANES]

    stages = (
        stage_pre,
        stage_feat,
        stage_env,
        stage_grow,
        stage_lp,
        stage_latent,
        stage_back,
        stage_shrink,
        stage_de,
        stage_edge,
        stage_fold,
    )
    teams = (range(0, blocks // 2), range(blocks // 2, blocks))
    for tick in range(len(stages) + 3):
        for late, team in enumerate(teams):
            if 0 <= tick - 3 * late < len(stages):
                for b in team:
                    stages[tick - 3 * late](b)
    for row in range(n_rows, chunks * 8):
        zd[row * 24 : row * 24 + 24, :] = jnp.zeros((24, LANES), F32)

    def put_parts(store, values):
        for c in range(3):
            high = values[c].astype(BF16).astype(F32)
            store(c, high)
            store(c + 3, values[c] - high)

    def backward_chunk(i, carry):
        zbase = i * 192

        def d(which):
            return zd[pl.ds(zbase + which, 8, stride=24), :]

        ux, uy, uz, rinv, denv = (sc[t, i] for t in range(5))
        dr = d(8) * denv
        for order in range(n_basis):
            dr = dr + d(order) * sc[5 + order, i]
        d1, d2, d3, d4, d5, d6, d7, d8 = (d(16 + m) for m in range(8))
        dux = R3 * d1 + R15 * (uy * d4 + uz * d7 + ux * d8)
        duy = R3 * d2 + R15 * (ux * d4 + uz * d5 - uy * d8)
        duz = R3 * d3 + R15 * (uy * d5 + ux * d7) + (3.0 * R5) * uz * d6
        radial = dr - rinv * (dux * ux + duy * uy + duz * uz)
        forces = [-(radial * u + rinv * du) for u, du in ((ux, dux), (uy, duy), (uz, duz))]
        at = pl.ds(i * 8, 8)
        for c in range(3):
            g3[c, at, :] = forces[c]

        def store(which, value):
            pt[pl.ds(i * 64 + which, 8, stride=8), :] = value

        put_parts(store, forces)
        return carry

    for i in range(chunks):
        backward_chunk(i, 0)

    halfway = blocks // 2
    pt[chunks * 64 :, :] = jnp.zeros((64, LANES), F32)
    sums = []
    for c in range(3):
        rows = jnp.concatenate(
            [
                jnp.sum(g3[c, b * per_block : (b + 1) * per_block, :], axis=0, keepdims=True)
                for b in range(blocks)
            ],
            axis=0,
        )
        rows = -(rows + pltpu.roll(rows, LANES // 2, 1))
        sums.append(jnp.where(lane1 < LANES // 2, rows[0:halfway], rows[halfway:]))
    for b in range(halfway):
        at = (n_rows + b) * 8

        def store(which, value):
            pt[at + which : at + which + 1, :] = value[b : b + 1]

        put_parts(store, sums)
        spread = (lane8 & (GROUP - 1)) + jnp.where(lane8 < LANES // 2, b, b + halfway) * GROUP
        dest = pick(whole(0, 4), spread)[0:1].astype(I32)
        pt[at + 6 : at + 7, :] = (dest >> 7).astype(F32)
        pt[at + 7 : at + 8, :] = (dest & (LANES - 1)).astype(F32)

    n_targets = len(TARGETS)
    tall = 96
    sub16 = lax.broadcasted_iota(I32, (16, LANES), 0)
    pair = jnp.where(sub16 >= 8, 1.0, 0.0)
    pairs = [(pair + 2.0 * b).astype(BF16) for b in range((n_targets + 1) // 2)]
    steps = [(sub16 + 16 * b).astype(F32).astype(BF16) for b in range(tall // 16)]
    zero16 = jnp.zeros((16, LANES), BF16)
    one16 = jnp.ones((16, LANES), BF16)

    spread_out = None
    rows_left = n_rows + halfway + (n_rows + halfway) % 2
    for first_row in range(0, rows_left, 8):
        lefts, rights = [], []
        for row in range(first_row, min(first_row + 8, rows_left)):
            v = pt[row * 8 : row * 8 + 8, :]
            where_to = jnp.broadcast_to(v[6:7], (16, LANES)).astype(BF16)
            lo = jnp.broadcast_to(v[7:8], (16, LANES)).astype(BF16)
            twice = jnp.concatenate([v, v], axis=0).astype(BF16)
            lefts.append(jnp.concatenate([jnp.where(where_to == p, twice, zero16) for p in pairs], axis=0))
            rights.append(jnp.concatenate([jnp.where(lo == p, one16, zero16) for p in steps], axis=0))
        part = nt_dot(jnp.concatenate(lefts, axis=1), jnp.concatenate(rights, axis=1))
        spread_out = part if spread_out is None else spread_out + part
    for t in range(n_targets):
        tile = spread_out[t * 8 : t * 8 + 8, :]
        ret_out[t, 0:3, 0:tall] = tile[0:3] + tile[3:6]
    for dx, dy in FAR:
        tile = jnp.concatenate([ret_out[target_slot(dx, dy)], jnp.zeros((4, LANES), F32)], axis=0)
        far_out[far_slot(dx, dy)] = jnp.where(
            lane1 < atoms + 10,
            tile[0:1],
            jnp.where(lane1 < atoms + 20, pltpu.roll(tile, 10, 1)[1:2], pltpu.roll(tile, 20, 1)[2:3]),
        )

    returns = []
    for group, slot, out, into, send_sems, recv_sems in (
        (NIGH, target_slot, ret_out, ret_in, ret_send, ret_recv),
        (FAR, far_slot, far_out, far_in, far_send, far_recv),
    ):
        for dx, dy in group:
            there = slot(-dx, -dy)
            copy = pltpu.make_async_remote_copy(
                src_ref=out.at[slot(dx, dy)],
                dst_ref=into.at[there],
                send_sem=send_sems.at[there],
                recv_sem=recv_sems.at[there],
                device_id=device(dx, dy),
                device_id_type=MESH,
            )
            copy.start()
            returns.append(copy)

    for copy in carried:
        copy.wait_recv()
    settle = jnp.broadcast_to(source, (8, LANES))
    mine, low, high = load[1], load[0], load[2]
    held = jnp.where(lane8 < atoms, mine, jnp.where(lane8 < atoms + 5, low, high))
    held = jnp.where(lane8 < LANES - 1, held, 0.0)
    held = pick(held, settle)
    total = ret_out[target_slot(0, 0)]
    for copy in returns:
        copy.wait_recv()
    for dx, dy in NIGH:
        total = total + ret_in[target_slot(dx, dy)]
    far = far_in[0]
    for t in range(1, len(FAR)):
        far = far + far_in[t]
    far = jnp.broadcast_to(far, (8, LANES))
    seats = jnp.logical_and(lane8 >= atoms, lane8 < atoms + 10)
    moved = jnp.where(sub8 == 0, far, jnp.where(sub8 == 1, pltpu.roll(far, LANES - 10, 1), pltpu.roll(far, LANES - 20, 1)))
    total = jnp.concatenate([total, jnp.zeros((4, LANES), F32)], axis=0) + jnp.where(seats, moved, 0.0)
    force = pick(total, settle)[0:3]
    fresh = held[0:3] + 0.5 * TIME_STEP * force * held[6:7]
    for c in range(3):
        both_ref[0, c] = fresh[c : c + 1, 0:atoms]
        both_ref[0, c + 3] = held[c + 3 : c + 4, 0:atoms]
    for copy in sends + carried + returns:
        copy.wait_send()


def on_device(*args):
    atoms = args[0].shape[3]
    slots = args[4].shape[2]
    ch = args[13].shape[0]
    chunks = (atoms // GROUP * (slots // 16) + 7) // 8
    n_gx, n_yz = lax.axis_size("gx"), lax.axis_size("yz")
    period = (n_gx * PX * SPACING, n_yz * PY * SPACING, PZ * SPACING)
    pos, vel, frc, spc, nbr, msk, sx, sy, ms, mr, wb, ec, en, we, wl, wo = args
    pos, vel, frc = (x.transpose(0, 2, 1, 3) for x in (pos, vel, frc))
    nbr, msk = (x.transpose(0, 1, 3, 2) for x in (nbr, msk))
    args = (pos, vel, frc, spc, nbr, msk, sx, sy, ms, mr, wb, ec.T, en.T, we, wl.T, wo.reshape(1, ch))

    def body(*refs):
        kernel_body(period, atoms, slots, *refs)

    vmem = pl.BlockSpec(memory_space=pltpu.VMEM)
    per_block = slots // 16
    blocks = atoms // GROUP
    dma = pltpu.SemaphoreType.DMA
    out = jax.ShapeDtypeStruct((1, 6, 1, atoms), F32)
    staged = tuple(
        (pltpu.SMEM if at in (8, 9) else pltpu.VMEM)(x.shape, x.dtype) for at, x in enumerate(args)
    )
    both = pl.pallas_call(
        body,
        out_shape=out,
        in_specs=[pl.BlockSpec(memory_space=pl.ANY)] * 16,
        out_specs=vmem,
        scratch_shapes=[
            staged,
            pltpu.VMEM((9, 8, LANES), F32),
            pltpu.VMEM((8, LANES), F32),
            pltpu.VMEM((3, 8, LANES), F32),
            pltpu.VMEM((15, 4, LANES), F32),
            pltpu.VMEM((15, 4, LANES), F32),
            pltpu.VMEM((6, 1, LANES), F32),
            pltpu.VMEM((6, 1, LANES), F32),
            pltpu.VMEM((atoms, LANES), F32),
            pltpu.VMEM((chunks * 8, LANES), F32),
            pltpu.VMEM((4, 8, LANES), F32),
            pltpu.VMEM((13, chunks, 8, LANES), F32),
            pltpu.VMEM((chunks * 128, LANES), F32),
            pltpu.VMEM((chunks * 128, LANES), F32),
            pltpu.VMEM((chunks * 192, LANES), F32),
            pltpu.VMEM((chunks * 64 + 64, LANES), F32),
            pltpu.VMEM((atoms // GROUP, ch, LANES), F32),
            pltpu.VMEM((2, 3, 3 * ch, ch), BF16),
            pltpu.VMEM((ch, 16), BF16),
            pltpu.VMEM((ch, LANES), F32),
            pltpu.VMEM((2, ch, LANES), F32),
            pltpu.VMEM((blocks, 10 * GROUP + 2 * ch, per_block * LANES), BF16),
            pltpu.VMEM((blocks * per_block, ch, LANES), F32),
            pltpu.VMEM((blocks * per_block, ch, LANES), F32),
            pltpu.VMEM((blocks * per_block, ch, LANES), F32),
            pltpu.VMEM((blocks, 2 * ch + 8 * GROUP, per_block * LANES), BF16),
            pltpu.VMEM((3, 64, LANES), F32),
            pltpu.VMEM((2, chunks, 8, LANES), I32),
            pltpu.VMEM((8, chunks, 8, LANES), F32),
            dma((16,)),
            dma((9,)),
            dma((9,)),
            dma((3,)),
            dma((3,)),
            dma((15,)),
            dma((15,)),
            dma((6,)),
            dma((6,)),
        ],
        compiler_params=pltpu.CompilerParams(
            collective_id=0, has_side_effects=True, vmem_limit_bytes=60 * 1024 * 1024
        ),
    )(*args)
    return both[:, 0:3].transpose(0, 2, 1, 3), both[:, 3:6].transpose(0, 2, 1, 3)


def solution(mesh):
    block4 = P("gx", "yz", None, None)
    block3 = P("gx", "yz", None)
    return jax.shard_map(
        on_device,
        mesh=mesh,
        in_specs=(block4, block4, block4, block3) + (block4,) * 6 + (P(),) * 6,
        out_specs=(block4, block4),
        check_vma=False,
    )
```

```python
import jax
import jax.numpy as jnp
from jax import lax
from jax.experimental import pallas as pl
from jax.experimental.pallas import tpu as pltpu
from jax.sharding import PartitionSpec as P

PX = 4
PY = 4
PZ = 5
STEPS = 1
SPACING = 2.15
CUTOFF = 6.0
TIME_STEP = 0.05
ENV_SCALE = 0.125
MASSES = (1.008, 12.011, 14.007, 15.999, 32.06)
HIGHEST = lax.Precision.HIGHEST
MESH = pl.DeviceIdType.MESH
F32 = jnp.float32
BF16 = jnp.bfloat16
I32 = jnp.int32

LANES = 128
GROUP = 8
PI = 3.141592653589793
R3 = 3.0**0.5
R5 = 5.0**0.5
R15 = 15.0**0.5

HALO = [(dx, dy) for dy in (-1, 0, 1) for dx in (-1, 0, 1)]
NEAR = sorted((pos for pos in HALO if pos != (0, 0)), key=lambda pos: -abs(pos[0]) - 2 * abs(pos[1]))
TARGETS = [(dx, dy) for dy in (-1, 0, 1) for dx in (-2, -1, 0, 1, 2)]
REST = sorted((pos for pos in TARGETS if pos != (0, 0)), key=lambda pos: -(abs(pos[0]) % 2) - 2 * abs(pos[1]))


FAR = [pos for pos in REST if abs(pos[0]) == 2]
NIGH = [pos for pos in REST if abs(pos[0]) < 2]
DROPPED = 127
EMPTY = 95


def far_slot(dx, dy):
    return (dy + 1) * 2 + (dx + 2) // 4


def halo_slot(dx, dy):
    return (dy + 1) * 3 + dx + 1


def target_slot(dx, dy):
    return (dy + 1) * 5 + dx + 2


def nt_dot(a, b, precision=None):
    return lax.dot_general(
        a, b, (((1,), (1,)), ((), ())), precision=precision, preferred_element_type=F32
    )


def nn_dot(a, b, precision=None):
    return jnp.dot(a, b, precision=precision, preferred_element_type=F32)


def halves(x):
    high = x.astype(BF16)
    low = (x - high.astype(F32)).astype(BF16)
    return high, low


def pick(rows, index):
    return jnp.take_along_axis(rows, index, axis=1, mode="promise_in_bounds")


def turn(eye, x):
    high, low = halves(x)
    return nt_dot(eye, high) + nt_dot(eye, low)


def split_dot(left, right):
    high, low = halves(left)
    return nn_dot(high, right) + nn_dot(low, right)


def sigmoid(x):
    return 0.5 * jnp.tanh(0.5 * x) + 0.5


def kernel_body(
    period,
    atoms,
    slots,
    *refs,
):
    raw, refs = refs[:16], refs[16:]
    (
        both_ref,
        staged,
        halo,
        edge,
        load,
        ret_out,
        ret_in,
        far_out,
        far_in,
        nb_pad,
        rows_code,
        table,
        sc,
        zf,
        zy,
        zd,
        pt,
        cterm,
        mats,
        w1s,
        wcol,
        w0pad,
        rhs,
        s1_s,
        ds_s,
        hid_s,
        dpt_s,
        g3,
        spot,
        early,
        load_sems,
        halo_send,
        halo_recv,
        load_send,
        load_recv,
        ret_send,
        ret_recv,
        far_send,
        far_recv,
    ) = refs
    gx = lax.axis_index("gx")
    yz = lax.axis_index("yz")
    n_gx = lax.axis_size("gx")
    n_yz = lax.axis_size("yz")
    blocks = atoms // GROUP
    per_block = slots // 16
    n_rows = blocks * per_block
    chunks = (n_rows + 7) // 8

    def device(dx, dy):
        return (lax.rem(gx + dx + n_gx, n_gx), lax.rem(yz + dy + n_yz, n_yz))

    barrier = pltpu.get_barrier_semaphore()
    loads = []
    first = (0, 1, 2, 3, 6, 7, 8, 9)
    for at, (far, close) in enumerate(zip(raw, staged)):
        loads.append(pltpu.make_async_copy(far, close, load_sems.at[at]))
    for dx, dy in NEAR:
        pl.semaphore_signal(barrier, inc=1, device_id=device(dx, dy), device_id_type=MESH)

    for at in first:
        loads[at].start()
    for at in range(16):
        if at not in first:
            loads[at].start()
    (
        pos_ref,
        vel_ref,
        frc_ref,
        spc_ref,
        nbr_ref,
        msk_ref,
        sx_ref,
        sy_ref,
        ms_ref,
        mr_ref,
        wb_ref,
        ec_ref,
        en_ref,
        we_ref,
        wl_ref,
        wo_ref,
    ) = staged
    for at in first:
        loads[at].wait()

    lane1 = lax.broadcasted_iota(I32, (1, LANES), 1)
    lane8 = lax.broadcasted_iota(I32, (8, LANES), 1)
    sub8 = lax.broadcasted_iota(I32, (8, LANES), 0)

    own = halo_slot(0, 0)
    kinds = spc_ref[0].astype(F32)
    minv = jnp.zeros_like(kinds)
    for kind, mass in enumerate(MASSES):
        minv = jnp.where(kinds == float(kind), 1.0 / jnp.float32(mass), minv)
    halo[own] = jnp.zeros((8, LANES), F32)
    load[1] = jnp.zeros((8, LANES), F32)
    for c in range(3):
        start = pos_ref[0, c]
        velocity = vel_ref[0, c] + 0.5 * TIME_STEP * frc_ref[0, c] * minv
        coords = start + TIME_STEP * velocity
        halo[own, c : c + 1, 0:atoms] = coords
        load[1, c : c + 1, 0:atoms] = velocity
        load[1, c + 3 : c + 4, 0:atoms] = (coords - start) / (STEPS * TIME_STEP)
    halo[own, 3:4, 0:atoms] = kinds
    code = lane1
    place = lane1
    source = lane1
    for side in (0, 1):
        for k in range(ms_ref.shape[3]):
            seat = atoms + 5 * (1 - side) + k
            code = jnp.where(lane1 == mr_ref[0, 0, side, k], DROPPED, code)
    for side in (0, 1):
        for k in range(ms_ref.shape[3]):
            seat = atoms + 5 * (1 - side) + k
            gone = ms_ref[0, 0, side, k]
            code = jnp.where(lane1 == gone, (2 * side - 1) * LANES + seat, code)
            place = jnp.where(lane1 == seat, gone, place)
            source = jnp.where(lane1 == gone, EMPTY, source)
    for side in (0, 1):
        for k in range(ms_ref.shape[3]):
            source = jnp.where(lane1 == mr_ref[0, 0, side, k], atoms + 5 * side + k, source)
    code = jnp.where(lane1 < atoms, code + LANES, 0)
    halo[own, 4:5, :] = code.astype(F32)
    halo[own, 6:8, 0:atoms] = sy_ref[0, 0].astype(F32)
    load[1, 6:7, 0:atoms] = minv
    width_x = sx_ref.shape[3]
    g3[0] = jnp.zeros((64, LANES), F32)
    g3[0, 0:2, 0:width_x] = sx_ref[0, 0].astype(F32)
    lists = g3[0, 0:8, :]
    outward = lists[1:2] + pltpu.roll(lists, width_x, 1)[0:1]
    edge[...] = pick(halo[own], jnp.broadcast_to(outward, (8, LANES)).astype(I32))
    load[1] = pick(load[1], jnp.broadcast_to(place, (8, LANES)))

    pl.semaphore_wait(barrier, len(NEAR))
    sends, carried = [], []
    for dx, dy in NEAR:
        there = halo_slot(-dx, -dy)
        copy = pltpu.make_async_remote_copy(
            src_ref=edge if dx else halo.at[own],
            dst_ref=halo.at[there],
            send_sem=halo_send.at[there],
            recv_sem=halo_recv.at[there],
            device_id=device(dx, dy),
            device_id_type=MESH,
        )
        copy.start()
        sends.append(copy)
    for dx in (-1, 1):
        there = 1 - dx
        copy = pltpu.make_async_remote_copy(
            src_ref=load.at[1],
            dst_ref=load.at[there],
            send_sem=load_send.at[there],
            recv_sem=load_recv.at[there],
            device_id=device(dx, 0),
            device_id_type=MESH,
        )
        copy.start()
        carried.append(copy)

    for t in range(len(TARGETS)):
        ret_out[t] = jnp.zeros((4, LANES), F32)

    for at in range(16):
        if at not in first:
            loads[at].wait()
    nb_pad[...] = jnp.zeros((atoms, LANES), F32)
    nb_pad[:, 0:slots] = nbr_ref[0, 0].astype(F32) + 512.0 * msk_ref[0, 0].astype(F32)
    rows_code[...] = jnp.zeros((chunks * 8, LANES), F32)
    in_row = (lane8 & (GROUP - 1)) == sub8
    for block in range(blocks):
        group = nb_pad[block * GROUP : (block + 1) * GROUP, :]
        for jb in range(per_block):
            moved = pick(group, (lane8 >> 3) + jb * 16)
            row = jnp.sum(jnp.where(in_row, moved, 0.0), axis=0, keepdims=True)
            r = block * per_block + jb
            rows_code[r : r + 1, :] = row

    ch = we_ref.shape[0]
    eye = (
        lax.broadcasted_iota(I32, (ch, ch), 0) == lax.broadcasted_iota(I32, (ch, ch), 1)
    ).astype(F32)
    n_basis = wb_ref.shape[0]
    n_kinds = en_ref.shape[0]
    wl_t = wl_ref[...]
    mixes = []
    eye16 = eye.astype(BF16)
    we_h, we_l = halves(we_ref[...])
    for part in range(3):
        part_t = wl_t[:, (part + 1) * ch : (part + 2) * ch]
        part_h, part_l = halves(part_t)
        mixes.append(ENV_SCALE * (nt_dot(part_h, we_h) + nt_dot(part_l, we_h) + nt_dot(part_h, we_l)))
    for part in range(3):
        turned = mixes[part]
        straight = turn(eye16, turned)
        for which, m in enumerate((straight, turned)):
            m_high, m_low = halves(m)
            mats[which, part] = jnp.concatenate([m_high, m_high, m_low], axis=0)
    w0_t = wl_t[:, 0:ch]
    w0 = turn(eye16, w0_t)
    ec = turn(eye16, ec_ref[...])
    w0pad[...] = jnp.zeros((2, ch, LANES), F32)
    w0pad[0, :, 80 : 80 + ch] = w0_t
    w0pad[1, :, 80 : 80 + ch] = w0
    w1f = jnp.concatenate(
        [
            nt_dot(eye16, wb_ref[...].astype(BF16)),
            nt_dot(eye16, en_ref[...].astype(BF16)),
            jnp.zeros((ch, 16 - n_basis - n_kinds), F32),
        ],
        axis=1,
    )
    w1s[...] = w1f.astype(BF16)
    row32 = lax.broadcasted_iota(I32, (32, LANES), 0)
    lane32 = lax.broadcasted_iota(I32, (32, LANES), 1)
    g3[1, 0:32, :] = jnp.zeros((32, LANES), F32)
    g3[1, 0:n_basis, 0:ch] = wb_ref[...]
    head = g3[1, 0:32, :] + jnp.where(
        (row32 == 8) & (lane32 >= ch) & (lane32 < 2 * ch), 1.0, 0.0
    ) + jnp.where((lane32 >= 2 * ch) & (row32 == 16 + ((lane32 - 2 * ch) >> 3)), 1.0, 0.0)
    w_last = head
    wcol[...] = jnp.broadcast_to(
        jnp.sum(jnp.where(eye > 0, wo_ref[...], 0.0), axis=1, keepdims=True), (ch, LANES)
    )

    def shifted(dx, dy):
        step = float(LANES * ((dy + 1) * 5 + dx + 1))
        return halo[halo_slot(dx, dy)] + jnp.where(sub8 == 4, step, 0.0)

    def whole(k, c):
        return jnp.broadcast_to(table[k, c : c + 1, :], (8, LANES))

    table[0] = shifted(0, 0)
    for i in range(chunks):
        word = rows_code[i * 8 : i * 8 + 8, :]
        n = jnp.where(word >= 512.0, word - 512.0, word).astype(I32)
        k = jnp.where(n >= atoms, 1, 0) + jnp.where(n >= 2 * atoms, 1, 0) + jnp.where(n >= 3 * atoms, 1, 0)
        n = n - atoms * k
        spot[0, i] = n
        spot[1, i] = k
        for c in range(5):
            early[c, i] = pick(whole(0, c), n)
        row = i * 8 + sub8
        block = jnp.zeros((8, LANES), I32)
        for b in range(1, blocks):
            block = block + jnp.where(row >= b * per_block, 1, 0)
        centre = block * GROUP + (lane8 & (GROUP - 1))
        for c in range(3):
            early[5 + c, i] = pick(whole(0, c), centre)

    kind_rows = jnp.broadcast_to(halo[own, 3:4, :], (8, LANES))
    for block in range(blocks):
        spread = (lane8 & (GROUP - 1)) + block * GROUP
        kind_row = jnp.broadcast_to(pick(kind_rows, spread)[0:1], (ch, LANES))
        term = jnp.zeros((ch, LANES), F32)
        for kind in range(n_kinds):
            term = jnp.where(
                kind_row == float(kind),
                jnp.broadcast_to(ec[:, kind : kind + 1], (ch, LANES)),
                term,
            )
        cterm[block] = term

    for copy in sends:
        copy.wait_recv()

    def row_index(rows, which):
        return jnp.broadcast_to(rows[which : which + 1, :], (8, LANES)).astype(I32)

    def x_ghosts(dy):
        return jnp.where(lane8 < width_x, shifted(-1, dy), shifted(1, dy))

    def y_ghosts(dy):
        base = shifted(0, dy)
        index = row_index(base, 7 if dy < 0 else 6)
        outer = index >= atoms
        return jnp.where(
            outer,
            pick(x_ghosts(dy), jnp.where(outer, index - atoms, 0)),
            pick(base, jnp.where(outer, 0, index)),
        )

    table[1] = x_ghosts(0)
    table[2] = y_ghosts(-1)
    table[3] = y_ghosts(1)

    def forward_chunk(i, carry):
        word = rows_code[pl.ds(i * 8, 8), :]
        live = word >= 512.0
        n, k = spot[0, i], spot[1, i]
        near = []
        for c in range(5):
            v = early[c, i]
            for part in (1, 2, 3):
                v = jnp.where(k == part, pick(whole(part, c), n), v)
            near.append(v)
        off = []
        for c in range(3):
            d = near[c] - early[5 + c, i]
            d = d - period[c] * jnp.floor(d / period[c] + 0.5)
            off.append(jnp.where(live, d, SPACING if c == 0 else 0.0))
        radius = jnp.sqrt(off[0] * off[0] + off[1] * off[1] + off[2] * off[2])
        rinv = 1.0 / radius
        ux, uy, uz = (o * rinv for o in off)
        q = radius / CUTOFF
        valid = jnp.logical_and(live, q < 1.0)
        q2 = q * q
        q5 = q2 * q2 * q
        q6 = q5 * q
        env = jnp.where(valid, 1.0 + q6 * (-28.0 + q * (48.0 - 21.0 * q)), 0.0)
        denv = jnp.where(valid, (168.0 / CUTOFF) * q5 * (-1.0 + q * (2.0 - q)), 0.0)
        u = PI * jnp.minimum(q, 1.0) - 0.5 * PI
        w = u * u
        sin1 = 1.0 + w * (-1 / 2 + w * (1 / 24 + w * (-1 / 720 + w * (1 / 40320 + w * (-1 / 3628800 + w * (1 / 479001600))))))
        cos1 = -u * (1.0 + w * (-1 / 6 + w * (1 / 120 + w * (-1 / 5040 + w * (1 / 362880 + w * (-1 / 39916800 + w * (1 / 6227020800)))))))
        sc[0, i] = ux
        sc[1, i] = uy
        sc[2, i] = uz
        sc[3, i] = rinv
        sc[4, i] = denv
        zbase = i * 128
        scale = (2.0 / CUTOFF) ** 0.5 * rinv
        s_prev, s_now = jnp.zeros_like(sin1), sin1
        c_prev, c_now = jnp.ones_like(cos1), cos1
        for order in range(1, n_basis + 1):
            bes = scale * s_now
            zf[pl.ds(zbase + order - 1, 8, stride=16), :] = bes
            sc[4 + order, i] = scale * (order * PI / CUTOFF) * c_now - bes * rinv
            s_prev, s_now = s_now, 2.0 * cos1 * s_now - s_prev
            c_prev, c_now = c_now, 2.0 * cos1 * c_now - c_prev
        for kind in range(n_kinds):
            zf[pl.ds(zbase + n_basis + kind, 8, stride=16), :] = jnp.where(near[3] == float(kind), 1.0, 0.0)
        for extra in range(n_basis + n_kinds, 16):
            zf[pl.ds(zbase + extra, 8, stride=16), :] = jnp.zeros((8, LANES), F32)
        ys = (
            R3 * ux,
            R3 * uy,
            R3 * uz,
            R15 * ux * uy,
            R15 * uy * uz,
            0.5 * R5 * (3.0 * uz * uz - 1.0),
            R15 * ux * uz,
            0.5 * R15 * (ux * ux - uy * uy),
        )
        for m, y in enumerate(ys):
            zy[pl.ds(zbase + m, 8, stride=16), :] = y
        zy[pl.ds(zbase + 8, 8, stride=16), :] = env
        dest = near[4].astype(I32)
        tbase = i * 64
        pt[pl.ds(tbase + 6, 8, stride=8), :] = (dest >> 7).astype(F32)
        pt[pl.ds(tbase + 7, 8, stride=8), :] = (dest & (LANES - 1)).astype(F32)
        return carry

    for i in range(chunks):
        forward_chunk(i, 0)

    n_harm = 8
    wide = n_harm * GROUP
    own_lane = (lane8 & (GROUP - 1)) == sub8
    every = jnp.concatenate([jnp.where(own_lane, 1.0, 0.0)] * n_harm, axis=0).astype(BF16)
    ones_row = jnp.concatenate([jnp.where(own_lane, 1.0, 0.0), jnp.zeros((8, LANES), F32)], axis=0).astype(BF16)
    at_ef = wide + 2 * GROUP
    at_dlp = at_ef + ch

    degree_rows = ((1, 0, 3 * GROUP), (2, 3 * GROUP, wide), (0, wide, wide + 2 * GROUP))

    def by_degree(which, sums):
        parts = []
        for degree, a, b in degree_rows:
            grown = exact_dot(jnp.concatenate([x[a:b] for x in sums], axis=0), which, degree)
            parts.append([grown[t * (b - a) : (t + 1) * (b - a)] for t in range(len(sums))])
        return [jnp.concatenate([p[t] for p in parts], axis=0) for t in range(len(sums))]

    def exact_dot(rows, which, degree):
        high = rows.astype(BF16).astype(F32)
        joined = jnp.concatenate([high, rows - high, high], axis=1).astype(BF16)
        return nn_dot(joined, mats[which, degree])

    def as_left(turned, pad):
        tall_one = jnp.concatenate([turned, jnp.zeros((LANES - at_ef, ch), F32)], axis=0)
        return (tall_one.T + pad)[:, 0:at_dlp]

    w_out = wcol[...]
    kept = {}

    def env_row(row):
        return zy[row * 16 + 8 : row * 16 + 9, :]

    def stage_pre(b):
        base = b * per_block
        feats = jnp.concatenate(
            [zf[(base + jb) * 16 : (base + jb + 1) * 16, :] for jb in range(per_block)], axis=1
        )
        kept["pre", b] = nn_dot(w1s[...], feats.astype(BF16))

    def stage_feat(b):
        centre_term = cterm[b]
        pre = kept.pop(("pre", b))
        for jb in range(per_block):
            row = b * per_block + jb
            cols = slice(jb * LANES, (jb + 1) * LANES)
            z = zy[row * 16 : row * 16 + 16, :]
            env = z[8:9]
            p = pre[:, cols] + centre_term
            sig = sigmoid(p)
            s1 = p * sig
            s1_s[row] = s1
            ds_s[row] = (sig + s1 * (1.0 - sig)) * env
            rhs[b, at_ef : at_ef + ch, cols] = (s1 * env).astype(BF16)
            for m in range(0, n_harm, 2):
                two = [jnp.where(own_lane, z[t : t + 1], 0.0) for t in (m, m + 1)]
                rhs[b, m * GROUP : (m + 2) * GROUP, cols] = jnp.concatenate(two, axis=0).astype(BF16)
            rhs[b, wide : wide + 2 * GROUP, cols] = ones_row

    def stage_env(b):
        kept["f", b] = nt_dot(rhs[b, 0:at_ef, :], rhs[b, at_ef : at_ef + ch, :])

    def stage_grow(b):
        half = blocks // 2
        if b % half == 0:
            grown = by_degree(0, [kept.pop(("f", t)) for t in range(b, b + half)])
            for t in range(half):
                kept["g", b + t] = grown[t]

    def stage_lp(b):
        left = as_left(kept["g", b], w0pad[0])
        kept["lp", b] = split_dot(left, rhs[b, 0:at_dlp, :])

    def stage_latent(b):
        lp_all = kept.pop(("lp", b))
        for jb in range(per_block):
            row = b * per_block + jb
            cols = slice(jb * LANES, (jb + 1) * LANES)
            env = env_row(row)
            lp = lp_all[:, cols]
            sig = sigmoid(lp)
            lat = lp * sig
            hid_s[row] = w_out * (s1_s[row] * env + lat)
            dlp = (w_out * env) * (sig + lat * (1.0 - sig))
            rhs[b, at_dlp : at_dlp + ch, cols] = dlp.astype(BF16)

    def stage_back(b):
        kept["f", b] = nt_dot(rhs[b, 0:at_ef, :], rhs[b, at_dlp : at_dlp + ch, :])

    def stage_shrink(b):
        half = blocks // 2
        if b % half == 0:
            grown = by_degree(1, [kept.pop(("f", t)) for t in range(b, b + half)])
            for t in range(half):
                kept["d", b + t] = grown[t]

    def stage_de(b):
        grown = kept.pop(("d", b))
        left = as_left(grown, w0pad[1])
        kept["de", b] = split_dot(left, jnp.concatenate([rhs[b, 0:at_ef, :], rhs[b, at_dlp : at_dlp + ch, :]], axis=0))
        both = jnp.concatenate([grown[0:wide], kept.pop(("g", b))[0:wide]], axis=1)
        kept["dy", b] = nn_dot(both.astype(BF16), rhs[b, at_ef : at_dlp + ch, :])

    def stage_edge(b):
        de_all = kept.pop(("de", b))
        dy_all = kept.pop(("dy", b))
        for jb in range(per_block):
            row = b * per_block + jb
            cols = slice(jb * LANES, (jb + 1) * LANES)
            de = de_all[:, cols] + w_out * env_row(row)
            dpt_s[b, 0:ch, cols] = (de * ds_s[row]).astype(BF16)
            dpt_s[b, ch : 2 * ch, cols] = (hid_s[row] + de * s1_s[row]).astype(BF16)
            dpt_s[b, 2 * ch :, cols] = dy_all[:, cols].astype(BF16) * every

    def stage_fold(b):
        got = split_dot(w_last, dpt_s[b])
        for jb in range(per_block):
            row = b * per_block + jb
            zd[row * 24 : row * 24 + 24, :] = got[0:24, jb * LANES : (jb + 1) * LANES]

    stages = (
        stage_pre,
        stage_feat,
        stage_env,
        stage_grow,
        stage_lp,
        stage_latent,
        stage_back,
        stage_shrink,
        stage_de,
        stage_edge,
        stage_fold,
    )
    teams = (range(0, blocks // 2), range(blocks // 2, blocks))
    for tick in range(len(stages) + 3):
        for late, team in enumerate(teams):
            if 0 <= tick - 3 * late < len(stages):
                for b in team:
                    stages[tick - 3 * late](b)
    for row in range(n_rows, chunks * 8):
        zd[row * 24 : row * 24 + 24, :] = jnp.zeros((24, LANES), F32)

    def put_parts(store, values):
        for c in range(3):
            high = values[c].astype(BF16).astype(F32)
            store(c, high)
            store(c + 3, values[c] - high)

    def backward_chunk(i, carry):
        zbase = i * 192

        def d(which):
            return zd[pl.ds(zbase + which, 8, stride=24), :]

        ux, uy, uz, rinv, denv = (sc[t, i] for t in range(5))
        dr = d(8) * denv
        for order in range(n_basis):
            dr = dr + d(order) * sc[5 + order, i]
        d1, d2, d3, d4, d5, d6, d7, d8 = (d(16 + m) for m in range(8))
        dux = R3 * d1 + R15 * (uy * d4 + uz * d7 + ux * d8)
        duy = R3 * d2 + R15 * (ux * d4 + uz * d5 - uy * d8)
        duz = R3 * d3 + R15 * (uy * d5 + ux * d7) + (3.0 * R5) * uz * d6
        radial = dr - rinv * (dux * ux + duy * uy + duz * uz)
        forces = [-(radial * u + rinv * du) for u, du in ((ux, dux), (uy, duy), (uz, duz))]
        at = pl.ds(i * 8, 8)
        for c in range(3):
            g3[c, at, :] = forces[c]

        def store(which, value):
            pt[pl.ds(i * 64 + which, 8, stride=8), :] = value

        put_parts(store, forces)
        return carry

    for i in range(chunks):
        backward_chunk(i, 0)

    halfway = blocks // 2
    pt[chunks * 64 :, :] = jnp.zeros((64, LANES), F32)
    sums = []
    for c in range(3):
        rows = jnp.concatenate(
            [
                jnp.sum(g3[c, b * per_block : (b + 1) * per_block, :], axis=0, keepdims=True)
                for b in range(blocks)
            ],
            axis=0,
        )
        rows = -(rows + pltpu.roll(rows, LANES // 2, 1))
        sums.append(jnp.where(lane1 < LANES // 2, rows[0:halfway], rows[halfway:]))
    for b in range(halfway):
        at = (n_rows + b) * 8

        def store(which, value):
            pt[at + which : at + which + 1, :] = value[b : b + 1]

        put_parts(store, sums)
        spread = (lane8 & (GROUP - 1)) + jnp.where(lane8 < LANES // 2, b, b + halfway) * GROUP
        dest = pick(whole(0, 4), spread)[0:1].astype(I32)
        pt[at + 6 : at + 7, :] = (dest >> 7).astype(F32)
        pt[at + 7 : at + 8, :] = (dest & (LANES - 1)).astype(F32)

    n_targets = len(TARGETS)
    tall = 96
    sub16 = lax.broadcasted_iota(I32, (16, LANES), 0)
    pair = jnp.where(sub16 >= 8, 1.0, 0.0)
    pairs = [(pair + 2.0 * b).astype(BF16) for b in range((n_targets + 1) // 2)]
    steps = [(sub16 + 16 * b).astype(F32).astype(BF16) for b in range(tall // 16)]
    zero16 = jnp.zeros((16, LANES), BF16)
    one16 = jnp.ones((16, LANES), BF16)

    spread_out = None
    rows_left = n_rows + halfway + (n_rows + halfway) % 2
    for first_row in range(0, rows_left, 8):
        lefts, rights = [], []
        for row in range(first_row, min(first_row + 8, rows_left)):
            v = pt[row * 8 : row * 8 + 8, :]
            where_to = jnp.broadcast_to(v[6:7], (16, LANES)).astype(BF16)
            lo = jnp.broadcast_to(v[7:8], (16, LANES)).astype(BF16)
            twice = jnp.concatenate([v, v], axis=0).astype(BF16)
            lefts.append(jnp.concatenate([jnp.where(where_to == p, twice, zero16) for p in pairs], axis=0))
            rights.append(jnp.concatenate([jnp.where(lo == p, one16, zero16) for p in steps], axis=0))
        part = nt_dot(jnp.concatenate(lefts, axis=1), jnp.concatenate(rights, axis=1))
        spread_out = part if spread_out is None else spread_out + part
    for t in range(n_targets):
        tile = spread_out[t * 8 : t * 8 + 8, :]
        ret_out[t, 0:3, 0:tall] = tile[0:3] + tile[3:6]
    for dx, dy in FAR:
        tile = jnp.concatenate([ret_out[target_slot(dx, dy)], jnp.zeros((4, LANES), F32)], axis=0)
        far_out[far_slot(dx, dy)] = jnp.where(
            lane1 < atoms + 10,
            tile[0:1],
            jnp.where(lane1 < atoms + 20, pltpu.roll(tile, 10, 1)[1:2], pltpu.roll(tile, 20, 1)[2:3]),
        )

    returns = []
    for group, slot, out, into, send_sems, recv_sems in (
        (NIGH, target_slot, ret_out, ret_in, ret_send, ret_recv),
        (FAR, far_slot, far_out, far_in, far_send, far_recv),
    ):
        for dx, dy in group:
            there = slot(-dx, -dy)
            copy = pltpu.make_async_remote_copy(
                src_ref=out.at[slot(dx, dy)],
                dst_ref=into.at[there],
                send_sem=send_sems.at[there],
                recv_sem=recv_sems.at[there],
                device_id=device(dx, dy),
                device_id_type=MESH,
            )
            copy.start()
            returns.append(copy)

    for copy in carried:
        copy.wait_recv()
    settle = jnp.broadcast_to(source, (8, LANES))
    mine, low, high = load[1], load[0], load[2]
    held = jnp.where(lane8 < atoms, mine, jnp.where(lane8 < atoms + 5, low, high))
    held = jnp.where(lane8 < LANES - 1, held, 0.0)
    held = pick(held, settle)
    total = ret_out[target_slot(0, 0)]
    for copy in returns:
        copy.wait_recv()
    for dx, dy in NIGH:
        total = total + ret_in[target_slot(dx, dy)]
    far = far_in[0]
    for t in range(1, len(FAR)):
        far = far + far_in[t]
    far = jnp.broadcast_to(far, (8, LANES))
    seats = jnp.logical_and(lane8 >= atoms, lane8 < atoms + 10)
    moved = jnp.where(sub8 == 0, far, jnp.where(sub8 == 1, pltpu.roll(far, LANES - 10, 1), pltpu.roll(far, LANES - 20, 1)))
    total = jnp.concatenate([total, jnp.zeros((4, LANES), F32)], axis=0) + jnp.where(seats, moved, 0.0)
    force = pick(total, settle)[0:3]
    fresh = held[0:3] + 0.5 * TIME_STEP * force * held[6:7]
    for c in range(3):
        both_ref[0, c] = fresh[c : c + 1, 0:atoms]
        both_ref[0, c + 3] = held[c + 3 : c + 4, 0:atoms]
    for copy in sends + carried + returns:
        copy.wait_send()


def on_device(*args):
    atoms = args[0].shape[3]
    slots = args[4].shape[2]
    ch = args[13].shape[0]
    chunks = (atoms // GROUP * (slots // 16) + 7) // 8
    n_gx, n_yz = lax.axis_size("gx"), lax.axis_size("yz")
    period = (n_gx * PX * SPACING, n_yz * PY * SPACING, PZ * SPACING)
    pos, vel, frc, spc, nbr, msk, sx, sy, ms, mr, wb, ec, en, we, wl, wo = args
    pos, vel, frc = (x.transpose(0, 2, 1, 3) for x in (pos, vel, frc))
    nbr, msk = (x.transpose(0, 1, 3, 2) for x in (nbr, msk))
    args = (pos, vel, frc, spc, nbr, msk, sx, sy, ms, mr, wb, ec.T, en.T, we, wl.T, wo.reshape(1, ch))

    def body(*refs):
        kernel_body(period, atoms, slots, *refs)

    vmem = pl.BlockSpec(memory_space=pltpu.VMEM)
    per_block = slots // 16
    blocks = atoms // GROUP
    dma = pltpu.SemaphoreType.DMA
    out = jax.ShapeDtypeStruct((1, 6, 1, atoms), F32)
    staged = tuple(
        (pltpu.SMEM if at in (8, 9) else pltpu.VMEM)(x.shape, x.dtype) for at, x in enumerate(args)
    )
    both = pl.pallas_call(
        body,
        out_shape=out,
        in_specs=[pl.BlockSpec(memory_space=pl.ANY)] * 16,
        out_specs=vmem,
        scratch_shapes=[
            staged,
            pltpu.VMEM((9, 8, LANES), F32),
            pltpu.VMEM((8, LANES), F32),
            pltpu.VMEM((3, 8, LANES), F32),
            pltpu.VMEM((15, 4, LANES), F32),
            pltpu.VMEM((15, 4, LANES), F32),
            pltpu.VMEM((6, 1, LANES), F32),
            pltpu.VMEM((6, 1, LANES), F32),
            pltpu.VMEM((atoms, LANES), F32),
            pltpu.VMEM((chunks * 8, LANES), F32),
            pltpu.VMEM((4, 8, LANES), F32),
            pltpu.VMEM((13, chunks, 8, LANES), F32),
            pltpu.VMEM((chunks * 128, LANES), F32),
            pltpu.VMEM((chunks * 128, LANES), F32),
            pltpu.VMEM((chunks * 192, LANES), F32),
            pltpu.VMEM((chunks * 64 + 64, LANES), F32),
            pltpu.VMEM((atoms // GROUP, ch, LANES), F32),
            pltpu.VMEM((2, 3, 3 * ch, ch), BF16),
            pltpu.VMEM((ch, 16), BF16),
            pltpu.VMEM((ch, LANES), F32),
            pltpu.VMEM((2, ch, LANES), F32),
            pltpu.VMEM((blocks, 10 * GROUP + 2 * ch, per_block * LANES), BF16),
            pltpu.VMEM((blocks * per_block, ch, LANES), F32),
            pltpu.VMEM((blocks * per_block, ch, LANES), F32),
            pltpu.VMEM((blocks * per_block, ch, LANES), F32),
            pltpu.VMEM((blocks, 2 * ch + 8 * GROUP, per_block * LANES), BF16),
            pltpu.VMEM((3, 64, LANES), F32),
            pltpu.VMEM((2, chunks, 8, LANES), I32),
            pltpu.VMEM((8, chunks, 8, LANES), F32),
            dma((16,)),
            dma((9,)),
            dma((9,)),
            dma((3,)),
            dma((3,)),
            dma((15,)),
            dma((15,)),
            dma((6,)),
            dma((6,)),
        ],
        compiler_params=pltpu.CompilerParams(
            collective_id=0, has_side_effects=True, vmem_limit_bytes=60 * 1024 * 1024
        ),
    )(*args)
    return both[:, 0:3].transpose(0, 2, 1, 3), both[:, 3:6].transpose(0, 2, 1, 3)


def solution(mesh):
    block4 = P("gx", "yz", None, None)
    block3 = P("gx", "yz", None)
    return jax.shard_map(
        on_device,
        mesh=mesh,
        in_specs=(block4, block4, block4, block3) + (block4,) * 6 + (P(),) * 6,
        out_specs=(block4, block4),
        check_vma=False,
    )
```

```python
import jax
import jax.numpy as jnp
from jax import lax
from jax.experimental import pallas as pl
from jax.experimental.pallas import tpu as pltpu
from jax.sharding import PartitionSpec as P

PX = 4
PY = 4
PZ = 5
STEPS = 1
SPACING = 2.15
CUTOFF = 6.0
TIME_STEP = 0.05
ENV_SCALE = 0.125
MASSES = (1.008, 12.011, 14.007, 15.999, 32.06)
HIGHEST = lax.Precision.HIGHEST
MESH = pl.DeviceIdType.MESH
F32 = jnp.float32
BF16 = jnp.bfloat16
I32 = jnp.int32

LANES = 128
GROUP = 8
PI = 3.141592653589793
R3 = 3.0**0.5
R5 = 5.0**0.5
R15 = 15.0**0.5

HALO = [(dx, dy) for dy in (-1, 0, 1) for dx in (-1, 0, 1)]
NEAR = sorted((pos for pos in HALO if pos != (0, 0)), key=lambda pos: -abs(pos[0]) - 2 * abs(pos[1]))
TARGETS = [(dx, dy) for dy in (-1, 0, 1) for dx in (-2, -1, 0, 1, 2)]
REST = sorted((pos for pos in TARGETS if pos != (0, 0)), key=lambda pos: -(abs(pos[0]) % 2) - 2 * abs(pos[1]))


FAR = [pos for pos in REST if abs(pos[0]) == 2]
NIGH = [pos for pos in REST if abs(pos[0]) < 2]
DROPPED = 127
EMPTY = 95


def far_slot(dx, dy):
    return (dy + 1) * 2 + (dx + 2) // 4


def halo_slot(dx, dy):
    return (dy + 1) * 3 + dx + 1


def target_slot(dx, dy):
    return (dy + 1) * 5 + dx + 2


def nt_dot(a, b, precision=None):
    return lax.dot_general(
        a, b, (((1,), (1,)), ((), ())), precision=precision, preferred_element_type=F32
    )


def nn_dot(a, b, precision=None):
    return jnp.dot(a, b, precision=precision, preferred_element_type=F32)


def halves(x):
    high = x.astype(BF16)
    low = (x - high.astype(F32)).astype(BF16)
    return high, low


def pick(rows, index):
    return jnp.take_along_axis(rows, index, axis=1, mode="promise_in_bounds")


def turn(eye, x):
    high, low = halves(x)
    return nt_dot(eye, high) + nt_dot(eye, low)


def split_dot(left, right):
    high, low = halves(left)
    return nn_dot(high, right) + nn_dot(low, right)


def sigmoid(x):
    return 0.5 * jnp.tanh(0.5 * x) + 0.5


def kernel_body(
    period,
    atoms,
    slots,
    *refs,
):
    raw, refs = refs[:16], refs[16:]
    (
        both_ref,
        staged,
        halo,
        edge,
        load,
        ret_out,
        ret_in,
        far_out,
        far_in,
        nb_pad,
        rows_code,
        table,
        sc,
        zf,
        zy,
        zd,
        pt,
        cterm,
        mats,
        w1s,
        wcol,
        w0pad,
        rhs,
        s1_s,
        ds_s,
        hid_s,
        dpt_s,
        g3,
        spot,
        early,
        load_sems,
        halo_send,
        halo_recv,
        load_send,
        load_recv,
        ret_send,
        ret_recv,
        far_send,
        far_recv,
    ) = refs
    gx = lax.axis_index("gx")
    yz = lax.axis_index("yz")
    n_gx = lax.axis_size("gx")
    n_yz = lax.axis_size("yz")
    blocks = atoms // GROUP
    per_block = slots // 16
    n_rows = blocks * per_block
    chunks = (n_rows + 7) // 8

    def device(dx, dy):
        return (lax.rem(gx + dx + n_gx, n_gx), lax.rem(yz + dy + n_yz, n_yz))

    barrier = pltpu.get_barrier_semaphore()
    loads = []
    first = (0, 1, 2, 3, 6, 7, 8, 9)
    for at, (far, close) in enumerate(zip(raw, staged)):
        loads.append(pltpu.make_async_copy(far, close, load_sems.at[at]))
    for dx, dy in NEAR:
        pl.semaphore_signal(barrier, inc=1, device_id=device(dx, dy), device_id_type=MESH)

    for at in first:
        loads[at].start()
    for at in range(16):
        if at not in first:
            loads[at].start()
    (
        pos_ref,
        vel_ref,
        frc_ref,
        spc_ref,
        nbr_ref,
        msk_ref,
        sx_ref,
        sy_ref,
        ms_ref,
        mr_ref,
        wb_ref,
        ec_ref,
        en_ref,
        we_ref,
        wl_ref,
        wo_ref,
    ) = staged
    for at in first:
        loads[at].wait()

    lane1 = lax.broadcasted_iota(I32, (1, LANES), 1)
    lane8 = lax.broadcasted_iota(I32, (8, LANES), 1)
    sub8 = lax.broadcasted_iota(I32, (8, LANES), 0)

    own = halo_slot(0, 0)
    kinds = spc_ref[0].astype(F32)
    minv = jnp.zeros_like(kinds)
    for kind, mass in enumerate(MASSES):
        minv = jnp.where(kinds == float(kind), 1.0 / jnp.float32(mass), minv)
    halo[own] = jnp.zeros((8, LANES), F32)
    load[1] = jnp.zeros((8, LANES), F32)
    for c in range(3):
        start = pos_ref[0, c]
        velocity = vel_ref[0, c] + 0.5 * TIME_STEP * frc_ref[0, c] * minv
        coords = start + TIME_STEP * velocity
        halo[own, c : c + 1, 0:atoms] = coords
        load[1, c : c + 1, 0:atoms] = velocity
        load[1, c + 3 : c + 4, 0:atoms] = (coords - start) / (STEPS * TIME_STEP)
    halo[own, 3:4, 0:atoms] = kinds
    code = lane1
    place = lane1
    source = lane1
    for side in (0, 1):
        for k in range(ms_ref.shape[3]):
            seat = atoms + 5 * (1 - side) + k
            code = jnp.where(lane1 == mr_ref[0, 0, side, k], DROPPED, code)
    for side in (0, 1):
        for k in range(ms_ref.shape[3]):
            seat = atoms + 5 * (1 - side) + k
            gone = ms_ref[0, 0, side, k]
            code = jnp.where(lane1 == gone, (2 * side - 1) * LANES + seat, code)
            place = jnp.where(lane1 == seat, gone, place)
            source = jnp.where(lane1 == gone, EMPTY, source)
    for side in (0, 1):
        for k in range(ms_ref.shape[3]):
            source = jnp.where(lane1 == mr_ref[0, 0, side, k], atoms + 5 * side + k, source)
    code = jnp.where(lane1 < atoms, code + LANES, 0)
    halo[own, 4:5, :] = code.astype(F32)
    halo[own, 6:8, 0:atoms] = sy_ref[0, 0].astype(F32)
    load[1, 6:7, 0:atoms] = minv
    width_x = sx_ref.shape[3]
    g3[0] = jnp.zeros((64, LANES), F32)
    g3[0, 0:2, 0:width_x] = sx_ref[0, 0].astype(F32)
    lists = g3[0, 0:8, :]
    outward = lists[1:2] + pltpu.roll(lists, width_x, 1)[0:1]
    edge[...] = pick(halo[own], jnp.broadcast_to(outward, (8, LANES)).astype(I32))
    load[1] = pick(load[1], jnp.broadcast_to(place, (8, LANES)))

    for at in range(16):
        if at not in first:
            loads[at].wait()
    nb_pad[...] = jnp.zeros((atoms, LANES), F32)
    nb_pad[:, 0:slots] = nbr_ref[0, 0].astype(F32) + 512.0 * msk_ref[0, 0].astype(F32)
    rows_code[...] = jnp.zeros((chunks * 8, LANES), F32)
    in_row = (lane8 & (GROUP - 1)) == sub8
    for block in range(blocks):
        group = nb_pad[block * GROUP : (block + 1) * GROUP, :]
        for jb in range(per_block):
            moved = pick(group, (lane8 >> 3) + jb * 16)
            row = jnp.sum(jnp.where(in_row, moved, 0.0), axis=0, keepdims=True)
            r = block * per_block + jb
            rows_code[r : r + 1, :] = row

    ch = we_ref.shape[0]
    eye = (
        lax.broadcasted_iota(I32, (ch, ch), 0) == lax.broadcasted_iota(I32, (ch, ch), 1)
    ).astype(F32)
    n_basis = wb_ref.shape[0]
    n_kinds = en_ref.shape[0]
    wl_t = wl_ref[...]
    mixes = []
    eye16 = eye.astype(BF16)
    we_h, we_l = halves(we_ref[...])
    for part in range(3):
        part_t = wl_t[:, (part + 1) * ch : (part + 2) * ch]
        part_h, part_l = halves(part_t)
        mixes.append(ENV_SCALE * (nt_dot(part_h, we_h) + nt_dot(part_l, we_h) + nt_dot(part_h, we_l)))
    for part in range(3):
        turned = mixes[part]
        straight = turn(eye16, turned)
        for which, m in enumerate((straight, turned)):
            m_high, m_low = halves(m)
            mats[which, part] = jnp.concatenate([m_high, m_high, m_low], axis=0)
    w0_t = wl_t[:, 0:ch]
    w0 = turn(eye16, w0_t)
    ec = turn(eye16, ec_ref[...])
    w0pad[...] = jnp.zeros((2, ch, LANES), F32)
    w0pad[0, :, 80 : 80 + ch] = w0_t
    w0pad[1, :, 80 : 80 + ch] = w0
    w1f = jnp.concatenate(
        [
            nt_dot(eye16, wb_ref[...].astype(BF16)),
            nt_dot(eye16, en_ref[...].astype(BF16)),
            jnp.zeros((ch, 16 - n_basis - n_kinds), F32),
        ],
        axis=1,
    )
    w1s[...] = w1f.astype(BF16)
    row32 = lax.broadcasted_iota(I32, (32, LANES), 0)
    lane32 = lax.broadcasted_iota(I32, (32, LANES), 1)
    g3[1, 0:32, :] = jnp.zeros((32, LANES), F32)
    g3[1, 0:n_basis, 0:ch] = wb_ref[...]
    head = g3[1, 0:32, :] + jnp.where(
        (row32 == 8) & (lane32 >= ch) & (lane32 < 2 * ch), 1.0, 0.0
    ) + jnp.where((lane32 >= 2 * ch) & (row32 == 16 + ((lane32 - 2 * ch) >> 3)), 1.0, 0.0)
    w_last = head
    wcol[...] = jnp.broadcast_to(
        jnp.sum(jnp.where(eye > 0, wo_ref[...], 0.0), axis=1, keepdims=True), (ch, LANES)
    )

    def shifted(dx, dy):
        step = float(LANES * ((dy + 1) * 5 + dx + 1))
        return halo[halo_slot(dx, dy)] + jnp.where(sub8 == 4, step, 0.0)

    def whole(k, c):
        return jnp.broadcast_to(table[k, c : c + 1, :], (8, LANES))

    table[0] = shifted(0, 0)
    for i in range(chunks):
        word = rows_code[i * 8 : i * 8 + 8, :]
        n = jnp.where(word >= 512.0, word - 512.0, word).astype(I32)
        k = jnp.where(n >= atoms, 1, 0) + jnp.where(n >= 2 * atoms, 1, 0) + jnp.where(n >= 3 * atoms, 1, 0)
        n = n - atoms * k
        spot[0, i] = n
        spot[1, i] = k
        for c in range(5):
            early[c, i] = pick(whole(0, c), n)
        row = i * 8 + sub8
        block = jnp.zeros((8, LANES), I32)
        for b in range(1, blocks):
            block = block + jnp.where(row >= b * per_block, 1, 0)
        centre = block * GROUP + (lane8 & (GROUP - 1))
        for c in range(3):
            early[5 + c, i] = pick(whole(0, c), centre)

    kind_rows = jnp.broadcast_to(halo[own, 3:4, :], (8, LANES))
    for block in range(blocks):
        spread = (lane8 & (GROUP - 1)) + block * GROUP
        kind_row = jnp.broadcast_to(pick(kind_rows, spread)[0:1], (ch, LANES))
        term = jnp.zeros((ch, LANES), F32)
        for kind in range(n_kinds):
            term = jnp.where(
                kind_row == float(kind),
                jnp.broadcast_to(ec[:, kind : kind + 1], (ch, LANES)),
                term,
            )
        cterm[block] = term

    pl.semaphore_wait(barrier, len(NEAR))
    sends, carried = [], []
    for dx, dy in NEAR:
        there = halo_slot(-dx, -dy)
        copy = pltpu.make_async_remote_copy(
            src_ref=edge if dx else halo.at[own],
            dst_ref=halo.at[there],
            send_sem=halo_send.at[there],
            recv_sem=halo_recv.at[there],
            device_id=device(dx, dy),
            device_id_type=MESH,
        )
        copy.start()
        sends.append(copy)
    for dx in (-1, 1):
        there = 1 - dx
        copy = pltpu.make_async_remote_copy(
            src_ref=load.at[1],
            dst_ref=load.at[there],
            send_sem=load_send.at[there],
            recv_sem=load_recv.at[there],
            device_id=device(dx, 0),
            device_id_type=MESH,
        )
        copy.start()
        carried.append(copy)

    for t in range(len(TARGETS)):
        ret_out[t] = jnp.zeros((4, LANES), F32)

    for copy in sends:
        copy.wait_recv()

    def row_index(rows, which):
        return jnp.broadcast_to(rows[which : which + 1, :], (8, LANES)).astype(I32)

    def x_ghosts(dy):
        return jnp.where(lane8 < width_x, shifted(-1, dy), shifted(1, dy))

    def y_ghosts(dy):
        base = shifted(0, dy)
        index = row_index(base, 7 if dy < 0 else 6)
        outer = index >= atoms
        return jnp.where(
            outer,
            pick(x_ghosts(dy), jnp.where(outer, index - atoms, 0)),
            pick(base, jnp.where(outer, 0, index)),
        )

    table[1] = x_ghosts(0)
    table[2] = y_ghosts(-1)
    table[3] = y_ghosts(1)

    def forward_chunk(i, carry):
        word = rows_code[pl.ds(i * 8, 8), :]
        live = word >= 512.0
        n, k = spot[0, i], spot[1, i]
        near = []
        for c in range(5):
            v = early[c, i]
            for part in (1, 2, 3):
                v = jnp.where(k == part, pick(whole(part, c), n), v)
            near.append(v)
        off = []
        for c in range(3):
            d = near[c] - early[5 + c, i]
            d = d - period[c] * jnp.floor(d / period[c] + 0.5)
            off.append(jnp.where(live, d, SPACING if c == 0 else 0.0))
        radius = jnp.sqrt(off[0] * off[0] + off[1] * off[1] + off[2] * off[2])
        rinv = 1.0 / radius
        ux, uy, uz = (o * rinv for o in off)
        q = radius / CUTOFF
        valid = jnp.logical_and(live, q < 1.0)
        q2 = q * q
        q5 = q2 * q2 * q
        q6 = q5 * q
        env = jnp.where(valid, 1.0 + q6 * (-28.0 + q * (48.0 - 21.0 * q)), 0.0)
        denv = jnp.where(valid, (168.0 / CUTOFF) * q5 * (-1.0 + q * (2.0 - q)), 0.0)
        u = PI * jnp.minimum(q, 1.0) - 0.5 * PI
        w = u * u
        sin1 = 1.0 + w * (-1 / 2 + w * (1 / 24 + w * (-1 / 720 + w * (1 / 40320 + w * (-1 / 3628800 + w * (1 / 479001600))))))
        cos1 = -u * (1.0 + w * (-1 / 6 + w * (1 / 120 + w * (-1 / 5040 + w * (1 / 362880 + w * (-1 / 39916800 + w * (1 / 6227020800)))))))
        sc[0, i] = ux
        sc[1, i] = uy
        sc[2, i] = uz
        sc[3, i] = rinv
        sc[4, i] = denv
        zbase = i * 128
        scale = (2.0 / CUTOFF) ** 0.5 * rinv
        s_prev, s_now = jnp.zeros_like(sin1), sin1
        c_prev, c_now = jnp.ones_like(cos1), cos1
        for order in range(1, n_basis + 1):
            bes = scale * s_now
            zf[pl.ds(zbase + order - 1, 8, stride=16), :] = bes
            sc[4 + order, i] = scale * (order * PI / CUTOFF) * c_now - bes * rinv
            s_prev, s_now = s_now, 2.0 * cos1 * s_now - s_prev
            c_prev, c_now = c_now, 2.0 * cos1 * c_now - c_prev
        for kind in range(n_kinds):
            zf[pl.ds(zbase + n_basis + kind, 8, stride=16), :] = jnp.where(near[3] == float(kind), 1.0, 0.0)
        for extra in range(n_basis + n_kinds, 16):
            zf[pl.ds(zbase + extra, 8, stride=16), :] = jnp.zeros((8, LANES), F32)
        ys = (
            R3 * ux,
            R3 * uy,
            R3 * uz,
            R15 * ux * uy,
            R15 * uy * uz,
            0.5 * R5 * (3.0 * uz * uz - 1.0),
            R15 * ux * uz,
            0.5 * R15 * (ux * ux - uy * uy),
        )
        for m, y in enumerate(ys):
            zy[pl.ds(zbase + m, 8, stride=16), :] = y
        zy[pl.ds(zbase + 8, 8, stride=16), :] = env
        dest = near[4].astype(I32)
        tbase = i * 64
        pt[pl.ds(tbase + 6, 8, stride=8), :] = (dest >> 7).astype(F32)
        pt[pl.ds(tbase + 7, 8, stride=8), :] = (dest & (LANES - 1)).astype(F32)
        return carry

    for i in range(chunks):
        forward_chunk(i, 0)

    n_harm = 8
    wide = n_harm * GROUP
    own_lane = (lane8 & (GROUP - 1)) == sub8
    every = jnp.concatenate([jnp.where(own_lane, 1.0, 0.0)] * n_harm, axis=0).astype(BF16)
    ones_row = jnp.concatenate([jnp.where(own_lane, 1.0, 0.0), jnp.zeros((8, LANES), F32)], axis=0).astype(BF16)
    at_ef = wide + 2 * GROUP
    at_dlp = at_ef + ch

    degree_rows = ((1, 0, 3 * GROUP), (2, 3 * GROUP, wide), (0, wide, wide + 2 * GROUP))

    def by_degree(which, sums):
        parts = []
        for degree, a, b in degree_rows:
            grown = exact_dot(jnp.concatenate([x[a:b] for x in sums], axis=0), which, degree)
            parts.append([grown[t * (b - a) : (t + 1) * (b - a)] for t in range(len(sums))])
        return [jnp.concatenate([p[t] for p in parts], axis=0) for t in range(len(sums))]

    def exact_dot(rows, which, degree):
        high = rows.astype(BF16).astype(F32)
        joined = jnp.concatenate([high, rows - high, high], axis=1).astype(BF16)
        return nn_dot(joined, mats[which, degree])

    def as_left(turned, pad):
        tall_one = jnp.concatenate([turned, jnp.zeros((LANES - at_ef, ch), F32)], axis=0)
        return (tall_one.T + pad)[:, 0:at_dlp]

    w_out = wcol[...]
    kept = {}

    def env_row(row):
        return zy[row * 16 + 8 : row * 16 + 9, :]

    def stage_pre(b):
        base = b * per_block
        feats = jnp.concatenate(
            [zf[(base + jb) * 16 : (base + jb + 1) * 16, :] for jb in range(per_block)], axis=1
        )
        kept["pre", b] = nn_dot(w1s[...], feats.astype(BF16))

    def stage_feat(b):
        centre_term = cterm[b]
        pre = kept.pop(("pre", b))
        for jb in range(per_block):
            row = b * per_block + jb
            cols = slice(jb * LANES, (jb + 1) * LANES)
            z = zy[row * 16 : row * 16 + 16, :]
            env = z[8:9]
            p = pre[:, cols] + centre_term
            sig = sigmoid(p)
            s1 = p * sig
            s1_s[row] = s1
            ds_s[row] = (sig + s1 * (1.0 - sig)) * env
            rhs[b, at_ef : at_ef + ch, cols] = (s1 * env).astype(BF16)
            for m in range(0, n_harm, 2):
                two = [jnp.where(own_lane, z[t : t + 1], 0.0) for t in (m, m + 1)]
                rhs[b, m * GROUP : (m + 2) * GROUP, cols] = jnp.concatenate(two, axis=0).astype(BF16)
            rhs[b, wide : wide + 2 * GROUP, cols] = ones_row

    def stage_env(b):
        kept["f", b] = nt_dot(rhs[b, 0:at_ef, :], rhs[b, at_ef : at_ef + ch, :])

    def stage_grow(b):
        half = blocks // 2
        if b % half == 0:
            grown = by_degree(0, [kept.pop(("f", t)) for t in range(b, b + half)])
            for t in range(half):
                kept["g", b + t] = grown[t]

    def stage_lp(b):
        left = as_left(kept["g", b], w0pad[0])
        kept["lp", b] = split_dot(left, rhs[b, 0:at_dlp, :])

    def stage_latent(b):
        lp_all = kept.pop(("lp", b))
        for jb in range(per_block):
            row = b * per_block + jb
            cols = slice(jb * LANES, (jb + 1) * LANES)
            env = env_row(row)
            lp = lp_all[:, cols]
            sig = sigmoid(lp)
            lat = lp * sig
            hid_s[row] = w_out * (s1_s[row] * env + lat)
            dlp = (w_out * env) * (sig + lat * (1.0 - sig))
            rhs[b, at_dlp : at_dlp + ch, cols] = dlp.astype(BF16)

    def stage_back(b):
        kept["f", b] = nt_dot(rhs[b, 0:at_ef, :], rhs[b, at_dlp : at_dlp + ch, :])

    def stage_shrink(b):
        half = blocks // 2
        if b % half == 0:
            grown = by_degree(1, [kept.pop(("f", t)) for t in range(b, b + half)])
            for t in range(half):
                kept["d", b + t] = grown[t]

    def stage_de(b):
        grown = kept.pop(("d", b))
        left = as_left(grown, w0pad[1])
        kept["de", b] = split_dot(left, jnp.concatenate([rhs[b, 0:at_ef, :], rhs[b, at_dlp : at_dlp + ch, :]], axis=0))
        both = jnp.concatenate([grown[0:wide], kept.pop(("g", b))[0:wide]], axis=1)
        kept["dy", b] = nn_dot(both.astype(BF16), rhs[b, at_ef : at_dlp + ch, :])

    def stage_edge(b):
        de_all = kept.pop(("de", b))
        dy_all = kept.pop(("dy", b))
        for jb in range(per_block):
            row = b * per_block + jb
            cols = slice(jb * LANES, (jb + 1) * LANES)
            de = de_all[:, cols] + w_out * env_row(row)
            dpt_s[b, 0:ch, cols] = (de * ds_s[row]).astype(BF16)
            dpt_s[b, ch : 2 * ch, cols] = (hid_s[row] + de * s1_s[row]).astype(BF16)
            dpt_s[b, 2 * ch :, cols] = dy_all[:, cols].astype(BF16) * every

    def stage_fold(b):
        got = split_dot(w_last, dpt_s[b])
        for jb in range(per_block):
            row = b * per_block + jb
            zd[row * 24 : row * 24 + 24, :] = got[0:24, jb * LANES : (jb + 1) * LANES]

    stages = (
        stage_pre,
        stage_feat,
        stage_env,
        stage_grow,
        stage_lp,
        stage_latent,
        stage_back,
        stage_shrink,
        stage_de,
        stage_edge,
        stage_fold,
    )
    teams = (range(0, blocks // 2), range(blocks // 2, blocks))
    for tick in range(len(stages) + 3):
        for late, team in enumerate(teams):
            if 0 <= tick - 3 * late < len(stages):
                for b in team:
                    stages[tick - 3 * late](b)
    for row in range(n_rows, chunks * 8):
        zd[row * 24 : row * 24 + 24, :] = jnp.zeros((24, LANES), F32)

    def put_parts(store, values):
        for c in range(3):
            high = values[c].astype(BF16).astype(F32)
            store(c, high)
            store(c + 3, values[c] - high)

    def backward_chunk(i, carry):
        zbase = i * 192

        def d(which):
            return zd[pl.ds(zbase + which, 8, stride=24), :]

        ux, uy, uz, rinv, denv = (sc[t, i] for t in range(5))
        dr = d(8) * denv
        for order in range(n_basis):
            dr = dr + d(order) * sc[5 + order, i]
        d1, d2, d3, d4, d5, d6, d7, d8 = (d(16 + m) for m in range(8))
        dux = R3 * d1 + R15 * (uy * d4 + uz * d7 + ux * d8)
        duy = R3 * d2 + R15 * (ux * d4 + uz * d5 - uy * d8)
        duz = R3 * d3 + R15 * (uy * d5 + ux * d7) + (3.0 * R5) * uz * d6
        radial = dr - rinv * (dux * ux + duy * uy + duz * uz)
        forces = [-(radial * u + rinv * du) for u, du in ((ux, dux), (uy, duy), (uz, duz))]
        at = pl.ds(i * 8, 8)
        for c in range(3):
            g3[c, at, :] = forces[c]

        def store(which, value):
            pt[pl.ds(i * 64 + which, 8, stride=8), :] = value

        put_parts(store, forces)
        return carry

    for i in range(chunks):
        backward_chunk(i, 0)

    halfway = blocks // 2
    pt[chunks * 64 :, :] = jnp.zeros((64, LANES), F32)
    sums = []
    for c in range(3):
        rows = jnp.concatenate(
            [
                jnp.sum(g3[c, b * per_block : (b + 1) * per_block, :], axis=0, keepdims=True)
                for b in range(blocks)
            ],
            axis=0,
        )
        rows = -(rows + pltpu.roll(rows, LANES // 2, 1))
        sums.append(jnp.where(lane1 < LANES // 2, rows[0:halfway], rows[halfway:]))
    for b in range(halfway):
        at = (n_rows + b) * 8

        def store(which, value):
            pt[at + which : at + which + 1, :] = value[b : b + 1]

        put_parts(store, sums)
        spread = (lane8 & (GROUP - 1)) + jnp.where(lane8 < LANES // 2, b, b + halfway) * GROUP
        dest = pick(whole(0, 4), spread)[0:1].astype(I32)
        pt[at + 6 : at + 7, :] = (dest >> 7).astype(F32)
        pt[at + 7 : at + 8, :] = (dest & (LANES - 1)).astype(F32)

    n_targets = len(TARGETS)
    tall = 96
    sub16 = lax.broadcasted_iota(I32, (16, LANES), 0)
    pair = jnp.where(sub16 >= 8, 1.0, 0.0)
    pairs = [(pair + 2.0 * b).astype(BF16) for b in range((n_targets + 1) // 2)]
    steps = [(sub16 + 16 * b).astype(F32).astype(BF16) for b in range(tall // 16)]
    zero16 = jnp.zeros((16, LANES), BF16)
    one16 = jnp.ones((16, LANES), BF16)

    spread_out = None
    rows_left = n_rows + halfway + (n_rows + halfway) % 2
    for first_row in range(0, rows_left, 8):
        lefts, rights = [], []
        for row in range(first_row, min(first_row + 8, rows_left)):
            v = pt[row * 8 : row * 8 + 8, :]
            where_to = jnp.broadcast_to(v[6:7], (16, LANES)).astype(BF16)
            lo = jnp.broadcast_to(v[7:8], (16, LANES)).astype(BF16)
            twice = jnp.concatenate([v, v], axis=0).astype(BF16)
            lefts.append(jnp.concatenate([jnp.where(where_to == p, twice, zero16) for p in pairs], axis=0))
            rights.append(jnp.concatenate([jnp.where(lo == p, one16, zero16) for p in steps], axis=0))
        part = nt_dot(jnp.concatenate(lefts, axis=1), jnp.concatenate(rights, axis=1))
        spread_out = part if spread_out is None else spread_out + part
    for t in range(n_targets):
        tile = spread_out[t * 8 : t * 8 + 8, :]
        ret_out[t, 0:3, 0:tall] = tile[0:3] + tile[3:6]
    for dx, dy in FAR:
        tile = jnp.concatenate([ret_out[target_slot(dx, dy)], jnp.zeros((4, LANES), F32)], axis=0)
        far_out[far_slot(dx, dy)] = jnp.where(
            lane1 < atoms + 10,
            tile[0:1],
            jnp.where(lane1 < atoms + 20, pltpu.roll(tile, 10, 1)[1:2], pltpu.roll(tile, 20, 1)[2:3]),
        )

    returns = []
    for group, slot, out, into, send_sems, recv_sems in (
        (NIGH, target_slot, ret_out, ret_in, ret_send, ret_recv),
        (FAR, far_slot, far_out, far_in, far_send, far_recv),
    ):
        for dx, dy in group:
            there = slot(-dx, -dy)
            copy = pltpu.make_async_remote_copy(
                src_ref=out.at[slot(dx, dy)],
                dst_ref=into.at[there],
                send_sem=send_sems.at[there],
                recv_sem=recv_sems.at[there],
                device_id=device(dx, dy),
                device_id_type=MESH,
            )
            copy.start()
            returns.append(copy)

    for copy in carried:
        copy.wait_recv()
    settle = jnp.broadcast_to(source, (8, LANES))
    mine, low, high = load[1], load[0], load[2]
    held = jnp.where(lane8 < atoms, mine, jnp.where(lane8 < atoms + 5, low, high))
    held = jnp.where(lane8 < LANES - 1, held, 0.0)
    held = pick(held, settle)
    total = ret_out[target_slot(0, 0)]
    for copy in returns:
        copy.wait_recv()
    for dx, dy in NIGH:
        total = total + ret_in[target_slot(dx, dy)]
    far = far_in[0]
    for t in range(1, len(FAR)):
        far = far + far_in[t]
    far = jnp.broadcast_to(far, (8, LANES))
    seats = jnp.logical_and(lane8 >= atoms, lane8 < atoms + 10)
    moved = jnp.where(sub8 == 0, far, jnp.where(sub8 == 1, pltpu.roll(far, LANES - 10, 1), pltpu.roll(far, LANES - 20, 1)))
    total = jnp.concatenate([total, jnp.zeros((4, LANES), F32)], axis=0) + jnp.where(seats, moved, 0.0)
    force = pick(total, settle)[0:3]
    fresh = held[0:3] + 0.5 * TIME_STEP * force * held[6:7]
    for c in range(3):
        both_ref[0, c] = fresh[c : c + 1, 0:atoms]
        both_ref[0, c + 3] = held[c + 3 : c + 4, 0:atoms]
    for copy in sends + carried + returns:
        copy.wait_send()


def on_device(*args):
    atoms = args[0].shape[3]
    slots = args[4].shape[2]
    ch = args[13].shape[0]
    chunks = (atoms // GROUP * (slots // 16) + 7) // 8
    n_gx, n_yz = lax.axis_size("gx"), lax.axis_size("yz")
    period = (n_gx * PX * SPACING, n_yz * PY * SPACING, PZ * SPACING)
    pos, vel, frc, spc, nbr, msk, sx, sy, ms, mr, wb, ec, en, we, wl, wo = args
    pos, vel, frc = (x.transpose(0, 2, 1, 3) for x in (pos, vel, frc))
    nbr, msk = (x.transpose(0, 1, 3, 2) for x in (nbr, msk))
    args = (pos, vel, frc, spc, nbr, msk, sx, sy, ms, mr, wb, ec.T, en.T, we, wl.T, wo.reshape(1, ch))

    def body(*refs):
        kernel_body(period, atoms, slots, *refs)

    vmem = pl.BlockSpec(memory_space=pltpu.VMEM)
    per_block = slots // 16
    blocks = atoms // GROUP
    dma = pltpu.SemaphoreType.DMA
    out = jax.ShapeDtypeStruct((1, 6, 1, atoms), F32)
    staged = tuple(
        (pltpu.SMEM if at in (8, 9) else pltpu.VMEM)(x.shape, x.dtype) for at, x in enumerate(args)
    )
    both = pl.pallas_call(
        body,
        out_shape=out,
        in_specs=[pl.BlockSpec(memory_space=pl.ANY)] * 16,
        out_specs=vmem,
        scratch_shapes=[
            staged,
            pltpu.VMEM((9, 8, LANES), F32),
            pltpu.VMEM((8, LANES), F32),
            pltpu.VMEM((3, 8, LANES), F32),
            pltpu.VMEM((15, 4, LANES), F32),
            pltpu.VMEM((15, 4, LANES), F32),
            pltpu.VMEM((6, 1, LANES), F32),
            pltpu.VMEM((6, 1, LANES), F32),
            pltpu.VMEM((atoms, LANES), F32),
            pltpu.VMEM((chunks * 8, LANES), F32),
            pltpu.VMEM((4, 8, LANES), F32),
            pltpu.VMEM((13, chunks, 8, LANES), F32),
            pltpu.VMEM((chunks * 128, LANES), F32),
            pltpu.VMEM((chunks * 128, LANES), F32),
            pltpu.VMEM((chunks * 192, LANES), F32),
            pltpu.VMEM((chunks * 64 + 64, LANES), F32),
            pltpu.VMEM((atoms // GROUP, ch, LANES), F32),
            pltpu.VMEM((2, 3, 3 * ch, ch), BF16),
            pltpu.VMEM((ch, 16), BF16),
            pltpu.VMEM((ch, LANES), F32),
            pltpu.VMEM((2, ch, LANES), F32),
            pltpu.VMEM((blocks, 10 * GROUP + 2 * ch, per_block * LANES), BF16),
            pltpu.VMEM((blocks * per_block, ch, LANES), F32),
            pltpu.VMEM((blocks * per_block, ch, LANES), F32),
            pltpu.VMEM((blocks * per_block, ch, LANES), F32),
            pltpu.VMEM((blocks, 2 * ch + 8 * GROUP, per_block * LANES), BF16),
            pltpu.VMEM((3, 64, LANES), F32),
            pltpu.VMEM((2, chunks, 8, LANES), I32),
            pltpu.VMEM((8, chunks, 8, LANES), F32),
            dma((16,)),
            dma((9,)),
            dma((9,)),
            dma((3,)),
            dma((3,)),
            dma((15,)),
            dma((15,)),
            dma((6,)),
            dma((6,)),
        ],
        compiler_params=pltpu.CompilerParams(
            collective_id=0, has_side_effects=True, vmem_limit_bytes=60 * 1024 * 1024
        ),
    )(*args)
    return both[:, 0:3].transpose(0, 2, 1, 3), both[:, 3:6].transpose(0, 2, 1, 3)


def solution(mesh):
    block4 = P("gx", "yz", None, None)
    block3 = P("gx", "yz", None)
    return jax.shard_map(
        on_device,
        mesh=mesh,
        in_specs=(block4, block4, block4, block3) + (block4,) * 6 + (P(),) * 6,
        out_specs=(block4, block4),
        check_vma=False,
    )
```
